256 devices in a mesh: arc: 8 (over z_lo, core), par: 32 (over z_hi, x, y).
Axes of the slice: x: 4, y: 4, z: 8 (z_hi: 2, z_lo: 4; z = z_hi * 4 + z_lo), core: 2. Of those that a mesh axis runs over, the one named last changes fastest.
Arguments:
- design: bfloat16 [16, 1024, 40960], P('arc', None, 'par'), may hold values from -0.1875 to 0.1875
- cov_factor: float32 [16, 1024, 1024], P('arc', 'par'), may hold values from -1 to 3, as said below
- active_blocks: int32 [16, 80], P('arc'), may hold values from 0 to 159, all different within a row
- panel_index: int32 [1], replicated, may hold values from 0 to 79
- reg_diag: float32 [40960], replicated, may hold values from 0.5 to 4
Outputs:
- solved: float32 [512, 40960], P(None, ('par', 'arc'))
The draws below stay inside these ranges and needn't reach their ends.
Inputs may be any that keep to these rules, and one draw needn't show every extreme that they name: Each cov_factor[a] is lower triangular with a positive diagonal.
All inputs are finite; a program needn't handle non-finite values.
Results may differ from the reference program's by a relative error of at most 0.0032.
Values may be sent and summed in bfloat16 or wider, within the bound.
A program may use at most 192 MiB of HBM per device.

```python
import math
import jax
import jax.numpy as jnp
from jax import lax

P_SIZE = 40960
OBS = 1024
PANEL = 512
BLK = 256
ACT = 80
ARCS = 16


def draw_cov_factor(key, part):
    first, second = jax.random.split(jax.random.fold_in(key, 7))
    spread = 0.5 / OBS ** 0.5
    diagonal = jax.random.uniform(first, (ARCS, OBS), jnp.float32, 1.0, 2.0)
    lower = jnp.clip(jax.random.normal(second, (ARCS, OBS, OBS), jnp.float32), -6.0, 6.0) * spread
    below = jnp.tril(jnp.ones((OBS, OBS), jnp.float32), -1)
    unit = jnp.eye(OBS, dtype=jnp.float32)
    return lower * below[None] + diagonal[:, :, None] * unit[None]


def shard_levels(stream_key, extent, cuts, low, high):
    level = 1.0
    for position, blocks in cuts:
        draws = jax.random.uniform(jax.random.fold_in(jax.random.fold_in(stream_key, 6), position), (blocks,), jnp.float32, low / len(cuts), high / len(cuts))
        level = level * jnp.repeat(jnp.exp(draws), extent[position] // blocks).reshape((-1,) + (1,) * (len(extent) - 1 - position))
    return level


def distinct(rng, rows, amount, top, lift):
    ranking = jax.random.permutation(jax.random.fold_in(rng, 1), amount)
    favour = ranking
    for power in range(3):
        favour = favour * favour // amount
    favour = favour * lift // amount
    chance = jax.random.randint(jax.random.fold_in(rng, 2), (rows, amount), 0, 4096) + favour
    holders = jax.random.permutation(jax.random.fold_in(rng, 3), rows)[jnp.arange(amount) % rows]
    chance = jnp.where(jnp.arange(rows)[:, None] == holders[None, :], 1 << 14, chance)
    merit = chance * amount + jnp.arange(amount)
    return lax.top_k(merit.astype(jnp.int32), top)[1].astype(jnp.int32)


def scatter_about(rng, extent, deviation, bound, cuts=(), kind=jnp.bfloat16):
    gain = shard_levels(rng, extent, cuts, -0.22, 0.18) if cuts else 1.0
    result = jax.random.normal(rng, extent, jnp.float32) * deviation * gain
    return jnp.minimum(jnp.maximum(result, -bound), bound).astype(kind)


def setup_inputs(seed: int = 0) -> dict:
    seeds = jax.random.split(jax.random.key(seed), 6)
    return {
        "design": scatter_about(seeds[0], (ARCS, OBS, P_SIZE), OBS ** -0.5, 0.1875, ((0, 8), (2, 32))),
        "cov_factor": draw_cov_factor(jax.random.fold_in(seeds[5], 71), 0),
        "active_blocks": distinct(seeds[2], ARCS, P_SIZE // BLK, ACT, 4096),
        "panel_index": jax.random.randint(seeds[3], (1,), 0, P_SIZE // PANEL).astype(jnp.int32),
        "reg_diag": jnp.clip(jnp.exp(jax.random.uniform(seeds[4], (P_SIZE,), jnp.float32, math.log(0.5), math.log(4.0))), 0.5, 4.0),
    }


def whiten(factor, rhs):
    size = factor.shape[0]
    step = min(128, size)
    pieces = []
    for index in range(size // step):
        low = index * step
        accum = rhs[low:low + step]
        if index > 0:
            done = jnp.concatenate(pieces, axis=0)
            accum = accum - jnp.dot(factor[low:low + step, :low].astype(jnp.float32), done.astype(jnp.float32), precision=lax.Precision.HIGHEST, preferred_element_type=jnp.float32)
        pieces.append(lax.linalg.triangular_solve(factor[low:low + step, low:low + step], accum, left_side=True, lower=True))
    return jnp.concatenate(pieces, axis=0)

def reference(design, cov_factor, active_blocks, panel_index, reg_diag):
    nblocks = P_SIZE // BLK
    start = (panel_index[0] * PANEL).astype(jnp.int32)
    block_ids = jnp.arange(nblocks, dtype=jnp.int32)

    def one_arc(normals, inputs):
        rows, factor, active = inputs
        hits = jnp.any(active[:, None] == block_ids[None, :], axis=0)
        col_mask = jnp.repeat(hits, BLK).astype(rows.dtype)
        masked = rows * col_mask[None, :]
        picked = rows.reshape(OBS, nblocks, BLK)[:, active, :].reshape(OBS, ACT * BLK)
        whitened = whiten(factor, picked.astype(jnp.float32)).astype(jnp.bfloat16)
        raw_panel = lax.dynamic_slice_in_dim(masked, start, PANEL, 1).astype(jnp.float32)
        panel = whiten(factor, raw_panel).astype(jnp.bfloat16)
        term = jnp.dot(panel.T.astype(jnp.float32), whitened.astype(jnp.float32), preferred_element_type=jnp.float32)
        grid = normals.reshape(PANEL, nblocks, BLK).at[:, active, :].add(term.reshape(PANEL, ACT, BLK))
        return (grid.reshape(PANEL, P_SIZE), None)
    normals, _ = lax.scan(one_arc, jnp.zeros((PANEL, P_SIZE), jnp.float32), (design, cov_factor, active_blocks))
    reg_panel = lax.dynamic_slice_in_dim(reg_diag, start, PANEL)
    block = lax.dynamic_slice_in_dim(normals, start, PANEL, 1) + jnp.diag(reg_panel)
    lower11 = jnp.linalg.cholesky(block)
    columns = jnp.arange(P_SIZE, dtype=jnp.int32)
    rows_at = start + jnp.arange(PANEL, dtype=jnp.int32)
    shifted = normals + jnp.where(columns[None, :] == rows_at[:, None], reg_panel[:, None], jnp.float32(0.0))
    return whiten(lower11, shifted)
```

```python
import functools
import jax
import jax.numpy as jnp
from jax import lax
from jax.experimental import pallas as pl
from jax.experimental.pallas import tpu as pltpu
from jax.sharding import Mesh
from jax.sharding import PartitionSpec as P

OBS_STEP = 256
BF = jnp.bfloat16
F32 = jnp.float32
KERNEL_VMEM = 56 * 1024 * 1024


def halves(value):
    high = value.astype(BF)
    return high, (value - high.astype(F32)).astype(BF)


def dot_by(a, b, dims):
    return lax.dot_general(a, b, (dims, ((), ())), preferred_element_type=F32)


def dot3(a, b, dims=((1,), (0,))):
    (ah, al), (bh, bl) = a, b
    return dot_by(ah, bh, dims) + (dot_by(ah, bl, dims) + dot_by(al, bh, dims))


def lanes(shape):
    return lax.broadcasted_iota(jnp.int32, shape, 1)


def rows_of(shape):
    return lax.broadcasted_iota(jnp.int32, shape, 0)


def invert_tiles(tiles):
    lane = lanes((8, 128))
    low = lane < 64
    base = jnp.where(low, 0, 64)
    packed, inverse = [], []
    for tile in tiles:
        packed.append(
            [jnp.where(low, tile[8 * g : 8 * g + 8], tile[64 + 8 * g : 72 + 8 * g]) for g in range(8)]
        )
        inverse.append(
            [
                jnp.where(lane - base == rows_of((8, 128)) + 8 * g, 1.0, 0.0).astype(F32)
                for g in range(8)
            ]
        )
    for j in range(64):
        at, sub = j // 8, j % 8
        index = base + j
        for pack, inv in zip(packed, inverse):
            coef = [jnp.take_along_axis(pack[g], index, axis=1) for g in range(at, 8)]
            pivot = inv[at][sub : sub + 1] / coef[0][sub : sub + 1]
            pivot = jnp.broadcast_to(pivot, (8, 128))
            row = rows_of((8, 128))
            inv[at] = jnp.where(
                row == sub, pivot, jnp.where(row > sub, inv[at] - coef[0] * pivot, inv[at])
            )
            for g in range(at + 1, 8):
                inv[g] = inv[g] - coef[g - at] * pivot
    return [jnp.concatenate(inv, axis=0) for inv in inverse]


def solve_kernel(arcs, factor_ref, rhs_ref, y_ref, qh_ref, ql_ref, inv, fh, fl, wh, wl, yh, yl):
    size = factor_ref.shape[1]
    tiles = size // 128

    @pl.loop(0, arcs * tiles // 4)
    def _(step):
        found = []
        for part in range(4):
            at = step * 4 + part
            arc, tile = at // tiles, lax.rem(at, tiles)
            spot = pl.ds(pl.multiple_of(tile * 128, 128), 128)
            found.append((arc, spot))
        values = [factor_ref[arc, spot, spot] for arc, spot in found]
        low = lanes((64, 128)) < 64
        for (arc, spot), value, done in zip(found, values, invert_tiles(values)):
            first = jnp.where(low, done, 0.0)
            second = jnp.where(low, 0.0, done)
            whole = jnp.concatenate([first, second], axis=0)
            cross = jnp.where(low, value[64:], 0.0)
            left = dot3(halves(cross), halves(whole))
            left = jnp.concatenate([jnp.zeros_like(left), left], axis=0)
            corner = dot3(halves(second), halves(left))
            inv[arc, spot, :] = jnp.concatenate([first, second - corner], axis=0)

    blocks = size // OBS_STEP
    for arc in range(arcs):
        for b in range(blocks):
            r = b * OBS_STEP
            one, two = inv[arc, r : r + 128, :], inv[arc, r + 128 : r + 256, :]
            cross = factor_ref[arc, r + 128 : r + 256, r : r + 128]
            corner = -dot3(halves(two), halves(dot3(halves(cross), halves(one))))
            zero = jnp.zeros((128, 128), BF)
            for (ref, a, c, d) in zip((wh, wl), halves(one), halves(corner), halves(two)):
                ref[arc, r : r + 128, 0:128] = a
                ref[arc, r : r + 128, 128:256] = zero
                ref[arc, r + 128 : r + 256, 0:128] = c
                ref[arc, r + 128 : r + 256, 128:256] = d
            if b:
                high, less = halves(factor_ref[arc, r : r + 256, 0:r])
                fh[arc, r : r + 256, 0:r] = high
                fl[arc, r : r + 256, 0:r] = less

    for b in range(blocks):
        r = b * OBS_STEP
        here = slice(r, r + OBS_STEP)
        for arc in range(arcs):
            value = rhs_ref[arc, here, :].astype(F32)
            if b:
                value = value - dot3(
                    (fh[arc, here, 0:r], fl[arc, here, 0:r]), (yh[arc, 0:r, :], yl[arc, 0:r, :])
                )
            value = dot3((wh[arc, here, :], wl[arc, here, :]), halves(value))
            high, less = halves(value)
            yh[arc, here, :] = high
            yl[arc, here, :] = less
            y_ref[arc, here, :] = high
    flip = ((0,), (0,))
    for b in reversed(range(blocks)):
        r = b * OBS_STEP
        here, after = slice(r, r + OBS_STEP), slice(r + OBS_STEP, size)
        for arc in range(arcs):
            value = yh[arc, here, :].astype(F32) + yl[arc, here, :].astype(F32)
            if b + 1 < blocks:
                value = value - dot3(
                    (fh[arc, after, here], fl[arc, after, here]),
                    (qh_ref[arc, after, :], ql_ref[arc, after, :]),
                    flip,
                )
            value = dot3((wh[arc, here, :], wl[arc, here, :]), halves(value), flip)
            qh_ref[arc, here, :], ql_ref[arc, here, :] = halves(value)


def solve_twice(factor, rhs):
    arcs, size, width = rhs.shape
    vm = pltpu.VMEM
    out = jax.ShapeDtypeStruct(rhs.shape, BF)
    return pl.pallas_call(
        functools.partial(solve_kernel, arcs),
        out_shape=(out, out, out),
        in_specs=[pl.BlockSpec(memory_space=vm)] * 2,
        out_specs=(pl.BlockSpec(memory_space=vm),) * 3,
        scratch_shapes=[
            vm((arcs, size, 128), F32),
            vm((arcs, size, size), BF),
            vm((arcs, size, size), BF),
            vm((arcs, size, OBS_STEP), BF),
            vm((arcs, size, OBS_STEP), BF),
            vm((arcs, size, width), BF),
            vm((arcs, size, width), BF),
        ],
        compiler_params=pltpu.CompilerParams(vmem_limit_bytes=KERNEL_VMEM),
    )(factor, rhs)


def split_rows(u):
    high, less = halves(u)
    return jnp.concatenate([high, high, less], axis=0), jnp.concatenate([high, less, high], axis=0)


def eliminate(panel, first):
    row = rows_of((8, 128))
    scale = [jnp.zeros((8, 128), F32) for _ in range(4)]
    for group in range(4):
        cols = []
        for t in range(8):
            lane = first + group * 8 + t
            cols.append(
                [
                    jnp.broadcast_to(panel[g][0][:, lane : lane + 1], (8, 128)) if g >= group else None
                    for g in range(4)
                ]
            )
        for t in range(8):
            pivot = lax.rsqrt(jnp.broadcast_to(cols[t][group][t : t + 1], (8, 128)))
            scale[group] = jnp.where(row == t, pivot, scale[group])
            inv = pivot * pivot
            mult = [None if g < group else cols[t][g] * inv for g in range(4)]
            mult[group] = jnp.where(row > t, mult[group], 0.0)
            for t2 in range(t + 1, 8):
                top = jnp.broadcast_to(cols[t2][group][t : t + 1], (8, 128))
                for g in range(group, 4):
                    cols[t2][g] = cols[t2][g] - mult[g] * top
            for c in range(len(panel[0])):
                top = jnp.broadcast_to(panel[group][c][t : t + 1], (8, 128))
                for g in range(group, 4):
                    panel[g][c] = panel[g][c] - mult[g] * top
    return jnp.concatenate(
        [jnp.concatenate([piece * scale[g] for piece in panel[g]], axis=1) for g in range(4)], axis=0
    )


def factor_and_solve(work):
    size, width = work.shape
    flip = ((0,), (0,))
    for k in range(size // 128):
        c0 = k * 128
        for q in range(4):
            r = c0 + q * 32
            panel = [
                [work[r + 8 * g : r + 8 * g + 8, c : c + 128] for c in range(c0, width, 128)]
                for g in range(4)
            ]
            done = eliminate(panel, q * 32)
            work[r : r + 32, c0:width] = done
            if q < 3:
                a, b = split_rows(done)
                less = dot_by(a[:, 0:128], b, flip)
                work[r + 32 : c0 + 128, c0:width] -= less[q * 32 + 32 : 128]
        if c0 + 128 < size:
            a, b = split_rows(work[c0 : c0 + 128, c0:width])
            for i in range(c0 + 128, size, 128):
                work[i : i + 128, i:width] -= dot_by(
                    a[:, i - c0 : i - c0 + 128], b[:, i - c0 :], flip
                )


def last_kernel(block_ref, reg_ref, rhs_ref, out_ref, work):
    size, share = rhs_ref.shape
    work[:, size:] = jnp.zeros((size, work.shape[1] - size), F32)
    for i in range(0, size, 128):
        work[i : i + 128, 0:size] = block_ref[i : i + 128, :]
        square = (128, 128)
        work[i : i + 128, i : i + 128] += jnp.where(
            lanes(square) == rows_of(square), reg_ref[:, i : i + 128], 0.0
        )
    work[:, size : size + share] = rhs_ref[...]
    factor_and_solve(work)
    out_ref[...] = work[:, size : size + share]


def last_solve(block, reg_panel, rhs):
    size, share = rhs.shape
    vm = pltpu.VMEM
    return pl.pallas_call(
        last_kernel,
        out_shape=jax.ShapeDtypeStruct(rhs.shape, F32),
        in_specs=[pl.BlockSpec(memory_space=vm)] * 3,
        out_specs=pl.BlockSpec(memory_space=vm),
        scratch_shapes=[vm((size, size + -(-share // 128) * 128), F32)],
        compiler_params=pltpu.CompilerParams(vmem_limit_bytes=KERNEL_VMEM),
    )(block, reg_panel[None], rhs)


PANEL = 512
BLK = 256
PAR = ("par_0", "par_1", "par_2")
PAR_ARC = ("par_0", "par_1", "par_2", "arc")


def in_blocks(shard, dim, count):
    before, after = (shard.shape[:dim], shard.shape[dim + 1 :])
    return jnp.moveaxis(shard.reshape(*before, count, -1, *after), dim, 0)


def sum_at_owner(shard, axis, dim):
    tiles = in_blocks(shard, dim, lax.axis_size(axis))
    arrived = lax.all_to_all(tiles, axis, split_axis=0, concat_axis=0, tiled=True)
    return arrived.astype(F32).sum(axis=0)


def sum_in_two_steps(shard, axes, dim):
    far, near = axes
    own = sum_at_owner(in_blocks(shard, dim, lax.axis_size(far)), near, dim + 1)
    return jnp.sum(
        lax.all_to_all(own.astype(BF), far, 0, 0, tiled=True).astype(F32), axis=0
    )


def from_everyone(shard, axis):
    copies = jnp.broadcast_to(shard, (lax.axis_size(axis), *shard.shape))
    return lax.all_to_all(copies, axis, split_axis=0, concat_axis=0, tiled=True)


def joined_along(tiles, dim):
    lengths = list(tiles.shape[1:])
    lengths[dim] *= tiles.shape[0]
    return jnp.moveaxis(tiles, 0, dim).reshape(lengths)


def whole_of(shard, axes, dim):
    far, near = axes
    first = from_everyone(shard, far)
    tiles = jnp.swapaxes(from_everyone(first, near), 0, 1)
    return joined_along(tiles.reshape(-1, *shard.shape), dim)


def sum_by_parts(shard, axes):
    lines = shard.reshape(-1, shard.shape[-1])
    own = sum_in_two_steps(lines, axes, 0)
    return whole_of(own.astype(BF), axes, 0).reshape(shard.shape)


def on_device(design, cov_factor, active_blocks, panel_index, reg_diag):
    arcs, observed, columns = design.shape
    local_blocks = columns // BLK
    par_id = lax.axis_index(PAR)
    arc_id = lax.axis_index("arc")
    factor = lax.all_gather(cov_factor, PAR, axis=1, tiled=True)
    block_ids = par_id * local_blocks + jnp.arange(local_blocks, dtype=jnp.int32)
    hits = jnp.any(active_blocks[:, :, None] == block_ids[None, None, :], axis=1)
    col_mask = jnp.repeat(hits, BLK, axis=1).astype(BF)
    masked = design * col_mask[:, None, :]
    start = panel_index[0] * PANEL
    offset = start - par_id * columns
    padded = jnp.pad(masked, ((0, 0), (0, 0), (PANEL, PANEL)))
    window = lax.dynamic_slice_in_dim(
        padded, jnp.clip(offset + PANEL, 0, columns + PANEL), PANEL, 2
    )
    raw = sum_by_parts(window, ("par_0", ("par_1", "par_2")))
    panel, solved_high, solved_low = solve_twice(factor, raw)
    gram = jnp.einsum(
        "haop,aoc->pc",
        jnp.stack([solved_high, solved_low]),
        masked,
        preferred_element_type=F32,
    )
    block = jnp.einsum("aop,aoq->pq", panel, panel, preferred_element_type=F32)
    share = columns // lax.axis_size("arc")
    tiles = in_blocks(gram.astype(BF), 1, lax.axis_size("arc"))
    arrived = lax.all_to_all(tiles, "arc", split_axis=0, concat_axis=0, tiled=True)
    block = lax.psum(block, "arc")
    gram = arrived.astype(F32).sum(axis=0)
    reg_panel = lax.dynamic_slice_in_dim(reg_diag, start, PANEL)
    global_cols = par_id * columns + arc_id * share + jnp.arange(share, dtype=jnp.int32)
    rows_at = start + jnp.arange(PANEL, dtype=jnp.int32)
    shifted = gram + jnp.where(
        global_cols[None, :] == rows_at[:, None], reg_panel[:, None], jnp.float32(0.0)
    )
    return last_solve(block, reg_panel, shifted)


def solution(mesh):
    split = Mesh(
        mesh.devices.reshape(mesh.shape["arc"], 2, 4, 4), ("arc", "par_0", "par_1", "par_2")
    )
    return jax.shard_map(
        on_device,
        mesh=split,
        in_specs=(P("arc", None, PAR), P("arc", PAR, None), P("arc", None), P(), P()),
        out_specs=P(None, PAR_ARC),
        check_vma=False,
    )
```

```python
import functools
import jax
import jax.numpy as jnp
from jax import lax
from jax.experimental import pallas as pl
from jax.experimental.pallas import tpu as pltpu
from jax.sharding import Mesh
from jax.sharding import PartitionSpec as P

OBS_STEP = 256
BF = jnp.bfloat16
F32 = jnp.float32
KERNEL_VMEM = 56 * 1024 * 1024


def halves(value):
    high = value.astype(BF)
    return high, (value - high.astype(F32)).astype(BF)


def dot_by(a, b, dims):
    return lax.dot_general(a, b, (dims, ((), ())), preferred_element_type=F32)


def dot3(a, b, dims=((1,), (0,))):
    (ah, al), (bh, bl) = a, b
    return dot_by(ah, bh, dims) + (dot_by(ah, bl, dims) + dot_by(al, bh, dims))


def lanes(shape):
    return lax.broadcasted_iota(jnp.int32, shape, 1)


def rows_of(shape):
    return lax.broadcasted_iota(jnp.int32, shape, 0)


def invert_tiles(tiles):
    lane = lanes((8, 128))
    low = lane < 64
    base = jnp.where(low, 0, 64)
    packed, inverse = [], []
    for tile in tiles:
        packed.append(
            [jnp.where(low, tile[8 * g : 8 * g + 8], tile[64 + 8 * g : 72 + 8 * g]) for g in range(8)]
        )
        inverse.append(
            [
                jnp.where(lane - base == rows_of((8, 128)) + 8 * g, 1.0, 0.0).astype(F32)
                for g in range(8)
            ]
        )
    for j in range(64):
        at, sub = j // 8, j % 8
        index = base + j
        for pack, inv in zip(packed, inverse):
            coef = [jnp.take_along_axis(pack[g], index, axis=1) for g in range(at, 8)]
            pivot = inv[at][sub : sub + 1] / coef[0][sub : sub + 1]
            pivot = jnp.broadcast_to(pivot, (8, 128))
            row = rows_of((8, 128))
            inv[at] = jnp.where(
                row == sub, pivot, jnp.where(row > sub, inv[at] - coef[0] * pivot, inv[at])
            )
            for g in range(at + 1, 8):
                inv[g] = inv[g] - coef[g - at] * pivot
    return [jnp.concatenate(inv, axis=0) for inv in inverse]


def spot_of(arc, row_slab, piece):
    big = row_slab // 16
    pair = row_slab + big * (31 - 2 * row_slab)
    near, far = lax.rem(pair, 4) if not isinstance(pair, int) else pair % 4, pair // 4
    place = (1 - arc) * (4 * far + near) + arc * (4 * near + far)
    return place, piece + big * (far + 1)


def tile_of(ref, arc, row, column):
    pieces = [ref[(arc, *spot_of(arc, 4 * row + i, column))] for i in range(4)]
    return jnp.concatenate(pieces, axis=0)


def solve_kernel(arcs, factor_ref, rhs_ref, y_ref, qh_ref, ql_ref, inv, fh, fl, wh, wl, yh, yl):
    size = rhs_ref.shape[1]
    tiles = size // 128

    @pl.loop(0, arcs * tiles // 4)
    def _(step):
        found = []
        for part in range(4):
            at = step * 4 + part
            arc, tile = at // tiles, lax.rem(at, tiles)
            spot = pl.ds(pl.multiple_of(tile * 128, 128), 128)
            found.append((arc, spot, tile))
        values = [tile_of(factor_ref, arc, tile, tile) for arc, spot, tile in found]
        low = lanes((64, 128)) < 64
        for (arc, spot, _), value, done in zip(found, values, invert_tiles(values)):
            first = jnp.where(low, done, 0.0)
            second = jnp.where(low, 0.0, done)
            whole = jnp.concatenate([first, second], axis=0)
            cross = jnp.where(low, value[64:], 0.0)
            left = dot3(halves(cross), halves(whole))
            left = jnp.concatenate([jnp.zeros_like(left), left], axis=0)
            corner = dot3(halves(second), halves(left))
            inv[arc, spot, :] = jnp.concatenate([first, second - corner], axis=0)

    blocks = size // OBS_STEP
    for arc in range(arcs):
        for b in range(blocks):
            r = b * OBS_STEP
            one, two = inv[arc, r : r + 128, :], inv[arc, r + 128 : r + 256, :]
            cross = tile_of(factor_ref, arc, 2 * b + 1, 2 * b)
            corner = -dot3(halves(two), halves(dot3(halves(cross), halves(one))))
            zero = jnp.zeros((128, 128), BF)
            for (ref, a, c, d) in zip((wh, wl), halves(one), halves(corner), halves(two)):
                ref[arc, r : r + 128, 0:128] = a
                ref[arc, r : r + 128, 128:256] = zero
                ref[arc, r + 128 : r + 256, 0:128] = c
                ref[arc, r + 128 : r + 256, 128:256] = d
            for row in (2 * b, 2 * b + 1):
                for column in range(2 * b):
                    high, less = halves(tile_of(factor_ref, arc, row, column))
                    fh[arc, row * 128 : row * 128 + 128, column * 128 : column * 128 + 128] = high
                    fl[arc, row * 128 : row * 128 + 128, column * 128 : column * 128 + 128] = less

    for b in range(blocks):
        r = b * OBS_STEP
        here = slice(r, r + OBS_STEP)
        for arc in range(arcs):
            value = rhs_ref[arc, here, :].astype(F32)
            if b:
                value = value - dot3(
                    (fh[arc, here, 0:r], fl[arc, here, 0:r]), (yh[arc, 0:r, :], yl[arc, 0:r, :])
                )
            value = dot3((wh[arc, here, :], wl[arc, here, :]), halves(value))
            high, less = halves(value)
            yh[arc, here, :] = high
            yl[arc, here, :] = less
            y_ref[arc, here, :] = high
    flip = ((0,), (0,))
    for b in reversed(range(blocks)):
        r = b * OBS_STEP
        here, after = slice(r, r + OBS_STEP), slice(r + OBS_STEP, size)
        for arc in range(arcs):
            value = yh[arc, here, :].astype(F32) + yl[arc, here, :].astype(F32)
            if b + 1 < blocks:
                value = value - dot3(
                    (fh[arc, after, here], fl[arc, after, here]),
                    (qh_ref[arc, after, :], ql_ref[arc, after, :]),
                    flip,
                )
            value = dot3((wh[arc, here, :], wl[arc, here, :]), halves(value), flip)
            qh_ref[arc, here, :], ql_ref[arc, here, :] = halves(value)


def solve_twice(factor, rhs):
    arcs, size, width = rhs.shape
    vm = pltpu.VMEM
    out = jax.ShapeDtypeStruct(rhs.shape, BF)
    return pl.pallas_call(
        functools.partial(solve_kernel, arcs),
        out_shape=(out, out, out),
        in_specs=[pl.BlockSpec(memory_space=vm)] * 2,
        out_specs=(pl.BlockSpec(memory_space=vm),) * 3,
        scratch_shapes=[
            vm((arcs, size, 128), F32),
            vm((arcs, size, size), BF),
            vm((arcs, size, size), BF),
            vm((arcs, size, OBS_STEP), BF),
            vm((arcs, size, OBS_STEP), BF),
            vm((arcs, size, width), BF),
            vm((arcs, size, width), BF),
        ],
        compiler_params=pltpu.CompilerParams(vmem_limit_bytes=KERNEL_VMEM),
    )(factor, rhs)


def split_rows(u):
    high, less = halves(u)
    return jnp.concatenate([high, high, less], axis=0), jnp.concatenate([high, less, high], axis=0)


def eliminate(panel, first):
    row = rows_of((8, 128))
    scale = [jnp.zeros((8, 128), F32) for _ in range(4)]
    for group in range(4):
        cols = []
        for t in range(8):
            lane = first + group * 8 + t
            cols.append(
                [
                    jnp.broadcast_to(panel[g][0][:, lane : lane + 1], (8, 128)) if g >= group else None
                    for g in range(4)
                ]
            )
        for t in range(8):
            pivot = lax.rsqrt(jnp.broadcast_to(cols[t][group][t : t + 1], (8, 128)))
            scale[group] = jnp.where(row == t, pivot, scale[group])
            inv = pivot * pivot
            mult = [None if g < group else cols[t][g] * inv for g in range(4)]
            mult[group] = jnp.where(row > t, mult[group], 0.0)
            for t2 in range(t + 1, 8):
                top = jnp.broadcast_to(cols[t2][group][t : t + 1], (8, 128))
                for g in range(group, 4):
                    cols[t2][g] = cols[t2][g] - mult[g] * top
            for c in range(len(panel[0])):
                top = jnp.broadcast_to(panel[group][c][t : t + 1], (8, 128))
                for g in range(group, 4):
                    panel[g][c] = panel[g][c] - mult[g] * top
    return jnp.concatenate(
        [jnp.concatenate([piece * scale[g] for piece in panel[g]], axis=1) for g in range(4)], axis=0
    )


def factor_and_invert(work):
    size = work.shape[0]
    flip = ((0,), (0,))
    for k in range(size // 128):
        c0 = k * 128
        width = size + 128 + c0
        for q in range(4):
            r = c0 + q * 32
            panel = [
                [work[r + 8 * g : r + 8 * g + 8, c : c + 128] for c in range(c0, width, 128)]
                for g in range(4)
            ]
            done = eliminate(panel, q * 32)
            work[r : r + 32, c0:width] = done
            if q < 3:
                a, b = split_rows(done)
                less = dot_by(a[:, 0:128], b, flip)
                work[r + 32 : c0 + 128, c0:width] -= less[q * 32 + 32 : 128]
        if c0 + 128 < size:
            a, b = split_rows(work[c0 : c0 + 128, c0:width])
            for i in range(c0 + 128, size, 128):
                work[i : i + 128, i:width] -= dot_by(
                    a[:, i - c0 : i - c0 + 128], b[:, i - c0 :], flip
                )


def tile_list(size):
    return [(i, j) for i in range(size // 128) for j in range(i, size // 128)]


def factor_kernel(block_ref, reg_ref, out_ref, work):
    size = out_ref.shape[0]
    square = (128, 128)
    eye = lanes(square) == rows_of(square)
    work[:, size:] = jnp.zeros((size, size), F32)
    for at, (i, j) in enumerate(tile_list(size)):
        value = block_ref[at * 128 : at * 128 + 128, :]
        if i == j:
            value = value + jnp.where(eye, reg_ref[:, i * 128 : i * 128 + 128], 0.0)
            work[i * 128 : i * 128 + 128, size + i * 128 : size + i * 128 + 128] = jnp.where(eye, 1.0, 0.0)
        work[i * 128 : i * 128 + 128, j * 128 : j * 128 + 128] = value
    factor_and_invert(work)
    out_ref[...] = work[:, size:]


def factor_inverse(block, reg_panel):
    size = reg_panel.shape[0]
    vm = pltpu.VMEM
    return pl.pallas_call(
        factor_kernel,
        out_shape=jax.ShapeDtypeStruct((size, size), F32),
        in_specs=[pl.BlockSpec(memory_space=vm)] * 2,
        out_specs=pl.BlockSpec(memory_space=vm),
        scratch_shapes=[vm((size, 2 * size), F32)],
        compiler_params=pltpu.CompilerParams(vmem_limit_bytes=KERNEL_VMEM),
        cost_estimate=pl.CostEstimate(flops=30_000_000_000, bytes_accessed=60_000_000, transcendentals=0),
    )(block, reg_panel[None])


def apply_kernel(shift_ref, arrived_ref, inverse_ref, reg_ref, out_ref):
    total = arrived_ref[0].astype(F32)
    for part in range(1, arrived_ref.shape[0]):
        total = total + arrived_ref[part].astype(F32)
    on = rows_of(total.shape) + shift_ref[0] == lanes(total.shape)
    total = total + jnp.where(on, reg_ref[...], 0.0)
    out_ref[...] = dot3(halves(inverse_ref[...]), halves(total), ((1,), (1,)))


def apply_inverse(shift, arrived, inverse, reg_panel):
    _, share, size = arrived.shape
    vm = pltpu.VMEM
    return pl.pallas_call(
        apply_kernel,
        out_shape=jax.ShapeDtypeStruct((size, share), F32),
        in_specs=[pl.BlockSpec(memory_space=pltpu.SMEM)] + [pl.BlockSpec(memory_space=vm)] * 3,
        out_specs=pl.BlockSpec(memory_space=vm),
        compiler_params=pltpu.CompilerParams(vmem_limit_bytes=KERNEL_VMEM),
    )(shift, arrived, inverse, reg_panel[None])


MESH = pl.DeviceIdType.MESH


def remote(src, dst, send, recv, device):
    return pltpu.make_async_remote_copy(
        src_ref=src, dst_ref=dst, send_sem=send, recv_sem=recv, device_id=device, device_id_type=MESH
    )


def meet(devices):
    barrier = pltpu.get_barrier_semaphore()
    for device in devices:
        pl.semaphore_signal(barrier, inc=1, device_id=device, device_id_type=MESH)
    pl.semaphore_wait(barrier, len(devices))


def ring_pair(slot, me, axis, send, recv):
    mine = slot(me)
    return [
        remote(mine, mine, send.at[d], recv.at[d], {axis: lax.rem(me + step, 4)})
        for d, step in enumerate((1, 3))
    ]


def ring_far(first, second, me, axis, send, recv):
    left, right = lax.rem(me + 3, 4), lax.rem(me + 1, 4)
    one, two = first(left), second(right)
    return [
        remote(one, one, send.at[2], recv.at[2], {axis: right}),
        remote(two, two, send.at[3], recv.at[3], {axis: left}),
    ]


def spread_kernel(
    cov_ref, win_ref, fac_ref, rhs_ref, slabs, got1, got2, gotz, sum1, sum2,
    ls, lr, m1s, m1r, m2s, m2r, mzs, mzr, gls, glr, gms, gmr,
):
    z, x, y = (lax.axis_index(name) for name in ("par_0", "par_1", "par_2"))
    arcs = cov_ref.shape[0]
    turned = lambda v: v + z * (3 - 2 * v)
    outer = [(x, "par_1"), (y, "par_2")]
    inner = [(y, "par_2"), (x, "par_1")]
    partner = {"par_0": 1 - z, "par_1": 3 - x, "par_2": 3 - y}
    ring = [{"par_1": lax.rem(x + k, 4)} for k in (1, 2, 3)] + [
        {"par_2": lax.rem(y + k, 4)} for k in (1, 2, 3)
    ]
    meet(ring + [{"par_0": 1 - z}, partner])

    small = turned(x) + 1
    held = small + z * (9 - 2 * small)

    def piece(c):
        spot = pl.ds(pl.multiple_of(c * 128, 128), 128)
        return remote(cov_ref.at[:, :, spot], slabs.at[z, :, :, spot], ls.at[c], lr.at[c], partner)

    pl.loop(0, held)(lambda c: piece(c).start())
    scatter1 = [
        remote(
            win_ref.at[arc, pl.ds(pl.multiple_of(lax.rem(outer[arc][0] + k, 4) * 256, 256), 256)],
            got1.at[arc, k - 1], m1s.at[arc, k - 1], m1r.at[arc, k - 1],
            {outer[arc][1]: lax.rem(outer[arc][0] + k, 4)},
        )
        for k in (1, 3, 2) for arc in range(arcs)
    ]
    for copy in scatter1:
        copy.start()
    slabs[z] = cov_ref[...]
    pl.loop(0, 9 - held)(lambda c: piece(c).wait_recv())

    @pl.loop(0, small)
    def _(c):
        spot = pl.ds(pl.multiple_of(c * 128, 128), 128)
        for arc in range(arcs):
            place = 4 * turned(outer[arc][0]) + turned(inner[arc][0])
            fac_ref[arc, place, c] = slabs[0, arc, :, spot]

    @pl.loop(0, 9 - small)
    def _(c):
        spot = pl.ds(pl.multiple_of(c * 128, 128), 128)
        for arc in range(arcs):
            place = 4 * turned(outer[arc][0]) + turned(inner[arc][0])
            fac_ref[arc, place, small + c] = slabs[1, arc, :, spot]

    def l_unit(arc, cut=slice(0, 9)):
        size = cut.stop - cut.start
        return lambda r: fac_ref.at[
            arc, 4 * turned(outer[arc][0]) + turned(r), pl.ds(cut.start, size)
        ]

    def l_group(arc, low=0, size=4):
        return lambda r: fac_ref.at[arc, pl.ds(4 * turned(r) + low, size)]

    def m_rows(arc, unit, base, low, size):
        return lambda r: rhs_ref.at[arc, pl.ds(pl.multiple_of(base + r * unit + low, 32), size)]

    def m_unit(arc, low=0, size=64):
        return m_rows(arc, 64, outer[arc][0] * 256, low, size)

    def m_group(arc, low=0, size=256):
        return m_rows(arc, 256, 0, low, size)

    def begin(copies):
        for copy in copies:
            copy.start()
        return copies

    def arrive(copies):
        for copy in copies:
            copy.wait_recv()
        return copies

    two = range(arcs)
    sent = list(scatter1)
    near = lambda slot, ax, stage, s, r: [
        copy for arc in two
        for copy in ring_pair(slot(arc), *ax[arc], s.at[arc, stage], r.at[arc, stage])
    ]
    far = lambda first, second, ax, stage, s, r: [
        copy for arc in two
        for copy in ring_far(first(arc), second(arc), *ax[arc], s.at[arc, stage], r.at[arc, stage])
    ]
    l1 = begin(near(l_unit, inner, 0, gls, glr))
    arrive(scatter1)
    scatter2 = []
    for arc in two:
        own = win_ref[arc, pl.ds(pl.multiple_of(outer[arc][0] * 256, 256), 256), :]
        sum1[arc] = (own + got1[arc, 0]) + (got1[arc, 1] + got1[arc, 2])
        i, axis = inner[arc]
        for k in (1, 3, 2):
            to = lax.rem(i + k, 4)
            scatter2 += begin([
                remote(
                    sum1.at[arc, pl.ds(pl.multiple_of(to * 64, 64), 64)],
                    got2.at[arc, k - 1], m2s.at[arc, k - 1], m2r.at[arc, k - 1], {axis: to},
                )
            ])
    arrive(l1)
    l2 = begin(far(lambda a: l_unit(a, slice(0, 5)), lambda a: l_unit(a, slice(5, 9)), inner, 0, gls, glr))
    arrive(scatter2)
    across = []
    for arc in two:
        own = sum1[arc, pl.ds(pl.multiple_of(inner[arc][0] * 64, 64), 64), :]
        sum2[arc] = (own + got2[arc, 0]) + (got2[arc, 1] + got2[arc, 2])
        across += begin([remote(sum2.at[arc], gotz.at[arc], mzs.at[arc], mzr.at[arc], {"par_0": 1 - z})])
    arrive(l2)
    l3 = begin(near(l_group, outer, 1, gls, glr))
    arrive(across)
    for arc in two:
        spot = pl.ds(pl.multiple_of(outer[arc][0] * 256 + inner[arc][0] * 64, 64), 64)
        rhs_ref[arc, spot, :] = sum2[arc] + gotz[arc]
    g1 = begin(near(m_unit, inner, 0, gms, gmr))
    arrive(g1)
    g2 = begin(far(lambda a: m_unit(a, 0, 32), lambda a: m_unit(a, 32, 32), inner, 0, gms, gmr))
    arrive(g2)
    g3 = begin(near(m_group, outer, 1, gms, gmr))
    arrive(l3)
    l4 = begin(far(lambda a: l_group(a, 0, 2), lambda a: l_group(a, 2, 2), outer, 1, gls, glr))
    arrive(g3)
    g4 = begin(far(lambda a: m_group(a, 0, 128), lambda a: m_group(a, 128, 128), outer, 1, gms, gmr))
    arrive(l4)
    arrive(g4)
    pl.loop(0, held)(lambda c: piece(c).wait_send())
    for copy in sent + scatter2 + across + l1 + l2 + l3 + l4 + g1 + g2 + g3 + g4:
        copy.wait_send()


def spread(cov, window):
    arcs, lines, size = cov.shape
    _, observed, width = window.shape
    vm, dma = pltpu.VMEM, pltpu.SemaphoreType.DMA
    return pl.pallas_call(
        spread_kernel,
        out_shape=(
            jax.ShapeDtypeStruct((arcs, 16, 9, lines, 128), F32),
            jax.ShapeDtypeStruct(window.shape, BF),
        ),
        in_specs=[pl.BlockSpec(memory_space=vm)] * 2,
        out_specs=(pl.BlockSpec(memory_space=vm),) * 2,
        scratch_shapes=[
            vm((2, arcs, lines, size), F32),
            vm((arcs, 3, 256, width), BF),
            vm((arcs, 3, 64, width), BF),
            vm((arcs, 64, width), BF),
            vm((arcs, 256, width), BF),
            vm((arcs, 64, width), BF),
            dma((8,)), dma((8,)),
            dma((arcs, 3)), dma((arcs, 3)), dma((arcs, 3)), dma((arcs, 3)),
            dma((arcs,)), dma((arcs,)),
            dma((arcs, 2, 4)), dma((arcs, 2, 4)), dma((arcs, 2, 4)), dma((arcs, 2, 4)),
        ],
        compiler_params=pltpu.CompilerParams(
            vmem_limit_bytes=KERNEL_VMEM, collective_id=0, has_side_effects=True
        ),
    )(cov, window)


def total_kernel(part_ref, out_ref, kept, mate, got, ps, pr, rs, rr, gs, gr, fs, fr):
    me = lax.axis_index("arc")
    core, chip = lax.rem(me, 2), me // 2
    other = {"arc": chip * 2 + 1 - core}
    chips = [lax.rem(chip + k, 4) for k in (1, 2, 3)]
    peers = [{"arc": c * 2 + core} for c in chips]
    meet(peers + [other])
    half = part_ref.shape[0] // 2
    quarter = half // 4
    rows = lambda base, n: pl.ds(pl.multiple_of(base, 32), n)
    swap = remote(part_ref.at[rows((1 - core) * half, half)], mate, ps, pr, other)
    swap.start()
    swap.wait_recv()
    kept[...] = part_ref[rows(core * half, half), :] + mate[...]
    scatter = [
        remote(kept.at[rows(c * quarter, quarter)], got.at[k], rs.at[k], rr.at[k], peer)
        for k, (c, peer) in enumerate(zip(chips, peers))
    ]
    for copy in scatter:
        copy.start()
    for copy in scatter:
        copy.wait_recv()
    mine = rows(core * half + chip * quarter, quarter)
    out_ref[mine, :] = (kept[rows(chip * quarter, quarter), :] + got[0]) + (got[1] + got[2])
    gather = [
        remote(out_ref.at[mine], out_ref.at[mine], gs.at[k], gr.at[k], peer)
        for k, peer in enumerate(peers)
    ]
    forward = [remote(out_ref.at[mine], out_ref.at[mine], fs.at[0], fr.at[0], other)]
    for copy in gather + forward:
        copy.start()
    for k in range(3):
        gather[k].wait_recv()
        came = rows(core * half + lax.rem(chip + 3 - k, 4) * quarter, quarter)
        copy = remote(out_ref.at[came], out_ref.at[came], fs.at[k + 1], fr.at[k + 1], other)
        copy.start()
        forward.append(copy)
    for copy in forward:
        copy.wait_recv()
    for copy in [swap] + scatter + gather + forward:
        copy.wait_send()


def total_over_arc(part):
    lines, width = part.shape
    vm, dma = pltpu.VMEM, pltpu.SemaphoreType.DMA
    return pl.pallas_call(
        total_kernel,
        out_shape=jax.ShapeDtypeStruct(part.shape, F32),
        in_specs=[pl.BlockSpec(memory_space=vm)],
        out_specs=pl.BlockSpec(memory_space=vm),
        scratch_shapes=[
            vm((lines // 2, width), F32),
            vm((lines // 2, width), F32),
            vm((3, lines // 8, width), F32),
            dma, dma, dma((3,)), dma((3,)), dma((3,)), dma((3,)), dma((4,)), dma((4,)),
        ],
        compiler_params=pltpu.CompilerParams(
            vmem_limit_bytes=KERNEL_VMEM, collective_id=1, has_side_effects=True
        ),
        cost_estimate=pl.CostEstimate(flops=20_000_000_000, bytes_accessed=40_000_000, transcendentals=0),
    )(part)


PANEL = 512
BLK = 256
PAR = ("par_0", "par_1", "par_2")
PAR_ARC = ("par_0", "par_1", "par_2", "arc")


def on_device(design, cov_factor, active_blocks, panel_index, reg_diag):
    arcs, observed, columns = design.shape
    local_blocks = columns // BLK
    par_id = lax.axis_index(PAR)
    arc_id = lax.axis_index("arc")
    start = panel_index[0] * PANEL
    block_ids = par_id * local_blocks + jnp.arange(local_blocks, dtype=jnp.int32)
    hits = jnp.any(active_blocks[:, :, None] == block_ids[None, None, :], axis=1)
    wanted = []
    for part in range(PANEL // BLK):
        local = start // BLK + part - par_id * local_blocks
        kept = jnp.clip(local, 0, local_blocks - 1)
        on = (local == kept) & lax.dynamic_slice_in_dim(hits, kept, 1, 1)
        piece = lax.dynamic_slice_in_dim(design, kept * BLK, BLK, 2)
        wanted.append(jnp.where(on[:, :, None], piece, jnp.zeros((), BF)))
    factor, raw = spread(cov_factor, jnp.concatenate(wanted, axis=2))
    panel, solved_high, solved_low = solve_twice(factor, raw)
    col_mask = jnp.repeat(hits, BLK, axis=1).astype(BF)
    masked = design * col_mask[:, None, :]
    gram = jnp.einsum(
        "haop,aoc->cp",
        jnp.stack([solved_high, solved_low]),
        masked,
        preferred_element_type=F32,
    )
    devices = lax.axis_size("arc")
    share = columns // devices
    tiles = gram.astype(BF).reshape(devices, share, PANEL)
    arrived = lax.all_to_all(tiles, "arc", split_axis=0, concat_axis=0, tiled=True)
    block = jnp.einsum("aop,aoq->pq", panel, panel, preferred_element_type=F32)
    upper = jnp.concatenate(
        [block[i * 128 : i * 128 + 128, j * 128 : j * 128 + 128] for i, j in tile_list(PANEL)], axis=0
    )
    reg_panel = lax.dynamic_slice_in_dim(reg_diag, start, PANEL)
    inverse = factor_inverse(total_over_arc(upper), reg_panel)
    shift = (par_id * columns + arc_id * share - start).astype(jnp.int32)[None]
    return apply_inverse(shift, arrived, inverse, reg_panel)


def solution(mesh):
    split = Mesh(
        mesh.devices.reshape(mesh.shape["arc"], 2, 4, 4), ("arc", "par_0", "par_1", "par_2")
    )
    return jax.shard_map(
        on_device,
        mesh=split,
        in_specs=(P("arc", None, PAR), P("arc", PAR, None), P("arc", None), P(), P()),
        out_specs=P(None, PAR_ARC),
        check_vma=False,
    )
```

```python
import functools
import jax
import jax.numpy as jnp
from jax import lax
from jax.experimental import pallas as pl
from jax.experimental.pallas import tpu as pltpu
from jax.sharding import Mesh
from jax.sharding import PartitionSpec as P

OBS_STEP = 256
BF = jnp.bfloat16
F32 = jnp.float32
KERNEL_VMEM = 56 * 1024 * 1024


def halves(value):
    high = value.astype(BF)
    return high, (value - high.astype(F32)).astype(BF)


def dot_by(a, b, dims):
    return lax.dot_general(a, b, (dims, ((), ())), preferred_element_type=F32)


def dot3(a, b, dims=((1,), (0,))):
    (ah, al), (bh, bl) = a, b
    return dot_by(ah, bh, dims) + (dot_by(ah, bl, dims) + dot_by(al, bh, dims))


def lanes(shape):
    return lax.broadcasted_iota(jnp.int32, shape, 1)


def rows_of(shape):
    return lax.broadcasted_iota(jnp.int32, shape, 0)


def invert_tiles(tiles):
    lane = lanes((8, 128))
    low = lane < 64
    base = jnp.where(low, 0, 64)
    packed, inverse = [], []
    for tile in tiles:
        packed.append(
            [jnp.where(low, tile[8 * g : 8 * g + 8], tile[64 + 8 * g : 72 + 8 * g]) for g in range(8)]
        )
        inverse.append(
            [
                jnp.where(lane - base == rows_of((8, 128)) + 8 * g, 1.0, 0.0).astype(F32)
                for g in range(8)
            ]
        )
    for j in range(64):
        at, sub = j // 8, j % 8
        index = base + j
        for pack, inv in zip(packed, inverse):
            coef = [jnp.take_along_axis(pack[g], index, axis=1) for g in range(at, 8)]
            pivot = inv[at][sub : sub + 1] / coef[0][sub : sub + 1]
            pivot = jnp.broadcast_to(pivot, (8, 128))
            row = rows_of((8, 128))
            inv[at] = jnp.where(
                row == sub, pivot, jnp.where(row > sub, inv[at] - coef[0] * pivot, inv[at])
            )
            for g in range(at + 1, 8):
                inv[g] = inv[g] - coef[g - at] * pivot
    return [jnp.concatenate(inv, axis=0) for inv in inverse]


def dot2(a, b, dims=((1,), (0,))):
    bh, bl = b
    return dot_by(a, bh, dims) + dot_by(a, bl, dims)


def spot_of(arc, slab):
    big = slab // 16
    pair = slab + big * (31 - 2 * slab)
    far = pair // 4
    near = pair - 4 * far
    place = (1 - arc) * (4 * far + near) + arc * (4 * near + far)
    return place, big, big * far


def tile_of(ref, arc, row, column):
    pieces = []
    for i in range(4):
        place, _, shift = spot_of(arc, 4 * row + i)
        pieces.append(ref[arc, place, shift + column])
    return jnp.concatenate(pieces, axis=0)


def diagonal_of(ref, arc, row):
    pieces = []
    for i in range(4):
        place, big, _ = spot_of(arc, 4 * row + i)
        pieces.append(
            ref[arc, place, 7 + 2 * big].astype(F32) + ref[arc, place, 8 + 2 * big].astype(F32)
        )
    return jnp.concatenate(pieces, axis=0)


def solve_kernel(arcs, factor_ref, rhs_ref, block_ref, qh_ref, ql_ref, inv, fh, wh, wl, yh, yl):
    size = rhs_ref.shape[1]
    tiles = size // 128

    @pl.loop(0, arcs * tiles // 4)
    def _(step):
        found = []
        for part in range(4):
            at = step * 4 + part
            arc, tile = at // tiles, lax.rem(at, tiles)
            spot = pl.ds(pl.multiple_of(tile * 128, 128), 128)
            found.append((arc, spot, tile))
        values = [diagonal_of(factor_ref, arc, tile) for arc, spot, tile in found]
        low = lanes((64, 128)) < 64
        for (arc, spot, _), value, done in zip(found, values, invert_tiles(values)):
            first = jnp.where(low, done, 0.0)
            second = jnp.where(low, 0.0, done)
            whole = jnp.concatenate([first, second], axis=0)
            cross = jnp.where(low, value[64:], 0.0)
            left = dot3(halves(cross), halves(whole))
            left = jnp.concatenate([jnp.zeros_like(left), left], axis=0)
            corner = dot3(halves(second), halves(left))
            inv[arc, spot, :] = jnp.concatenate([first, second - corner], axis=0)

    blocks = size // OBS_STEP
    for arc in range(arcs):
        for b in range(blocks):
            r = b * OBS_STEP
            one, two = inv[arc, r : r + 128, :], inv[arc, r + 128 : r + 256, :]
            cross = tile_of(factor_ref, arc, 2 * b + 1, 2 * b)
            corner = -dot3(halves(two), halves(dot2(cross, halves(one))))
            zero = jnp.zeros((128, 128), BF)
            for (ref, a, c, d) in zip((wh, wl), halves(one), halves(corner), halves(two)):
                ref[arc, r : r + 128, 0:128] = a
                ref[arc, r : r + 128, 128:256] = zero
                ref[arc, r + 128 : r + 256, 0:128] = c
                ref[arc, r + 128 : r + 256, 128:256] = d
            for row in (2 * b, 2 * b + 1):
                for column in range(2 * b):
                    fh[arc, row * 128 : row * 128 + 128, column * 128 : column * 128 + 128] = tile_of(
                        factor_ref, arc, row, column
                    )

    for b in range(blocks):
        r = b * OBS_STEP
        here = slice(r, r + OBS_STEP)
        for arc in range(arcs):
            value = rhs_ref[arc, here, :].astype(F32)
            if b:
                value = value - dot2(fh[arc, here, 0:r], (yh[arc, 0:r, :], yl[arc, 0:r, :]))
            value = dot3((wh[arc, here, :], wl[arc, here, :]), halves(value))
            high, less = halves(value)
            yh[arc, here, :] = high
            yl[arc, here, :] = less
    flip = ((0,), (0,))
    for b in reversed(range(blocks)):
        r = b * OBS_STEP
        here, after = slice(r, r + OBS_STEP), slice(r + OBS_STEP, size)
        for arc in range(arcs):
            value = yh[arc, here, :].astype(F32) + yl[arc, here, :].astype(F32)
            if b + 1 < blocks:
                value = value - dot2(
                    fh[arc, after, here], (qh_ref[arc, after, :], ql_ref[arc, after, :]), flip
                )
            value = dot3((wh[arc, here, :], wl[arc, here, :]), halves(value), flip)
            qh_ref[arc, here, :], ql_ref[arc, here, :] = halves(value)
    at = 0
    for i in range(0, rhs_ref.shape[2], 128):
        strip = sum(dot_by(yh[arc, :, i : i + 128], yh[arc, :, i:], flip) for arc in range(arcs))
        for j in range(0, strip.shape[1], 128):
            block_ref[at : at + 128, :] = strip[:, j : j + 128]
            at += 128


def solve_twice(factor, rhs):
    arcs, size, width = rhs.shape
    vm = pltpu.VMEM
    out = jax.ShapeDtypeStruct(rhs.shape, BF)
    tiles = len(tile_list(width))
    return pl.pallas_call(
        functools.partial(solve_kernel, arcs),
        out_shape=(jax.ShapeDtypeStruct((tiles * 128, 128), F32), out, out),
        in_specs=[pl.BlockSpec(memory_space=vm)] * 2,
        out_specs=(pl.BlockSpec(memory_space=vm),) * 3,
        scratch_shapes=[
            vm((arcs, size, 128), F32),
            vm((arcs, size, size), BF),
            vm((arcs, size, OBS_STEP), BF),
            vm((arcs, size, OBS_STEP), BF),
            vm((arcs, size, width), BF),
            vm((arcs, size, width), BF),
        ],
        compiler_params=pltpu.CompilerParams(vmem_limit_bytes=KERNEL_VMEM),
    )(factor, rhs)


def split_rows(u):
    high, less = halves(u)
    return jnp.concatenate([high, high, less], axis=0), jnp.concatenate([high, less, high], axis=0)


def eliminate(panel, first):
    row = rows_of((8, 128))
    scale = [jnp.zeros((8, 128), F32) for _ in range(4)]
    for group in range(4):
        cols = []
        for t in range(8):
            lane = first + group * 8 + t
            cols.append(
                [
                    jnp.broadcast_to(panel[g][0][:, lane : lane + 1], (8, 128)) if g >= group else None
                    for g in range(4)
                ]
            )
        for t in range(8):
            pivot = lax.rsqrt(jnp.broadcast_to(cols[t][group][t : t + 1], (8, 128)))
            scale[group] = jnp.where(row == t, pivot, scale[group])
            inv = pivot * pivot
            mult = [None if g < group else cols[t][g] * inv for g in range(4)]
            mult[group] = jnp.where(row > t, mult[group], 0.0)
            for t2 in range(t + 1, 8):
                top = jnp.broadcast_to(cols[t2][group][t : t + 1], (8, 128))
                for g in range(group, 4):
                    cols[t2][g] = cols[t2][g] - mult[g] * top
            for c in range(len(panel[0])):
                top = jnp.broadcast_to(panel[group][c][t : t + 1], (8, 128))
                for g in range(group, 4):
                    panel[g][c] = panel[g][c] - mult[g] * top
    return jnp.concatenate(
        [jnp.concatenate([piece * scale[g] for piece in panel[g]], axis=1) for g in range(4)], axis=0
    )


def factor_and_invert(work):
    size = work.shape[0]
    flip = ((0,), (0,))
    for k in range(size // 128):
        c0 = k * 128
        width = size + 128 + c0
        for q in range(4):
            r = c0 + q * 32
            panel = [
                [work[r + 8 * g : r + 8 * g + 8, c : c + 128] for c in range(c0, width, 128)]
                for g in range(4)
            ]
            done = eliminate(panel, q * 32)
            work[r : r + 32, c0:width] = done
            if q < 3:
                a, b = split_rows(done)
                less = dot_by(a[:, 0:128], b, flip)
                work[r + 32 : c0 + 128, c0:width] -= less[q * 32 + 32 : 128]
        if c0 + 128 < size:
            a, b = split_rows(work[c0 : c0 + 128, c0:width])
            for i in range(c0 + 128, size, 128):
                work[i : i + 128, i:width] -= dot_by(
                    a[:, i - c0 : i - c0 + 128], b[:, i - c0 :], flip
                )


def tile_list(size):
    return [(i, j) for i in range(size // 128) for j in range(i, size // 128)]


def factor_kernel(at_ref, block_ref, reg_ref, out_ref, work):
    size = out_ref.shape[0]
    square = (128, 128)
    eye = lanes(square) == rows_of(square)
    work[:, size:] = jnp.zeros((size, size), F32)
    for at, (i, j) in enumerate(tile_list(size)):
        value = block_ref[at * 128 : at * 128 + 128, :]
        if i == j:
            value = value + jnp.where(eye, reg_ref[0, :, i * 128 : i * 128 + 128], 0.0)
            work[i * 128 : i * 128 + 128, size + i * 128 : size + i * 128 + 128] = jnp.where(eye, 1.0, 0.0)
        work[i * 128 : i * 128 + 128, j * 128 : j * 128 + 128] = value
    factor_and_invert(work)
    out_ref[...] = work[:, size:]


def whole(shape):
    return pl.BlockSpec(shape, lambda i, at: (0,) * len(shape))


def factor_inverse(at, block, reg):
    size = reg.shape[-1]
    return pl.pallas_call(
        factor_kernel,
        out_shape=jax.ShapeDtypeStruct((size, size), F32),
        grid_spec=pltpu.PrefetchScalarGridSpec(
            num_scalar_prefetch=1,
            grid=(1,),
            in_specs=[whole(block.shape), pl.BlockSpec((1, 1, size), lambda i, at: (at[0], 0, 0))],
            out_specs=whole((size, size)),
            scratch_shapes=[pltpu.VMEM((size, 2 * size), F32)],
        ),
        compiler_params=pltpu.CompilerParams(vmem_limit_bytes=KERNEL_VMEM),
        cost_estimate=pl.CostEstimate(flops=30_000_000_000, bytes_accessed=60_000_000, transcendentals=0),
    )(at, block, reg)


def apply_kernel(at_ref, arrived_ref, own_ref, inverse_ref, reg_ref, out_ref):
    total = own_ref[...]
    for part in range(arrived_ref.shape[0]):
        total = total + jnp.where(at_ref[2] == part, 0.0, arrived_ref[part].astype(F32))
    on = rows_of(total.shape) + at_ref[1] == lanes(total.shape)
    total = total + jnp.where(on, reg_ref[0], 0.0)
    out_ref[...] = dot3(halves(total), halves(inverse_ref[...]), ((1,), (1,)))


def apply_inverse(at, arrived, own, inverse, reg):
    share, size = own.shape
    return pl.pallas_call(
        apply_kernel,
        out_shape=jax.ShapeDtypeStruct((share, size), F32),
        grid_spec=pltpu.PrefetchScalarGridSpec(
            num_scalar_prefetch=1,
            grid=(1,),
            in_specs=[
                whole(arrived.shape),
                whole(own.shape),
                whole(inverse.shape),
                pl.BlockSpec((1, 1, size), lambda i, at: (at[0], 0, 0)),
            ],
            out_specs=whole((share, size)),
        ),
        compiler_params=pltpu.CompilerParams(vmem_limit_bytes=KERNEL_VMEM),
    )(at, arrived, own, inverse, reg)


def window_kernel(at_ref, on_ref, design_ref, out_ref):
    part = pl.program_id(0)
    for arc in range(out_ref.shape[0]):
        on = on_ref[part * out_ref.shape[0] + arc] > 0
        out_ref[arc] = jnp.where(on, design_ref[arc], jnp.zeros((), BF))


def window_of(at, on, design):
    arcs, observed, _ = design.shape
    parts = at.shape[0]
    block = (arcs, observed, BLK)
    return pl.pallas_call(
        window_kernel,
        out_shape=jax.ShapeDtypeStruct((arcs, observed, parts * BLK), BF),
        grid_spec=pltpu.PrefetchScalarGridSpec(
            num_scalar_prefetch=2,
            grid=(parts,),
            in_specs=[pl.BlockSpec(block, lambda i, at, on: (0, 0, at[i]))],
            out_specs=pl.BlockSpec(block, lambda i, at, on: (0, 0, i)),
        ),
        compiler_params=pltpu.CompilerParams(vmem_limit_bytes=KERNEL_VMEM),
    )(at, on, design)


def gram_kernel(on_ref, design_ref, qh_ref, ql_ref, out_ref):
    arcs = design_ref.shape[0]
    out_ref[...] = jnp.zeros_like(out_ref)
    for arc in range(arcs):

        @pl.when(on_ref[pl.program_id(0) * arcs + arc] > 0)
        def _():
            flip = ((0,), (0,))
            out_ref[...] += dot_by(design_ref[arc], qh_ref[arc], flip) + dot_by(
                design_ref[arc], ql_ref[arc], flip
            )


def gram_of(on, design, high, less):
    arcs, observed, columns = design.shape
    width = high.shape[2]
    return pl.pallas_call(
        gram_kernel,
        out_shape=jax.ShapeDtypeStruct((columns, width), F32),
        grid_spec=pltpu.PrefetchScalarGridSpec(
            num_scalar_prefetch=1,
            grid=(columns // BLK,),
            in_specs=[
                pl.BlockSpec((arcs, observed, BLK), lambda i, on: (0, 0, i)),
                whole(high.shape),
                whole(less.shape),
            ],
            out_specs=pl.BlockSpec((BLK, width), lambda i, on: (i, 0)),
        ),
        compiler_params=pltpu.CompilerParams(vmem_limit_bytes=KERNEL_VMEM),
    )(on, design, high, less)


MESH = pl.DeviceIdType.MESH


def remote(src, dst, send, recv, device):
    return pltpu.make_async_remote_copy(
        src_ref=src, dst_ref=dst, send_sem=send, recv_sem=recv, device_id=device, device_id_type=MESH
    )


def meet(devices):
    barrier = pltpu.get_barrier_semaphore()
    for device in devices:
        pl.semaphore_signal(barrier, inc=1, device_id=device, device_id_type=MESH)
    pl.semaphore_wait(barrier, len(devices))


def ring_pair(slot, me, axis, send, recv):
    mine = slot(me)
    return [
        remote(mine, mine, send.at[d], recv.at[d], {axis: lax.rem(me + step, 4)})
        for d, step in enumerate((1, 3))
    ]


def ring_far(first, second, me, axis, send, recv):
    left, right = lax.rem(me + 3, 4), lax.rem(me + 1, 4)
    one, two = first(left), second(right)
    return [
        remote(one, one, send.at[2], recv.at[2], {axis: right}),
        remote(two, two, send.at[3], recv.at[3], {axis: left}),
    ]


def spread_kernel(
    cov_ref, win_ref, fac_ref, rhs_ref, slabs, got1, got2, gotz, sum1, sum2,
    ls, lr, m1s, m1r, m2s, m2r, mzs, mzr, gls, glr, gms, gmr,
):
    z, x, y = (lax.axis_index(name) for name in ("par_0", "par_1", "par_2"))
    arcs = cov_ref.shape[0]
    turned = lambda v: v + z * (3 - 2 * v)
    outer = [(x, "par_1"), (y, "par_2")]
    inner = [(y, "par_2"), (x, "par_1")]
    partner = {"par_0": 1 - z, "par_1": 3 - x, "par_2": 3 - y}
    ring = [{"par_1": lax.rem(x + k, 4)} for k in (1, 2, 3)] + [
        {"par_2": lax.rem(y + k, 4)} for k in (1, 2, 3)
    ]
    meet(ring + [{"par_0": 1 - z}, partner])

    small = turned(x) + 1
    held = small + z * (9 - 2 * small)

    def piece(c):
        return remote(slabs.at[z, c], slabs.at[z, c], ls.at[c], lr.at[c], partner)

    def came(c):
        return remote(slabs.at[1 - z, c], slabs.at[1 - z, c], ls.at[c], lr.at[c], partner)

    last = cov_ref[:, :, pl.ds(pl.multiple_of((held - 1) * 128, 128), 128)]
    slabs[z, 8] = (last - last.astype(BF).astype(F32)).astype(BF)
    for c in range(8):
        slabs[z, c] = cov_ref[:, :, c * 128 : c * 128 + 128].astype(BF)
    pl.loop(0, held)(lambda c: piece(c).start())
    piece(8).start()
    scatter1 = [
        remote(
            win_ref.at[arc, pl.ds(pl.multiple_of(lax.rem(outer[arc][0] + k, 4) * 256, 256), 256)],
            got1.at[arc, k - 1], m1s.at[arc, k - 1], m1r.at[arc, k - 1],
            {outer[arc][1]: lax.rem(outer[arc][0] + k, 4)},
        )
        for k in (1, 3, 2) for arc in range(arcs)
    ]
    for copy in scatter1:
        copy.start()
    pl.loop(0, 9 - held)(lambda c: came(c).wait_recv())
    came(8).wait_recv()
    for arc in range(arcs):
        place = 4 * turned(outer[arc][0]) + turned(inner[arc][0])

        @pl.loop(0, small - 1)
        def _(c):
            fac_ref[arc, place, c] = slabs[0, c, arc]

        @pl.loop(0, 8 - small)
        def _(c):
            fac_ref[arc, place, small - 1 + c] = slabs[1, c, arc]

        fac_ref[arc, place, 7] = slabs[0, small - 1, arc]
        fac_ref[arc, place, 8] = slabs[0, 8, arc]
        fac_ref[arc, place, 9] = slabs[1, 8 - small, arc]
        fac_ref[arc, place, 10] = slabs[1, 8, arc]

    def l_unit(arc, cut=slice(0, 11)):
        size = cut.stop - cut.start
        return lambda r: fac_ref.at[
            arc, 4 * turned(outer[arc][0]) + turned(r), pl.ds(cut.start, size)
        ]

    def l_group(arc, low=0, size=4):
        return lambda r: fac_ref.at[arc, pl.ds(4 * turned(r) + low, size)]

    def m_rows(arc, unit, base, low, size):
        return lambda r: rhs_ref.at[arc, pl.ds(pl.multiple_of(base + r * unit + low, 32), size)]

    def m_unit(arc, low=0, size=64):
        return m_rows(arc, 64, outer[arc][0] * 256, low, size)

    def m_group(arc, low=0, size=256):
        return m_rows(arc, 256, 0, low, size)

    def begin(copies):
        for copy in copies:
            copy.start()
        return copies

    def arrive(copies):
        for copy in copies:
            copy.wait_recv()
        return copies

    two = range(arcs)
    sent = list(scatter1)
    near = lambda slot, ax, stage, s, r: [
        copy for arc in two
        for copy in ring_pair(slot(arc), *ax[arc], s.at[arc, stage], r.at[arc, stage])
    ]
    far = lambda first, second, ax, stage, s, r: [
        copy for arc in two
        for copy in ring_far(first(arc), second(arc), *ax[arc], s.at[arc, stage], r.at[arc, stage])
    ]
    l1 = begin(near(l_unit, inner, 0, gls, glr))
    arrive(scatter1)
    scatter2 = []
    for arc in two:
        own = win_ref[arc, pl.ds(pl.multiple_of(outer[arc][0] * 256, 256), 256), :]
        sum1[arc] = (own + got1[arc, 0]) + (got1[arc, 1] + got1[arc, 2])
        i, axis = inner[arc]
        for k in (1, 3, 2):
            to = lax.rem(i + k, 4)
            scatter2 += begin([
                remote(
                    sum1.at[arc, pl.ds(pl.multiple_of(to * 64, 64), 64)],
                    got2.at[arc, k - 1], m2s.at[arc, k - 1], m2r.at[arc, k - 1], {axis: to},
                )
            ])
    arrive(l1)
    l2 = begin(far(lambda a: l_unit(a, slice(0, 6)), lambda a: l_unit(a, slice(6, 11)), inner, 0, gls, glr))
    arrive(scatter2)
    across = []
    for arc in two:
        own = sum1[arc, pl.ds(pl.multiple_of(inner[arc][0] * 64, 64), 64), :]
        sum2[arc] = (own + got2[arc, 0]) + (got2[arc, 1] + got2[arc, 2])
        across += begin([remote(sum2.at[arc], gotz.at[arc], mzs.at[arc], mzr.at[arc], {"par_0": 1 - z})])
    arrive(l2)
    l3 = begin(near(l_group, outer, 1, gls, glr))
    arrive(across)
    for arc in two:
        spot = pl.ds(pl.multiple_of(outer[arc][0] * 256 + inner[arc][0] * 64, 64), 64)
        rhs_ref[arc, spot, :] = sum2[arc] + gotz[arc]
    g1 = begin(near(m_unit, inner, 0, gms, gmr))
    arrive(g1)
    g2 = begin(far(lambda a: m_unit(a, 0, 32), lambda a: m_unit(a, 32, 32), inner, 0, gms, gmr))
    arrive(g2)
    g3 = begin(near(m_group, outer, 1, gms, gmr))
    arrive(l3)
    l4 = begin(far(lambda a: l_group(a, 0, 2), lambda a: l_group(a, 2, 2), outer, 1, gls, glr))
    arrive(g3)
    g4 = begin(far(lambda a: m_group(a, 0, 128), lambda a: m_group(a, 128, 128), outer, 1, gms, gmr))
    arrive(l4)
    arrive(g4)
    pl.loop(0, held)(lambda c: piece(c).wait_send())
    piece(8).wait_send()
    for copy in sent + scatter2 + across + l1 + l2 + l3 + l4 + g1 + g2 + g3 + g4:
        copy.wait_send()


def spread(cov, window):
    arcs, lines, size = cov.shape
    _, observed, width = window.shape
    vm, dma = pltpu.VMEM, pltpu.SemaphoreType.DMA
    return pl.pallas_call(
        spread_kernel,
        out_shape=(
            jax.ShapeDtypeStruct((arcs, 16, 11, lines, 128), BF),
            jax.ShapeDtypeStruct(window.shape, BF),
        ),
        in_specs=[pl.BlockSpec(memory_space=vm)] * 2,
        out_specs=(pl.BlockSpec(memory_space=vm),) * 2,
        scratch_shapes=[
            vm((2, 9, arcs, lines, 128), BF),
            vm((arcs, 3, 256, width), BF),
            vm((arcs, 3, 64, width), BF),
            vm((arcs, 64, width), BF),
            vm((arcs, 256, width), BF),
            vm((arcs, 64, width), BF),
            dma((9,)), dma((9,)),
            dma((arcs, 3)), dma((arcs, 3)), dma((arcs, 3)), dma((arcs, 3)),
            dma((arcs,)), dma((arcs,)),
            dma((arcs, 2, 4)), dma((arcs, 2, 4)), dma((arcs, 2, 4)), dma((arcs, 2, 4)),
        ],
        compiler_params=pltpu.CompilerParams(
            vmem_limit_bytes=KERNEL_VMEM, collective_id=0, has_side_effects=True
        ),
    )(cov, window)


def total_kernel(
    part_ref, gram_ref, out_ref, sum_ref, own_ref, kept, mate, got, pair,
    ps, pr, qs, qr, rs, rr, gs, gr, fs, fr,
):
    chip, core = lax.axis_index("line"), lax.axis_index("core")
    other = {"core": 1 - core}
    chips = [lax.rem(chip + k, 4) for k in (1, 2, 3)]
    peers = [{"line": c} for c in chips]
    meet(peers + [other])
    half = part_ref.shape[0] // 2
    quarter = half // 4
    rows = lambda base, n: pl.ds(pl.multiple_of(base, 32), n)
    swap = remote(part_ref.at[rows((1 - core) * half, half)], mate, ps, pr, other)
    swap.start()
    trade = remote(gram_ref.at[:, 1 - core], pair, qs, qr, other)
    trade.start()
    swap.wait_recv()
    kept[...] = part_ref[rows(core * half, half), :] + mate[...]
    scatter = [
        remote(kept.at[rows(c * quarter, quarter)], got.at[k], rs.at[k], rr.at[k], peer)
        for k, (c, peer) in enumerate(zip(chips, peers))
    ]
    for copy in scatter:
        copy.start()
    trade.wait_recv()
    for c in range(4):
        sum_ref[c] = (gram_ref[c, core] + pair[c]).astype(BF)
    own_ref[...] = gram_ref[chip, core] + pair[chip]
    for copy in scatter:
        copy.wait_recv()
    mine = rows(core * half + chip * quarter, quarter)
    out_ref[mine, :] = (kept[rows(chip * quarter, quarter), :] + got[0]) + (got[1] + got[2])
    gather = [
        remote(out_ref.at[mine], out_ref.at[mine], gs.at[k], gr.at[k], peer)
        for k, peer in enumerate(peers)
    ]
    forward = [remote(out_ref.at[mine], out_ref.at[mine], fs.at[0], fr.at[0], other)]
    for copy in gather + forward:
        copy.start()
    for k in range(3):
        gather[k].wait_recv()
        came = rows(core * half + lax.rem(chip + 3 - k, 4) * quarter, quarter)
        copy = remote(out_ref.at[came], out_ref.at[came], fs.at[k + 1], fr.at[k + 1], other)
        copy.start()
        forward.append(copy)
    for copy in forward:
        copy.wait_recv()
    for copy in [swap, trade] + scatter + gather + forward:
        copy.wait_send()


def total_over_arc(part, gram):
    lines, width = part.shape
    chips, _, share, size = gram.shape
    vm, dma = pltpu.VMEM, pltpu.SemaphoreType.DMA
    return pl.pallas_call(
        total_kernel,
        out_shape=(
            jax.ShapeDtypeStruct(part.shape, F32),
            jax.ShapeDtypeStruct((chips, share, size), BF),
            jax.ShapeDtypeStruct((share, size), F32),
        ),
        in_specs=[pl.BlockSpec(memory_space=vm)] * 2,
        out_specs=(pl.BlockSpec(memory_space=vm),) * 3,
        scratch_shapes=[
            vm((lines // 2, width), F32),
            vm((lines // 2, width), F32),
            vm((3, lines // 8, width), F32),
            vm((chips, share, size), F32),
            dma, dma, dma, dma, dma((3,)), dma((3,)), dma((3,)), dma((3,)), dma((4,)), dma((4,)),
        ],
        compiler_params=pltpu.CompilerParams(
            vmem_limit_bytes=KERNEL_VMEM, collective_id=1, has_side_effects=True
        ),
    )(part, gram)


PANEL = 512
BLK = 256
PAR = ("par_0", "par_1", "par_2")


def on_device(design, cov_factor, active_blocks, panel_index, reg_diag):
    arcs, observed, columns = design.shape
    local_blocks = columns // BLK
    par_id = lax.axis_index(PAR)
    chip, core = lax.axis_index("line"), lax.axis_index("core")
    start = panel_index[0] * PANEL
    block_ids = par_id * local_blocks + jnp.arange(local_blocks, dtype=jnp.int32)
    hits = jnp.any(active_blocks[:, :, None] == block_ids[None, None, :], axis=1)
    parts = jnp.arange(PANEL // BLK, dtype=jnp.int32)
    wanted = panel_index[0] * (PANEL // BLK) + parts
    local = wanted - par_id * local_blocks
    inside = (local >= 0) & (local < local_blocks)
    active = jnp.any(active_blocks[None] == wanted[:, None, None], axis=2)
    window = window_of(
        jnp.clip(local, 0, local_blocks - 1),
        (inside[:, None] & active).astype(jnp.int32).reshape(-1),
        design,
    )
    factor, raw = spread(cov_factor, window)
    block, high, less = solve_twice(factor, raw)
    gram = gram_of(hits.T.astype(jnp.int32).reshape(-1), design, high, less)
    share = columns // (4 * 2)
    block, sums, own = total_over_arc(block, gram.reshape(4, 2, share, PANEL))
    arrived = lax.all_to_all(sums, "line", split_axis=0, concat_axis=0, tiled=True)
    reg = reg_diag.reshape(-1, 1, PANEL)
    shift = par_id * columns + (chip * 2 + core) * share - start
    at = jnp.stack([panel_index[0], shift, chip]).astype(jnp.int32)
    inverse = factor_inverse(at, block, reg)
    return apply_inverse(at, arrived, own, inverse, reg).T


def solution(mesh):
    split = Mesh(
        mesh.devices.reshape(mesh.shape["arc"] // 2, 2, 2, 4, 4), ("line", "core") + PAR
    )
    arc = ("line", "core")
    return jax.shard_map(
        on_device,
        mesh=split,
        in_specs=(P(arc, None, PAR), P(arc, PAR, None), P(arc, None), P(), P()),
        out_specs=P(None, PAR + arc),
        check_vma=False,
    )
```

```python
import functools
import jax
import jax.numpy as jnp
from jax import lax
from jax.experimental import pallas as pl
from jax.experimental.pallas import tpu as pltpu
from jax.sharding import Mesh
from jax.sharding import PartitionSpec as P

OBS_STEP = 256
GROUP = 8
BF = jnp.bfloat16
F32 = jnp.float32
KERNEL_VMEM = 56 * 1024 * 1024


def halves(value):
    high = value.astype(BF)
    return high, (value - high.astype(F32)).astype(BF)


def dot_by(a, b, dims):
    return lax.dot_general(a, b, (dims, ((), ())), preferred_element_type=F32)


def dot3(a, b, dims=((1,), (0,))):
    (ah, al), (bh, bl) = a, b
    return dot_by(ah, bh, dims) + (dot_by(ah, bl, dims) + dot_by(al, bh, dims))


def lanes(shape):
    return lax.broadcasted_iota(jnp.int32, shape, 1)


def rows_of(shape):
    return lax.broadcasted_iota(jnp.int32, shape, 0)


def invert_tiles(tiles):
    lane = lanes((8, 128))
    row = rows_of((8, 128))
    base = lane - lax.rem(lane, 32)
    packed, inverse, scales = [], [], []
    for tile in tiles:
        pack, inv, scale = [], [], jnp.zeros((8, 128), F32)
        for g in range(4):
            piece = tile[96 + 8 * g : 104 + 8 * g]
            for part in (2, 1, 0):
                low = 32 * part + 8 * g
                piece = jnp.where(base == 32 * part, tile[low : low + 8], piece)
            pivot = 1.0 / jnp.take_along_axis(piece, base + row + 8 * g, axis=1)
            on = lane - base == row + 8 * g
            scale = scale + jnp.where(on, pivot, 0.0)
            pack.append(piece * pivot)
            inv.append(jnp.where(on, 1.0, 0.0).astype(F32))
        packed.append(pack)
        inverse.append(inv)
        scales.append(jnp.sum(scale, axis=0, keepdims=True))
    for j in range(31):
        at, sub = j // 8, j % 8
        index = base + j
        for pack, inv in zip(packed, inverse):
            top = jnp.broadcast_to(inv[at][sub : sub + 1], (8, 128))
            for g in range(at, 4):
                coef = jnp.take_along_axis(pack[g], index, axis=1)
                if g == at:
                    coef = jnp.where(row > sub, coef, 0.0)
                inv[g] = inv[g] - coef * top
    wide = lanes((32, 128)) // 32
    zero = jnp.zeros((32, 128), F32)
    results = []
    for tile, inv, scale in zip(tiles, inverse, scales):
        value = jnp.concatenate(inv, axis=0) * scale
        parts = [jnp.where(wide == g, value, 0.0) for g in range(4)]
        cross = [jnp.where(wide == g - 1, tile[32 * g : 32 * g + 32], 0.0) for g in (1, 3)]
        left = dot3(halves(jnp.concatenate(cross, axis=0)), halves(jnp.concatenate(parts, axis=0)))
        left = jnp.concatenate([zero, left[:32], zero, left[32:]], axis=0)
        odd = jnp.concatenate([parts[1], parts[3]], axis=0)
        odd = odd - dot3(halves(odd), halves(left))
        first = jnp.concatenate([parts[0], odd[:32]], axis=0)
        second = jnp.concatenate([parts[2], odd[32:]], axis=0)
        half = jnp.concatenate([first, second], axis=0)
        cross = jnp.where(lanes((64, 128)) < 64, tile[64:], 0.0)
        left = dot3(halves(cross), halves(half))
        left = jnp.concatenate([jnp.zeros_like(left), left], axis=0)
        results.append(jnp.concatenate([first, second - dot3(halves(second), halves(left))], axis=0))
    return results


def dot2(a, b, dims=((1,), (0,))):
    bh, bl = b
    return dot_by(a, bh, dims) + dot_by(a, bl, dims)


def spot_of(arc, slab):
    big = slab // 16
    pair = slab + big * (31 - 2 * slab)
    far = pair // 4
    near = pair - 4 * far
    place = (1 - arc) * (4 * far + near) + arc * (4 * near + far)
    return place, big, big * far


def tile_of(ref, arc, row, column):
    pieces = []
    for i in range(4):
        place, _, shift = spot_of(arc, 4 * row + i)
        pieces.append(ref[arc, place, shift + column])
    return jnp.concatenate(pieces, axis=0)


def diagonal_of(ref, arc, row):
    pieces = []
    for i in range(4):
        place, big, _ = spot_of(arc, 4 * row + i)
        pieces.append(
            ref[arc, place, 7 + 2 * big].astype(F32) + ref[arc, place, 8 + 2 * big].astype(F32)
        )
    return jnp.concatenate(pieces, axis=0)


def solve_kernel(arcs, factor_ref, rhs_ref, block_ref, qh_ref, ql_ref, inv, fh, wh, wl, yh, yl):
    size = rhs_ref.shape[1]
    tiles = size // 128

    @pl.loop(0, arcs * tiles // GROUP)
    def _(step):
        found = []
        for part in range(GROUP):
            at = step * GROUP + part
            arc, tile = at // tiles, lax.rem(at, tiles)
            spot = pl.ds(pl.multiple_of(tile * 128, 128), 128)
            found.append((arc, spot, tile))
        done = invert_tiles([diagonal_of(factor_ref, arc, tile) for arc, spot, tile in found])
        for (arc, spot, _), value in zip(found, done):
            inv[arc, spot, :] = value

    blocks = size // OBS_STEP
    for arc in range(arcs):
        for b in range(blocks):
            r = b * OBS_STEP
            one, two = inv[arc, r : r + 128, :], inv[arc, r + 128 : r + 256, :]
            cross = tile_of(factor_ref, arc, 2 * b + 1, 2 * b)
            corner = -dot3(halves(two), halves(dot2(cross, halves(one))))
            zero = jnp.zeros((128, 128), BF)
            for (ref, a, c, d) in zip((wh, wl), halves(one), halves(corner), halves(two)):
                ref[arc, r : r + 128, 0:128] = a
                ref[arc, r : r + 128, 128:256] = zero
                ref[arc, r + 128 : r + 256, 0:128] = c
                ref[arc, r + 128 : r + 256, 128:256] = d
            for row in (2 * b, 2 * b + 1):
                for column in range(2 * b):
                    fh[arc, row * 128 : row * 128 + 128, column * 128 : column * 128 + 128] = tile_of(
                        factor_ref, arc, row, column
                    )

    for b in range(blocks):
        r = b * OBS_STEP
        here = slice(r, r + OBS_STEP)
        for arc in range(arcs):
            value = rhs_ref[arc, here, :].astype(F32)
            if b:
                value = value - dot2(fh[arc, here, 0:r], (yh[arc, 0:r, :], yl[arc, 0:r, :]))
            value = dot3((wh[arc, here, :], wl[arc, here, :]), halves(value))
            high, less = halves(value)
            yh[arc, here, :] = high
            yl[arc, here, :] = less
    flip = ((0,), (0,))
    for b in reversed(range(blocks)):
        r = b * OBS_STEP
        here, after = slice(r, r + OBS_STEP), slice(r + OBS_STEP, size)
        for arc in range(arcs):
            value = yh[arc, here, :].astype(F32) + yl[arc, here, :].astype(F32)
            if b + 1 < blocks:
                value = value - dot2(
                    fh[arc, after, here], (qh_ref[arc, after, :], ql_ref[arc, after, :]), flip
                )
            value = dot3((wh[arc, here, :], wl[arc, here, :]), halves(value), flip)
            qh_ref[arc, here, :], ql_ref[arc, here, :] = halves(value)
    at = 0
    for i in range(0, rhs_ref.shape[2], 128):
        strip = sum(dot_by(yh[arc, :, i : i + 128], yh[arc, :, i:], flip) for arc in range(arcs))
        for j in range(0, strip.shape[1], 128):
            block_ref[at : at + 128, :] = strip[:, j : j + 128]
            at += 128


def solve_twice(factor, rhs):
    arcs, size, width = rhs.shape
    vm = pltpu.VMEM
    out = jax.ShapeDtypeStruct(rhs.shape, BF)
    tiles = len(tile_list(width))
    return pl.pallas_call(
        functools.partial(solve_kernel, arcs),
        out_shape=(jax.ShapeDtypeStruct((tiles * 128, 128), F32), out, out),
        in_specs=[pl.BlockSpec(memory_space=vm)] * 2,
        out_specs=(pl.BlockSpec(memory_space=vm),) * 3,
        scratch_shapes=[
            vm((arcs, size, 128), F32),
            vm((arcs, size, size), BF),
            vm((arcs, size, OBS_STEP), BF),
            vm((arcs, size, OBS_STEP), BF),
            vm((arcs, size, width), BF),
            vm((arcs, size, width), BF),
        ],
        compiler_params=pltpu.CompilerParams(vmem_limit_bytes=KERNEL_VMEM),
    )(factor, rhs)


def split_rows(u):
    high, less = halves(u)
    return jnp.concatenate([high, high, less], axis=0), jnp.concatenate([high, less, high], axis=0)


def eliminate(panel, first):
    row = rows_of((8, 128))
    scale = [jnp.zeros((8, 128), F32) for _ in range(4)]
    for group in range(4):
        cols = []
        for t in range(8):
            lane = first + group * 8 + t
            cols.append(
                [
                    jnp.broadcast_to(panel[g][0][:, lane : lane + 1], (8, 128)) if g >= group else None
                    for g in range(4)
                ]
            )
        for t in range(8):
            pivot = lax.rsqrt(jnp.broadcast_to(cols[t][group][t : t + 1], (8, 128)))
            scale[group] = jnp.where(row == t, pivot, scale[group])
            inv = pivot * pivot
            mult = [None if g < group else cols[t][g] * inv for g in range(4)]
            mult[group] = jnp.where(row > t, mult[group], 0.0)
            for t2 in range(t + 1, 8):
                top = jnp.broadcast_to(cols[t2][group][t : t + 1], (8, 128))
                for g in range(group, 4):
                    cols[t2][g] = cols[t2][g] - mult[g] * top
            for c in range(len(panel[0])):
                top = jnp.broadcast_to(panel[group][c][t : t + 1], (8, 128))
                for g in range(group, 4):
                    panel[g][c] = panel[g][c] - mult[g] * top
    return jnp.concatenate(
        [jnp.concatenate([piece * scale[g] for piece in panel[g]], axis=1) for g in range(4)], axis=0
    )


def factor_and_invert(work):
    size = work.shape[0]
    flip = ((0,), (0,))
    for k in range(size // 128):
        c0 = k * 128
        width = size + 128 + c0
        for q in range(4):
            r = c0 + q * 32
            panel = [
                [work[r + 8 * g : r + 8 * g + 8, c : c + 128] for c in range(c0, width, 128)]
                for g in range(4)
            ]
            done = eliminate(panel, q * 32)
            work[r : r + 32, c0:width] = done
            if q < 3:
                a, b = split_rows(done)
                less = dot_by(a[:, 0:128], b, flip)
                work[r + 32 : c0 + 128, c0:width] -= less[q * 32 + 32 : 128]
        if c0 + 128 < size:
            a, b = split_rows(work[c0 : c0 + 128, c0:width])
            for i in range(c0 + 128, size, 128):
                work[i : i + 128, i:width] -= dot_by(
                    a[:, i - c0 : i - c0 + 128], b[:, i - c0 :], flip
                )


def tile_list(size):
    return [(i, j) for i in range(size // 128) for j in range(i, size // 128)]


def factor_kernel(at_ref, block_ref, reg_ref, out_ref, work):
    size = out_ref.shape[0]
    square = (128, 128)
    eye = lanes(square) == rows_of(square)
    work[:, size:] = jnp.zeros((size, size), F32)
    for at, (i, j) in enumerate(tile_list(size)):
        value = block_ref[at * 128 : at * 128 + 128, :]
        if i == j:
            value = value + jnp.where(eye, reg_ref[0, :, i * 128 : i * 128 + 128], 0.0)
            work[i * 128 : i * 128 + 128, size + i * 128 : size + i * 128 + 128] = jnp.where(eye, 1.0, 0.0)
        work[i * 128 : i * 128 + 128, j * 128 : j * 128 + 128] = value
    factor_and_invert(work)
    out_ref[...] = work[:, size:]


def whole(shape):
    return pl.BlockSpec(shape, lambda i, at: (0,) * len(shape))


def factor_inverse(at, block, reg):
    size = reg.shape[-1]
    return pl.pallas_call(
        factor_kernel,
        out_shape=jax.ShapeDtypeStruct((size, size), F32),
        grid_spec=pltpu.PrefetchScalarGridSpec(
            num_scalar_prefetch=1,
            grid=(1,),
            in_specs=[whole(block.shape), pl.BlockSpec((1, 1, size), lambda i, at: (at[0], 0, 0))],
            out_specs=whole((size, size)),
            scratch_shapes=[pltpu.VMEM((size, 2 * size), F32)],
        ),
        compiler_params=pltpu.CompilerParams(vmem_limit_bytes=KERNEL_VMEM),
        cost_estimate=pl.CostEstimate(flops=30_000_000_000, bytes_accessed=60_000_000, transcendentals=0),
    )(at, block, reg)


def apply_kernel(at_ref, arrived_ref, own_ref, inverse_ref, reg_ref, out_ref):
    total = own_ref[...]
    for part in range(arrived_ref.shape[0]):
        total = total + jnp.where(at_ref[2] == part, 0.0, arrived_ref[part].astype(F32))
    on = rows_of(total.shape) + at_ref[1] == lanes(total.shape)
    total = total + jnp.where(on, reg_ref[0], 0.0)
    out_ref[...] = dot3(halves(total), halves(inverse_ref[...]), ((1,), (1,)))


def apply_inverse(at, arrived, own, inverse, reg):
    share, size = own.shape
    return pl.pallas_call(
        apply_kernel,
        out_shape=jax.ShapeDtypeStruct((share, size), F32),
        grid_spec=pltpu.PrefetchScalarGridSpec(
            num_scalar_prefetch=1,
            grid=(1,),
            in_specs=[
                whole(arrived.shape),
                whole(own.shape),
                whole(inverse.shape),
                pl.BlockSpec((1, 1, size), lambda i, at: (at[0], 0, 0)),
            ],
            out_specs=whole((share, size)),
        ),
        compiler_params=pltpu.CompilerParams(vmem_limit_bytes=KERNEL_VMEM),
    )(at, arrived, own, inverse, reg)


def window_kernel(at_ref, on_ref, design_ref, out_ref):
    part = pl.program_id(0)
    for arc in range(out_ref.shape[0]):
        on = on_ref[part * out_ref.shape[0] + arc] > 0
        out_ref[arc] = jnp.where(on, design_ref[arc], jnp.zeros((), BF))


def window_of(at, on, design):
    arcs, observed, _ = design.shape
    parts = at.shape[0]
    block = (arcs, observed, BLK)
    return pl.pallas_call(
        window_kernel,
        out_shape=jax.ShapeDtypeStruct((arcs, observed, parts * BLK), BF),
        grid_spec=pltpu.PrefetchScalarGridSpec(
            num_scalar_prefetch=2,
            grid=(parts,),
            in_specs=[pl.BlockSpec(block, lambda i, at, on: (0, 0, at[i]))],
            out_specs=pl.BlockSpec(block, lambda i, at, on: (0, 0, i)),
        ),
        compiler_params=pltpu.CompilerParams(vmem_limit_bytes=KERNEL_VMEM),
    )(at, on, design)


MESH = pl.DeviceIdType.MESH


def remote(src, dst, send, recv, device):
    return pltpu.make_async_remote_copy(
        src_ref=src, dst_ref=dst, send_sem=send, recv_sem=recv, device_id=device, device_id_type=MESH
    )


def meet(devices):
    barrier = pltpu.get_barrier_semaphore()
    for device in devices:
        pl.semaphore_signal(barrier, inc=1, device_id=device, device_id_type=MESH)
    pl.semaphore_wait(barrier, len(devices))


def ring_pair(slot, me, axis, send, recv):
    mine = slot(me)
    return [
        remote(mine, mine, send.at[d], recv.at[d], {axis: lax.rem(me + step, 4)})
        for d, step in enumerate((1, 3))
    ]


def ring_far(first, second, me, axis, send, recv):
    left, right = lax.rem(me + 3, 4), lax.rem(me + 1, 4)
    one, two = first(left), second(right)
    return [
        remote(one, one, send.at[2], recv.at[2], {axis: right}),
        remote(two, two, send.at[3], recv.at[3], {axis: left}),
    ]


def spread_kernel(
    cov_ref, win_ref, fac_ref, rhs_ref, slabs, got1, got2, gotz, sum1, sum2,
    ls, lr, m1s, m1r, m2s, m2r, mzs, mzr, gls, glr, gms, gmr,
):
    z, x, y = (lax.axis_index(name) for name in ("par_0", "par_1", "par_2"))
    arcs = cov_ref.shape[0]
    turned = lambda v: v + z * (3 - 2 * v)
    outer = [(x, "par_1"), (y, "par_2")]
    inner = [(y, "par_2"), (x, "par_1")]
    partner = {"par_0": 1 - z, "par_1": 3 - x, "par_2": 3 - y}
    ring = [{"par_1": lax.rem(x + k, 4)} for k in (1, 2, 3)] + [
        {"par_2": lax.rem(y + k, 4)} for k in (1, 2, 3)
    ]
    meet(ring + [{"par_0": 1 - z}, partner])

    small = turned(x) + 1
    held = small + z * (9 - 2 * small)

    def piece(c):
        return remote(slabs.at[z, c], slabs.at[z, c], ls.at[c], lr.at[c], partner)

    def came(c):
        return remote(slabs.at[1 - z, c], slabs.at[1 - z, c], ls.at[c], lr.at[c], partner)

    last = cov_ref[:, :, pl.ds(pl.multiple_of((held - 1) * 128, 128), 128)]
    slabs[z, 8] = (last - last.astype(BF).astype(F32)).astype(BF)
    for c in range(8):
        slabs[z, c] = cov_ref[:, :, c * 128 : c * 128 + 128].astype(BF)
    pl.loop(0, held)(lambda c: piece(c).start())
    piece(8).start()
    scatter1 = [
        remote(
            win_ref.at[arc, pl.ds(pl.multiple_of(lax.rem(outer[arc][0] + k, 4) * 256, 256), 256)],
            got1.at[arc, k - 1], m1s.at[arc, k - 1], m1r.at[arc, k - 1],
            {outer[arc][1]: lax.rem(outer[arc][0] + k, 4)},
        )
        for k in (1, 3, 2) for arc in range(arcs)
    ]
    for copy in scatter1:
        copy.start()
    pl.loop(0, 9 - held)(lambda c: came(c).wait_recv())
    came(8).wait_recv()
    for arc in range(arcs):
        place = 4 * turned(outer[arc][0]) + turned(inner[arc][0])

        @pl.loop(0, small - 1)
        def _(c):
            fac_ref[arc, place, c] = slabs[0, c, arc]

        @pl.loop(0, 8 - small)
        def _(c):
            fac_ref[arc, place, small - 1 + c] = slabs[1, c, arc]

        fac_ref[arc, place, 7] = slabs[0, small - 1, arc]
        fac_ref[arc, place, 8] = slabs[0, 8, arc]
        fac_ref[arc, place, 9] = slabs[1, 8 - small, arc]
        fac_ref[arc, place, 10] = slabs[1, 8, arc]

    def l_unit(arc, cut=slice(0, 11)):
        size = cut.stop - cut.start
        return lambda r: fac_ref.at[
            arc, 4 * turned(outer[arc][0]) + turned(r), pl.ds(cut.start, size)
        ]

    def l_group(arc, low=0, size=4):
        return lambda r: fac_ref.at[arc, pl.ds(4 * turned(r) + low, size)]

    def m_rows(arc, unit, base, low, size):
        return lambda r: rhs_ref.at[arc, pl.ds(pl.multiple_of(base + r * unit + low, 32), size)]

    def m_unit(arc, low=0, size=64):
        return m_rows(arc, 64, outer[arc][0] * 256, low, size)

    def m_group(arc, low=0, size=256):
        return m_rows(arc, 256, 0, low, size)

    def begin(copies):
        for copy in copies:
            copy.start()
        return copies

    def arrive(copies):
        for copy in copies:
            copy.wait_recv()
        return copies

    two = range(arcs)
    sent = list(scatter1)
    near = lambda slot, ax, stage, s, r: [
        copy for arc in two
        for copy in ring_pair(slot(arc), *ax[arc], s.at[arc, stage], r.at[arc, stage])
    ]
    far = lambda first, second, ax, stage, s, r: [
        copy for arc in two
        for copy in ring_far(first(arc), second(arc), *ax[arc], s.at[arc, stage], r.at[arc, stage])
    ]
    l1 = begin(near(l_unit, inner, 0, gls, glr))
    arrive(scatter1)
    scatter2 = []
    for arc in two:
        own = win_ref[arc, pl.ds(pl.multiple_of(outer[arc][0] * 256, 256), 256), :]
        sum1[arc] = (own + got1[arc, 0]) + (got1[arc, 1] + got1[arc, 2])
        i, axis = inner[arc]
        for k in (1, 3, 2):
            to = lax.rem(i + k, 4)
            scatter2 += begin([
                remote(
                    sum1.at[arc, pl.ds(pl.multiple_of(to * 64, 64), 64)],
                    got2.at[arc, k - 1], m2s.at[arc, k - 1], m2r.at[arc, k - 1], {axis: to},
                )
            ])
    arrive(l1)
    l2 = begin(far(lambda a: l_unit(a, slice(0, 6)), lambda a: l_unit(a, slice(6, 11)), inner, 0, gls, glr))
    arrive(scatter2)
    across = []
    for arc in two:
        own = sum1[arc, pl.ds(pl.multiple_of(inner[arc][0] * 64, 64), 64), :]
        sum2[arc] = (own + got2[arc, 0]) + (got2[arc, 1] + got2[arc, 2])
        across += begin([remote(sum2.at[arc], gotz.at[arc], mzs.at[arc], mzr.at[arc], {"par_0": 1 - z})])
    arrive(l2)
    l3 = begin(near(l_group, outer, 1, gls, glr))
    arrive(across)
    for arc in two:
        spot = pl.ds(pl.multiple_of(outer[arc][0] * 256 + inner[arc][0] * 64, 64), 64)
        rhs_ref[arc, spot, :] = sum2[arc] + gotz[arc]
    g1 = begin(near(m_unit, inner, 0, gms, gmr))
    arrive(g1)
    g2 = begin(far(lambda a: m_unit(a, 0, 32), lambda a: m_unit(a, 32, 32), inner, 0, gms, gmr))
    arrive(g2)
    g3 = begin(near(m_group, outer, 1, gms, gmr))
    arrive(l3)
    l4 = begin(far(lambda a: l_group(a, 0, 2), lambda a: l_group(a, 2, 2), outer, 1, gls, glr))
    arrive(g3)
    g4 = begin(far(lambda a: m_group(a, 0, 128), lambda a: m_group(a, 128, 128), outer, 1, gms, gmr))
    arrive(l4)
    arrive(g4)
    pl.loop(0, held)(lambda c: piece(c).wait_send())
    piece(8).wait_send()
    for copy in sent + scatter2 + across + l1 + l2 + l3 + l4 + g1 + g2 + g3 + g4:
        copy.wait_send()


def spread(cov, window):
    arcs, lines, size = cov.shape
    _, observed, width = window.shape
    vm, dma = pltpu.VMEM, pltpu.SemaphoreType.DMA
    return pl.pallas_call(
        spread_kernel,
        out_shape=(
            jax.ShapeDtypeStruct((arcs, 16, 11, lines, 128), BF),
            jax.ShapeDtypeStruct(window.shape, BF),
        ),
        in_specs=[pl.BlockSpec(memory_space=vm)] * 2,
        out_specs=(pl.BlockSpec(memory_space=vm),) * 2,
        scratch_shapes=[
            vm((2, 9, arcs, lines, 128), BF),
            vm((arcs, 3, 256, width), BF),
            vm((arcs, 3, 64, width), BF),
            vm((arcs, 64, width), BF),
            vm((arcs, 256, width), BF),
            vm((arcs, 64, width), BF),
            dma((9,)), dma((9,)),
            dma((arcs, 3)), dma((arcs, 3)), dma((arcs, 3)), dma((arcs, 3)),
            dma((arcs,)), dma((arcs,)),
            dma((arcs, 2, 4)), dma((arcs, 2, 4)), dma((arcs, 2, 4)), dma((arcs, 2, 4)),
        ],
        compiler_params=pltpu.CompilerParams(
            vmem_limit_bytes=KERNEL_VMEM, collective_id=0, has_side_effects=True
        ),
    )(cov, window)


def total_kernel(
    on_ref, part_ref, design_ref, high_ref, less_ref, out_ref, sum_ref, own_ref, gram, kept, mate, got, pair,
    ps, pr, qs, qr, rs, rr, gs, gr, fs, fr,
):
    chip, core = lax.axis_index("line"), lax.axis_index("core")
    other = {"core": 1 - core}
    chips = [lax.rem(chip + k, 4) for k in (1, 2, 3)]
    peers = [{"line": c} for c in chips]
    meet(peers + [other])
    half = part_ref.shape[0] // 2
    quarter = half // 4
    rows = lambda base, n: pl.ds(pl.multiple_of(base, 32), n)
    arcs, _, columns = design_ref.shape
    width = high_ref.shape[2]
    share = gram.shape[2]
    swap = remote(part_ref.at[rows((1 - core) * half, half)], mate, ps, pr, other)
    swap.start()

    def product(block):
        flip = ((0,), (0,))
        total = jnp.zeros((BLK, width), F32)
        for arc in range(arcs):
            piece = design_ref[arc, :, block * BLK : block * BLK + BLK]
            on = on_ref[block * arcs + arc].astype(F32)
            one = dot_by(piece, high_ref[arc], flip) + dot_by(piece, less_ref[arc], flip)
            total = total + one * on
        low = block * BLK
        while low < block * BLK + BLK:
            at = low // share
            stop = min((at + 1) * share, block * BLK + BLK)
            gram[at // 2, at % 2, low - at * share : stop - at * share, :] = total[
                low - block * BLK : stop - block * BLK
            ]
            low = stop

    blocks = columns // BLK
    product(0)
    swap.wait_recv()
    kept[...] = part_ref[rows(core * half, half), :] + mate[...]
    scatter = [
        remote(kept.at[rows(c * quarter, quarter)], got.at[k], rs.at[k], rr.at[k], peer)
        for k, (c, peer) in enumerate(zip(chips, peers))
    ]
    for copy in scatter:
        copy.start()
    for block in range(1, blocks):
        product(block)
    trade = remote(gram.at[:, 1 - core], pair, qs, qr, other)
    trade.start()
    for copy in scatter:
        copy.wait_recv()
    mine = rows(core * half + chip * quarter, quarter)
    out_ref[mine, :] = (kept[rows(chip * quarter, quarter), :] + got[0]) + (got[1] + got[2])
    gather = [
        remote(out_ref.at[mine], out_ref.at[mine], gs.at[k], gr.at[k], peer)
        for k, peer in enumerate(peers)
    ]
    forward = [remote(out_ref.at[mine], out_ref.at[mine], fs.at[0], fr.at[0], other)]
    for copy in gather + forward:
        copy.start()
    trade.wait_recv()
    for c in range(4):
        sum_ref[c] = (gram[c, core] + pair[c]).astype(BF)
    own_ref[...] = gram[chip, core] + pair[chip]
    for k in range(3):
        gather[k].wait_recv()
        came = rows(core * half + lax.rem(chip + 3 - k, 4) * quarter, quarter)
        copy = remote(out_ref.at[came], out_ref.at[came], fs.at[k + 1], fr.at[k + 1], other)
        copy.start()
        forward.append(copy)
    for copy in forward:
        copy.wait_recv()
    for copy in [swap, trade] + scatter + gather + forward:
        copy.wait_send()


def total_over_arc(on, part, design, high, less):
    lines, width = part.shape
    size = high.shape[2]
    chips = 4
    share = design.shape[2] // (2 * chips)
    vm, dma = pltpu.VMEM, pltpu.SemaphoreType.DMA
    return pl.pallas_call(
        total_kernel,
        out_shape=(
            jax.ShapeDtypeStruct(part.shape, F32),
            jax.ShapeDtypeStruct((chips, share, size), BF),
            jax.ShapeDtypeStruct((share, size), F32),
        ),
        in_specs=[pl.BlockSpec(memory_space=pltpu.SMEM)] + [pl.BlockSpec(memory_space=vm)] * 4,
        out_specs=(pl.BlockSpec(memory_space=vm),) * 3,
        scratch_shapes=[
            vm((chips, 2, share, size), F32),
            vm((lines // 2, width), F32),
            vm((lines // 2, width), F32),
            vm((3, lines // 8, width), F32),
            vm((chips, share, size), F32),
            dma, dma, dma, dma, dma((3,)), dma((3,)), dma((3,)), dma((3,)), dma((4,)), dma((4,)),
        ],
        compiler_params=pltpu.CompilerParams(
            vmem_limit_bytes=KERNEL_VMEM, collective_id=1, has_side_effects=True
        ),
    )(on, part, design, high, less)


PANEL = 512
BLK = 256
PAR = ("par_0", "par_1", "par_2")


def on_device(design, cov_factor, active_blocks, panel_index, reg_diag):
    arcs, observed, columns = design.shape
    local_blocks = columns // BLK
    par_id = lax.axis_index(PAR)
    chip, core = lax.axis_index("line"), lax.axis_index("core")
    start = panel_index[0] * PANEL
    block_ids = par_id * local_blocks + jnp.arange(local_blocks, dtype=jnp.int32)
    hits = jnp.any(active_blocks[:, :, None] == block_ids[None, None, :], axis=1)
    parts = jnp.arange(PANEL // BLK, dtype=jnp.int32)
    wanted = panel_index[0] * (PANEL // BLK) + parts
    local = wanted - par_id * local_blocks
    inside = (local >= 0) & (local < local_blocks)
    active = jnp.any(active_blocks[None] == wanted[:, None, None], axis=2)
    window = window_of(
        jnp.clip(local, 0, local_blocks - 1),
        (inside[:, None] & active).astype(jnp.int32).reshape(-1),
        design,
    )
    factor, raw = spread(cov_factor, window)
    block, high, less = solve_twice(factor, raw)
    share = columns // (4 * 2)
    on = hits.T.astype(jnp.int32).reshape(-1)
    block, sums, own = total_over_arc(on, block, design, high, less)
    arrived = lax.all_to_all(sums, "line", split_axis=0, concat_axis=0, tiled=True)
    reg = reg_diag.reshape(-1, 1, PANEL)
    shift = par_id * columns + (chip * 2 + core) * share - start
    at = jnp.stack([panel_index[0], shift, chip]).astype(jnp.int32)
    inverse = factor_inverse(at, block, reg)
    return apply_inverse(at, arrived, own, inverse, reg).T


def solution(mesh):
    split = Mesh(
        mesh.devices.reshape(mesh.shape["arc"] // 2, 2, 2, 4, 4), ("line", "core") + PAR
    )
    arc = ("line", "core")
    return jax.shard_map(
        on_device,
        mesh=split,
        in_specs=(P(arc, None, PAR), P(arc, PAR, None), P(arc, None), P(), P()),
        out_specs=P(None, PAR + arc),
        check_vma=False,
    )
```

```python
import functools
import jax
import jax.numpy as jnp
from jax import lax
from jax.experimental import pallas as pl
from jax.experimental.pallas import tpu as pltpu
from jax.sharding import Mesh
from jax.sharding import PartitionSpec as P

OBS_STEP = 256
GROUP = 8
BF = jnp.bfloat16
F32 = jnp.float32
KERNEL_VMEM = 56 * 1024 * 1024


def halves(value):
    high = value.astype(BF)
    return high, (value - high.astype(F32)).astype(BF)


def dot_by(a, b, dims):
    return lax.dot_general(a, b, (dims, ((), ())), preferred_element_type=F32)


def dot3(a, b, dims=((1,), (0,))):
    (ah, al), (bh, bl) = a, b
    return dot_by(ah, bh, dims) + (dot_by(ah, bl, dims) + dot_by(al, bh, dims))


def lanes(shape):
    return lax.broadcasted_iota(jnp.int32, shape, 1)


def rows_of(shape):
    return lax.broadcasted_iota(jnp.int32, shape, 0)


def invert_tiles(tiles):
    lane = lanes((8, 128))
    row = rows_of((8, 128))
    base = lane - lax.rem(lane, 32)
    packed, inverse, scales = [], [], []
    for tile in tiles:
        pack, inv, scale = [], [], jnp.zeros((8, 128), F32)
        for g in range(4):
            piece = tile[96 + 8 * g : 104 + 8 * g]
            for part in (2, 1, 0):
                low = 32 * part + 8 * g
                piece = jnp.where(base == 32 * part, tile[low : low + 8], piece)
            pivot = 1.0 / jnp.take_along_axis(piece, base + row + 8 * g, axis=1)
            on = lane - base == row + 8 * g
            scale = scale + jnp.where(on, pivot, 0.0)
            pack.append(piece * pivot)
            inv.append(jnp.where(on, 1.0, 0.0).astype(F32))
        packed.append(pack)
        inverse.append(inv)
        scales.append(jnp.sum(scale, axis=0, keepdims=True))
    for j in range(31):
        at, sub = j // 8, j % 8
        index = base + j
        for pack, inv in zip(packed, inverse):
            top = jnp.broadcast_to(inv[at][sub : sub + 1], (8, 128))
            for g in range(at, 4):
                coef = jnp.take_along_axis(pack[g], index, axis=1)
                if g == at:
                    coef = jnp.where(row > sub, coef, 0.0)
                inv[g] = inv[g] - coef * top
    wide = lanes((32, 128)) // 32
    zero = jnp.zeros((32, 128), F32)
    results = []
    for tile, inv, scale in zip(tiles, inverse, scales):
        value = jnp.concatenate(inv, axis=0) * scale
        parts = [jnp.where(wide == g, value, 0.0) for g in range(4)]
        cross = [jnp.where(wide == g - 1, tile[32 * g : 32 * g + 32], 0.0) for g in (1, 3)]
        left = dot3(halves(jnp.concatenate(cross, axis=0)), halves(jnp.concatenate(parts, axis=0)))
        left = jnp.concatenate([zero, left[:32], zero, left[32:]], axis=0)
        odd = jnp.concatenate([parts[1], parts[3]], axis=0)
        odd = odd - dot3(halves(odd), halves(left))
        first = jnp.concatenate([parts[0], odd[:32]], axis=0)
        second = jnp.concatenate([parts[2], odd[32:]], axis=0)
        half = jnp.concatenate([first, second], axis=0)
        cross = jnp.where(lanes((64, 128)) < 64, tile[64:], 0.0)
        left = dot3(halves(cross), halves(half))
        left = jnp.concatenate([jnp.zeros_like(left), left], axis=0)
        results.append(jnp.concatenate([first, second - dot3(halves(second), halves(left))], axis=0))
    return results


def dot2(a, b, dims=((1,), (0,))):
    bh, bl = b
    return dot_by(a, bh, dims) + dot_by(a, bl, dims)


def spot_of(arc, slab):
    big = slab // 16
    pair = slab + big * (31 - 2 * slab)
    far = pair // 4
    near = pair - 4 * far
    place = (1 - arc) * (4 * far + near) + arc * (4 * near + far)
    return place, big, big * far


def tile_of(ref, arc, row, column):
    pieces = []
    for i in range(4):
        place, _, shift = spot_of(arc, 4 * row + i)
        pieces.append(ref[arc, place, shift + column])
    return jnp.concatenate(pieces, axis=0)


def diagonal_of(ref, arc, row):
    pieces = []
    for i in range(4):
        place, big, _ = spot_of(arc, 4 * row + i)
        pieces.append(
            ref[arc, place, 7 + 2 * big].astype(F32) + ref[arc, place, 8 + 2 * big].astype(F32)
        )
    return jnp.concatenate(pieces, axis=0)


def invert_all(step, factor_ref, inv):
    tiles = inv.shape[1] // 128
    found = []
    for part in range(GROUP):
        at = step * GROUP + part
        arc, tile = at // tiles, lax.rem(at, tiles)
        spot = pl.ds(pl.multiple_of(tile * 128, 128), 128)
        found.append((arc, spot, tile))
    done = invert_tiles([diagonal_of(factor_ref, arc, tile) for arc, spot, tile in found])
    for (arc, spot, _), value in zip(found, done):
        inv[arc, spot, :] = value


def join_tiles(arc, factor_ref, inv, fh, wh, wl):
    for b in range(inv.shape[1] // OBS_STEP):
        r = b * OBS_STEP
        one, two = inv[arc, r : r + 128, :], inv[arc, r + 128 : r + 256, :]
        cross = tile_of(factor_ref, arc, 2 * b + 1, 2 * b)
        corner = -dot3(halves(two), halves(dot2(cross, halves(one))))
        zero = jnp.zeros((128, 128), BF)
        for ref, a, c, d in zip((wh, wl), halves(one), halves(corner), halves(two)):
            ref[arc, r : r + 128, 0:128] = a
            ref[arc, r : r + 128, 128:256] = zero
            ref[arc, r + 128 : r + 256, 0:128] = c
            ref[arc, r + 128 : r + 256, 128:256] = d
        for row in (2 * b, 2 * b + 1):
            for column in range(2 * b):
                fh[arc, row * 128 : row * 128 + 128, column * 128 : column * 128 + 128] = tile_of(
                    factor_ref, arc, row, column
                )


def solve_forward(b, rhs_ref, fh, wh, wl, yh, yl):
    r = b * OBS_STEP
    here = slice(r, r + OBS_STEP)
    for arc in range(rhs_ref.shape[0]):
        value = rhs_ref[arc, here, :].astype(F32)
        if b:
            value = value - dot2(fh[arc, here, 0:r], (yh[arc, 0:r, :], yl[arc, 0:r, :]))
        value = dot3((wh[arc, here, :], wl[arc, here, :]), halves(value))
        yh[arc, here, :], yl[arc, here, :] = halves(value)


def solve_back(b, fh, wh, wl, yh, yl, qh, ql):
    flip = ((0,), (0,))
    size = yh.shape[1]
    r = b * OBS_STEP
    here, after = slice(r, r + OBS_STEP), slice(r + OBS_STEP, size)
    for arc in range(yh.shape[0]):
        value = yh[arc, here, :].astype(F32) + yl[arc, here, :].astype(F32)
        if r + OBS_STEP < size:
            value = value - dot2(fh[arc, after, here], (qh[arc, after, :], ql[arc, after, :]), flip)
        value = dot3((wh[arc, here, :], wl[arc, here, :]), halves(value), flip)
        qh[arc, here, :], ql[arc, here, :] = halves(value)


def block_tiles(yh, block_ref):
    at = 0
    for i in range(0, yh.shape[2], 128):
        strip = sum(
            dot_by(yh[arc, :, i : i + 128], yh[arc, :, i:], ((0,), (0,))) for arc in range(yh.shape[0])
        )
        for j in range(0, strip.shape[1], 128):
            block_ref[at : at + 128, :] = strip[:, j : j + 128]
            at += 128


def split_rows(u):
    high, less = halves(u)
    return jnp.concatenate([high, high, less], axis=0), jnp.concatenate([high, less, high], axis=0)


def eliminate(panel, first):
    row = rows_of((8, 128))
    scale = [jnp.zeros((8, 128), F32) for _ in range(4)]
    for group in range(4):
        cols = []
        for t in range(8):
            lane = first + group * 8 + t
            cols.append(
                [
                    jnp.broadcast_to(panel[g][0][:, lane : lane + 1], (8, 128)) if g >= group else None
                    for g in range(4)
                ]
            )
        for t in range(8):
            pivot = lax.rsqrt(jnp.broadcast_to(cols[t][group][t : t + 1], (8, 128)))
            scale[group] = jnp.where(row == t, pivot, scale[group])
            inv = pivot * pivot
            mult = [None if g < group else cols[t][g] * inv for g in range(4)]
            mult[group] = jnp.where(row > t, mult[group], 0.0)
            for t2 in range(t + 1, 8):
                top = jnp.broadcast_to(cols[t2][group][t : t + 1], (8, 128))
                for g in range(group, 4):
                    cols[t2][g] = cols[t2][g] - mult[g] * top
            for c in range(len(panel[0])):
                top = jnp.broadcast_to(panel[group][c][t : t + 1], (8, 128))
                for g in range(group, 4):
                    panel[g][c] = panel[g][c] - mult[g] * top
    return jnp.concatenate(
        [jnp.concatenate([piece * scale[g] for piece in panel[g]], axis=1) for g in range(4)], axis=0
    )


def factor_and_invert(work):
    size = work.shape[0]
    flip = ((0,), (0,))
    for k in range(size // 128):
        c0 = k * 128
        width = size + 128 + c0
        for q in range(4):
            r = c0 + q * 32
            panel = [
                [work[r + 8 * g : r + 8 * g + 8, c : c + 128] for c in range(c0, width, 128)]
                for g in range(4)
            ]
            done = eliminate(panel, q * 32)
            work[r : r + 32, c0:width] = done
            if q < 3:
                a, b = split_rows(done)
                less = dot_by(a[:, 0:128], b, flip)
                work[r + 32 : c0 + 128, c0:width] -= less[q * 32 + 32 : 128]
        if c0 + 128 < size:
            a, b = split_rows(work[c0 : c0 + 128, c0:width])
            for i in range(c0 + 128, size, 128):
                work[i : i + 128, i:width] -= dot_by(
                    a[:, i - c0 : i - c0 + 128], b[:, i - c0 :], flip
                )


def tile_list(size):
    return [(i, j) for i in range(size // 128) for j in range(i, size // 128)]


def factor_kernel(at_ref, block_ref, reg_ref, out_ref, work):
    size = out_ref.shape[0]
    square = (128, 128)
    eye = lanes(square) == rows_of(square)
    work[:, size:] = jnp.zeros((size, size), F32)
    for at, (i, j) in enumerate(tile_list(size)):
        value = block_ref[at * 128 : at * 128 + 128, :]
        if i == j:
            value = value + jnp.where(eye, reg_ref[0, :, i * 128 : i * 128 + 128], 0.0)
            work[i * 128 : i * 128 + 128, size + i * 128 : size + i * 128 + 128] = jnp.where(eye, 1.0, 0.0)
        work[i * 128 : i * 128 + 128, j * 128 : j * 128 + 128] = value
    factor_and_invert(work)
    out_ref[...] = work[:, size:]


def whole(shape):
    return pl.BlockSpec(shape, lambda i, at: (0,) * len(shape))


def factor_inverse(at, block, reg):
    size = reg.shape[-1]
    return pl.pallas_call(
        factor_kernel,
        out_shape=jax.ShapeDtypeStruct((size, size), F32),
        grid_spec=pltpu.PrefetchScalarGridSpec(
            num_scalar_prefetch=1,
            grid=(1,),
            in_specs=[whole(block.shape), pl.BlockSpec((1, 1, size), lambda i, at: (at[0], 0, 0))],
            out_specs=whole((size, size)),
            scratch_shapes=[pltpu.VMEM((size, 2 * size), F32)],
        ),
        compiler_params=pltpu.CompilerParams(vmem_limit_bytes=KERNEL_VMEM),
        cost_estimate=pl.CostEstimate(flops=30_000_000_000, bytes_accessed=60_000_000, transcendentals=0),
    )(at, block, reg)


def apply_kernel(at_ref, arrived_ref, own_ref, inverse_ref, reg_ref, out_ref):
    total = own_ref[...]
    for part in range(arrived_ref.shape[0]):
        total = total + jnp.where(at_ref[2] == part, 0.0, arrived_ref[part].astype(F32))
    on = rows_of(total.shape) + at_ref[1] == lanes(total.shape)
    total = total + jnp.where(on, reg_ref[0], 0.0)
    out_ref[...] = dot3(halves(total), halves(inverse_ref[...]), ((1,), (1,)))


def apply_inverse(at, arrived, own, inverse, reg):
    share, size = own.shape
    return pl.pallas_call(
        apply_kernel,
        out_shape=jax.ShapeDtypeStruct((share, size), F32),
        grid_spec=pltpu.PrefetchScalarGridSpec(
            num_scalar_prefetch=1,
            grid=(1,),
            in_specs=[
                whole(arrived.shape),
                whole(own.shape),
                whole(inverse.shape),
                pl.BlockSpec((1, 1, size), lambda i, at: (at[0], 0, 0)),
            ],
            out_specs=whole((share, size)),
        ),
        compiler_params=pltpu.CompilerParams(vmem_limit_bytes=KERNEL_VMEM),
    )(at, arrived, own, inverse, reg)


def window_kernel(at_ref, on_ref, design_ref, out_ref):
    part = pl.program_id(0)
    for arc in range(out_ref.shape[0]):
        on = on_ref[part * out_ref.shape[0] + arc] > 0
        out_ref[arc] = jnp.where(on, design_ref[arc], jnp.zeros((), BF))


def window_of(at, on, design):
    arcs, observed, _ = design.shape
    parts = at.shape[0]
    block = (arcs, observed, BLK)
    return pl.pallas_call(
        window_kernel,
        out_shape=jax.ShapeDtypeStruct((arcs, observed, parts * BLK), BF),
        grid_spec=pltpu.PrefetchScalarGridSpec(
            num_scalar_prefetch=2,
            grid=(parts,),
            in_specs=[pl.BlockSpec(block, lambda i, at, on: (0, 0, at[i]))],
            out_specs=pl.BlockSpec(block, lambda i, at, on: (0, 0, i)),
        ),
        compiler_params=pltpu.CompilerParams(vmem_limit_bytes=KERNEL_VMEM),
    )(at, on, design)


MESH = pl.DeviceIdType.MESH


def remote(src, dst, send, recv, device):
    return pltpu.make_async_remote_copy(
        src_ref=src, dst_ref=dst, send_sem=send, recv_sem=recv, device_id=device, device_id_type=MESH
    )


def meet(devices):
    barrier = pltpu.get_barrier_semaphore()
    for device in devices:
        pl.semaphore_signal(barrier, inc=1, device_id=device, device_id_type=MESH)
    pl.semaphore_wait(barrier, len(devices))


def ring_pair(slot, me, axis, send, recv):
    mine = slot(me)
    return [
        remote(mine, mine, send.at[d], recv.at[d], {axis: lax.rem(me + step, 4)})
        for d, step in enumerate((1, 3))
    ]


def ring_far(first, second, me, axis, send, recv):
    left, right = lax.rem(me + 3, 4), lax.rem(me + 1, 4)
    one, two = first(left), second(right)
    return [
        remote(one, one, send.at[2], recv.at[2], {axis: right}),
        remote(two, two, send.at[3], recv.at[3], {axis: left}),
    ]


def main_kernel(
    on_ref, cov_ref, win_ref, design_hbm, out_ref, sum_ref, own_ref,
    fac_ref, rhs_ref, slabs, got1, got2, gotz, sum1, sum2, inv, fh, wh, wl, yh, yl, qh, ql, design_ref,
    part_ref, gram, kept, mate, got, pair,
    ls, lr, m1s, m1r, m2s, m2r, mzs, mzr, gls, glr, gms, gmr,
    ds, ps, pr, qs, qr, rs, rr, gs, gr, fs, fr,
):
    z, x, y = (lax.axis_index(name) for name in ("par_0", "par_1", "par_2"))
    chip, core = lax.axis_index("line"), lax.axis_index("core")
    other = {"core": 1 - core}
    chips = [lax.rem(chip + k, 4) for k in (1, 2, 3)]
    peers = [{"line": c} for c in chips]
    load = pltpu.make_async_copy(design_hbm, design_ref, ds)
    load.start()
    arcs = cov_ref.shape[0]
    turned = lambda v: v + z * (3 - 2 * v)
    outer = [(x, "par_1"), (y, "par_2")]
    inner = [(y, "par_2"), (x, "par_1")]
    partner = {"par_0": 1 - z, "par_1": 3 - x, "par_2": 3 - y}
    ring = [{"par_1": lax.rem(x + k, 4)} for k in (1, 2, 3)] + [
        {"par_2": lax.rem(y + k, 4)} for k in (1, 2, 3)
    ]
    meet(ring + [{"par_0": 1 - z}, partner] + peers + [other])

    small = turned(x) + 1
    held = small + z * (9 - 2 * small)

    def piece(c):
        return remote(slabs.at[z, c], slabs.at[z, c], ls.at[c], lr.at[c], partner)

    def came(c):
        return remote(slabs.at[1 - z, c], slabs.at[1 - z, c], ls.at[c], lr.at[c], partner)

    last = cov_ref[:, :, pl.ds(pl.multiple_of((held - 1) * 128, 128), 128)]
    slabs[z, 8] = (last - last.astype(BF).astype(F32)).astype(BF)
    for c in range(8):
        slabs[z, c] = cov_ref[:, :, c * 128 : c * 128 + 128].astype(BF)
    pl.loop(0, held)(lambda c: piece(c).start())
    piece(8).start()
    scatter1 = [
        remote(
            win_ref.at[arc, pl.ds(pl.multiple_of(lax.rem(outer[arc][0] + k, 4) * 256, 256), 256)],
            got1.at[arc, k - 1], m1s.at[arc, k - 1], m1r.at[arc, k - 1],
            {outer[arc][1]: lax.rem(outer[arc][0] + k, 4)},
        )
        for k in (1, 3, 2) for arc in range(arcs)
    ]
    for copy in scatter1:
        copy.start()
    pl.loop(0, 9 - held)(lambda c: came(c).wait_recv())
    came(8).wait_recv()
    for arc in range(arcs):
        place = 4 * turned(outer[arc][0]) + turned(inner[arc][0])

        @pl.loop(0, small - 1)
        def _(c):
            fac_ref[arc, place, c] = slabs[0, c, arc]

        @pl.loop(0, 8 - small)
        def _(c):
            fac_ref[arc, place, small - 1 + c] = slabs[1, c, arc]

        fac_ref[arc, place, 7] = slabs[0, small - 1, arc]
        fac_ref[arc, place, 8] = slabs[0, 8, arc]
        fac_ref[arc, place, 9] = slabs[1, 8 - small, arc]
        fac_ref[arc, place, 10] = slabs[1, 8, arc]

    def l_unit(arc, cut=slice(0, 11)):
        size = cut.stop - cut.start
        return lambda r: fac_ref.at[
            arc, 4 * turned(outer[arc][0]) + turned(r), pl.ds(cut.start, size)
        ]

    def l_group(arc, low=0, size=4):
        return lambda r: fac_ref.at[arc, pl.ds(4 * turned(r) + low, size)]

    def m_rows(arc, unit, base, low, size):
        return lambda r: rhs_ref.at[arc, pl.ds(pl.multiple_of(base + r * unit + low, 32), size)]

    def m_unit(arc, low=0, size=64):
        return m_rows(arc, 64, outer[arc][0] * 256, low, size)

    def m_group(arc, low=0, size=256):
        return m_rows(arc, 256, 0, low, size)

    def begin(copies):
        for copy in copies:
            copy.start()
        return copies

    def arrive(copies):
        for copy in copies:
            copy.wait_recv()
        return copies

    two = range(arcs)
    sent = list(scatter1)
    near = lambda slot, ax, stage, s, r: [
        copy for arc in two
        for copy in ring_pair(slot(arc), *ax[arc], s.at[arc, stage], r.at[arc, stage])
    ]
    far = lambda first, second, ax, stage, s, r: [
        copy for arc in two
        for copy in ring_far(first(arc), second(arc), *ax[arc], s.at[arc, stage], r.at[arc, stage])
    ]
    l1 = begin(near(l_unit, inner, 0, gls, glr))
    arrive(scatter1)
    scatter2 = []
    for arc in two:
        own = win_ref[arc, pl.ds(pl.multiple_of(outer[arc][0] * 256, 256), 256), :]
        sum1[arc] = (own + got1[arc, 0]) + (got1[arc, 1] + got1[arc, 2])
        i, axis = inner[arc]
        for k in (1, 3, 2):
            to = lax.rem(i + k, 4)
            scatter2 += begin([
                remote(
                    sum1.at[arc, pl.ds(pl.multiple_of(to * 64, 64), 64)],
                    got2.at[arc, k - 1], m2s.at[arc, k - 1], m2r.at[arc, k - 1], {axis: to},
                )
            ])
    arrive(l1)
    l2 = begin(far(lambda a: l_unit(a, slice(0, 6)), lambda a: l_unit(a, slice(6, 11)), inner, 0, gls, glr))
    arrive(scatter2)
    across = []
    for arc in two:
        own = sum1[arc, pl.ds(pl.multiple_of(inner[arc][0] * 64, 64), 64), :]
        sum2[arc] = (own + got2[arc, 0]) + (got2[arc, 1] + got2[arc, 2])
        across += begin([remote(sum2.at[arc], gotz.at[arc], mzs.at[arc], mzr.at[arc], {"par_0": 1 - z})])
    arrive(l2)
    l3 = begin(near(l_group, outer, 1, gls, glr))
    arrive(across)
    for arc in two:
        spot = pl.ds(pl.multiple_of(outer[arc][0] * 256 + inner[arc][0] * 64, 64), 64)
        rhs_ref[arc, spot, :] = sum2[arc] + gotz[arc]
    g1 = begin(near(m_unit, inner, 0, gms, gmr))
    arrive(g1)
    g2 = begin(far(lambda a: m_unit(a, 0, 32), lambda a: m_unit(a, 32, 32), inner, 0, gms, gmr))
    arrive(g2)
    g3 = begin(near(m_group, outer, 1, gms, gmr))
    arrive(l3)
    l4 = begin(far(lambda a: l_group(a, 0, 2), lambda a: l_group(a, 2, 2), outer, 1, gls, glr))
    arrive(l4)
    invert_all(0, fac_ref, inv)
    arrive(g3)
    g4 = begin(far(lambda a: m_group(a, 0, 128), lambda a: m_group(a, 128, 128), outer, 1, gms, gmr))
    invert_all(1, fac_ref, inv)
    for arc in two:
        join_tiles(arc, fac_ref, inv, fh, wh, wl)
    arrive(g4)
    blocks = rhs_ref.shape[1] // OBS_STEP
    for b in range(blocks):
        solve_forward(b, rhs_ref, fh, wh, wl, yh, yl)
    block_tiles(yh, part_ref)

    half = part_ref.shape[0] // 2
    quarter = half // 4
    rows = lambda base, n: pl.ds(pl.multiple_of(base, 32), n)
    columns = design_ref.shape[2]
    width = qh.shape[2]
    share = gram.shape[2]
    swap = remote(part_ref.at[rows((1 - core) * half, half)], mate, ps, pr, other)
    swap.start()

    def product(block):
        flip = ((0,), (0,))
        total = jnp.zeros((BLK, width), F32)
        for arc in range(arcs):
            piece = design_ref[arc, :, block * BLK : block * BLK + BLK]
            on = on_ref[block * arcs + arc].astype(F32)
            one = dot_by(piece, qh[arc], flip) + dot_by(piece, ql[arc], flip)
            total = total + one * on
        low = block * BLK
        while low < block * BLK + BLK:
            at = low // share
            stop = min((at + 1) * share, block * BLK + BLK)
            gram[at // 2, at % 2, low - at * share : stop - at * share, :] = total[
                low - block * BLK : stop - block * BLK
            ]
            low = stop

    for b in reversed(range(1, blocks)):
        solve_back(b, fh, wh, wl, yh, yl, qh, ql)
        if b == blocks - 1:
            swap.wait_recv()
            kept[...] = part_ref[rows(core * half, half), :] + mate[...]
            scatter = begin([
                remote(kept.at[rows(c * quarter, quarter)], got.at[k], rs.at[k], rr.at[k], peer)
                for k, (c, peer) in enumerate(zip(chips, peers))
            ])
    solve_back(0, fh, wh, wl, yh, yl, qh, ql)
    load.wait()
    product(0)
    product(1)
    arrive(scatter)
    mine = rows(core * half + chip * quarter, quarter)
    out_ref[mine, :] = (kept[rows(chip * quarter, quarter), :] + got[0]) + (got[1] + got[2])
    gather = begin([
        remote(out_ref.at[mine], out_ref.at[mine], gs.at[k], gr.at[k], peer)
        for k, peer in enumerate(peers)
    ])
    forward = begin([remote(out_ref.at[mine], out_ref.at[mine], fs.at[0], fr.at[0], other)])
    for block in range(2, columns // BLK):
        product(block)
    trade = remote(gram.at[:, 1 - core], pair, qs, qr, other)
    trade.start()
    for k in range(3):
        gather[k].wait_recv()
        from_chip = rows(core * half + lax.rem(chip + 3 - k, 4) * quarter, quarter)
        forward += begin([
            remote(out_ref.at[from_chip], out_ref.at[from_chip], fs.at[k + 1], fr.at[k + 1], other)
        ])
    trade.wait_recv()
    for c in range(4):
        sum_ref[c] = (gram[c, core] + pair[c]).astype(BF)
    own_ref[...] = gram[chip, core] + pair[chip]
    arrive(forward)
    pl.loop(0, held)(lambda c: piece(c).wait_send())
    piece(8).wait_send()
    for copy in sent + scatter2 + across + l1 + l2 + l3 + l4 + g1 + g2 + g3 + g4:
        copy.wait_send()
    for copy in [swap, trade] + scatter + gather + forward:
        copy.wait_send()


def block_and_gram(on, cov, window, design):
    arcs, lines, size = cov.shape
    _, observed, width = window.shape
    chips = 4
    share = design.shape[2] // (2 * chips)
    total = len(tile_list(width)) * 128
    vm, dma = pltpu.VMEM, pltpu.SemaphoreType.DMA
    return pl.pallas_call(
        main_kernel,
        out_shape=(
            jax.ShapeDtypeStruct((total, 128), F32),
            jax.ShapeDtypeStruct((chips, share, width), BF),
            jax.ShapeDtypeStruct((share, width), F32),
        ),
        in_specs=[pl.BlockSpec(memory_space=pltpu.SMEM)]
        + [pl.BlockSpec(memory_space=vm)] * 2
        + [pl.BlockSpec(memory_space=pl.ANY)],
        out_specs=(pl.BlockSpec(memory_space=vm),) * 3,
        scratch_shapes=[
            vm((arcs, 16, 11, lines, 128), BF),
            vm((arcs, size, width), BF),
            vm((2, 9, arcs, lines, 128), BF),
            vm((arcs, 3, 256, width), BF),
            vm((arcs, 3, 64, width), BF),
            vm((arcs, 64, width), BF),
            vm((arcs, 256, width), BF),
            vm((arcs, 64, width), BF),
            vm((arcs, size, 128), F32),
            vm((arcs, size, size), BF),
            vm((arcs, size, OBS_STEP), BF),
            vm((arcs, size, OBS_STEP), BF),
            vm((arcs, size, width), BF),
            vm((arcs, size, width), BF),
            vm((arcs, size, width), BF),
            vm((arcs, size, width), BF),
            vm(design.shape, BF),
            vm((total, 128), F32),
            vm((chips, 2, share, width), F32),
            vm((total // 2, 128), F32),
            vm((total // 2, 128), F32),
            vm((3, total // 8, 128), F32),
            vm((chips, share, width), F32),
            dma((9,)), dma((9,)),
            dma((arcs, 3)), dma((arcs, 3)), dma((arcs, 3)), dma((arcs, 3)),
            dma((arcs,)), dma((arcs,)),
            dma((arcs, 2, 4)), dma((arcs, 2, 4)), dma((arcs, 2, 4)), dma((arcs, 2, 4)),
            dma, dma, dma, dma, dma, dma((3,)), dma((3,)), dma((3,)), dma((3,)), dma((4,)), dma((4,)),
        ],
        compiler_params=pltpu.CompilerParams(
            vmem_limit_bytes=KERNEL_VMEM, collective_id=0, has_side_effects=True
        ),
    )(on, cov, window, design)


PANEL = 512
BLK = 256
PAR = ("par_0", "par_1", "par_2")


def on_device(design, cov_factor, active_blocks, panel_index, reg_diag):
    arcs, observed, columns = design.shape
    local_blocks = columns // BLK
    par_id = lax.axis_index(PAR)
    chip, core = lax.axis_index("line"), lax.axis_index("core")
    start = panel_index[0] * PANEL
    block_ids = par_id * local_blocks + jnp.arange(local_blocks, dtype=jnp.int32)
    hits = jnp.any(active_blocks[:, :, None] == block_ids[None, None, :], axis=1)
    parts = jnp.arange(PANEL // BLK, dtype=jnp.int32)
    wanted = panel_index[0] * (PANEL // BLK) + parts
    local = wanted - par_id * local_blocks
    inside = (local >= 0) & (local < local_blocks)
    active = jnp.any(active_blocks[None] == wanted[:, None, None], axis=2)
    window = window_of(
        jnp.clip(local, 0, local_blocks - 1),
        (inside[:, None] & active).astype(jnp.int32).reshape(-1),
        design,
    )
    share = columns // (4 * 2)
    on = hits.T.astype(jnp.int32).reshape(-1)
    block, sums, own = block_and_gram(on, cov_factor, window, design)
    arrived = lax.all_to_all(sums, "line", split_axis=0, concat_axis=0, tiled=True)
    reg = reg_diag.reshape(-1, 1, PANEL)
    shift = par_id * columns + (chip * 2 + core) * share - start
    at = jnp.stack([panel_index[0], shift, chip]).astype(jnp.int32)
    inverse = factor_inverse(at, block, reg)
    return apply_inverse(at, arrived, own, inverse, reg).T


def solution(mesh):
    split = Mesh(
        mesh.devices.reshape(mesh.shape["arc"] // 2, 2, 2, 4, 4), ("line", "core") + PAR
    )
    arc = ("line", "core")
    return jax.shard_map(
        on_device,
        mesh=split,
        in_specs=(P(arc, None, PAR), P(arc, PAR, None), P(arc, None), P(), P()),
        out_specs=P(None, PAR + arc),
        check_vma=False,
    )
```

```python
import functools
import jax
import jax.numpy as jnp
from jax import lax
from jax.experimental import pallas as pl
from jax.experimental.pallas import tpu as pltpu
from jax.sharding import Mesh
from jax.sharding import PartitionSpec as P

OBS_STEP = 256
GROUP = 8
PARTS = 2
PART = 512 // PARTS
ORDER = "lablablablabablabl0ab1ab2"
BF = jnp.bfloat16
F32 = jnp.float32
KERNEL_VMEM = 56 * 1024 * 1024


def halves(value):
    high = value.astype(BF)
    return high, (value - high.astype(F32)).astype(BF)


def dot_by(a, b, dims):
    return lax.dot_general(a, b, (dims, ((), ())), preferred_element_type=F32)


def dot3(a, b, dims=((1,), (0,))):
    (ah, al), (bh, bl) = a, b
    return dot_by(ah, bh, dims) + (dot_by(ah, bl, dims) + dot_by(al, bh, dims))


def lanes(shape):
    return lax.broadcasted_iota(jnp.int32, shape, 1)


def rows_of(shape):
    return lax.broadcasted_iota(jnp.int32, shape, 0)


def invert_tiles(tiles):
    lane = lanes((8, 128))
    row = rows_of((8, 128))
    base = lane - lax.rem(lane, 32)
    packed, inverse, scales = [], [], []
    for tile in tiles:
        pack, inv, scale = [], [], jnp.zeros((8, 128), F32)
        for g in range(4):
            piece = tile[96 + 8 * g : 104 + 8 * g]
            for part in (2, 1, 0):
                low = 32 * part + 8 * g
                piece = jnp.where(base == 32 * part, tile[low : low + 8], piece)
            pivot = 1.0 / jnp.take_along_axis(piece, base + row + 8 * g, axis=1)
            on = lane - base == row + 8 * g
            scale = scale + jnp.where(on, pivot, 0.0)
            pack.append(piece * pivot)
            inv.append(jnp.where(on, 1.0, 0.0).astype(F32))
        packed.append(pack)
        inverse.append(inv)
        scales.append(jnp.sum(scale, axis=0, keepdims=True))
    for j in range(31):
        at, sub = j // 8, j % 8
        index = base + j
        for pack, inv in zip(packed, inverse):
            top = jnp.broadcast_to(inv[at][sub : sub + 1], (8, 128))
            for g in range(at, 4):
                coef = jnp.take_along_axis(pack[g], index, axis=1)
                if g == at:
                    coef = jnp.where(row > sub, coef, 0.0)
                inv[g] = inv[g] - coef * top
    wide = lanes((32, 128)) // 32
    zero = jnp.zeros((32, 128), F32)
    results = []
    for tile, inv, scale in zip(tiles, inverse, scales):
        value = jnp.concatenate(inv, axis=0) * scale
        parts = [jnp.where(wide == g, value, 0.0) for g in range(4)]
        cross = [jnp.where(wide == g - 1, tile[32 * g : 32 * g + 32], 0.0) for g in (1, 3)]
        left = dot3(halves(jnp.concatenate(cross, axis=0)), halves(jnp.concatenate(parts, axis=0)))
        left = jnp.concatenate([zero, left[:32], zero, left[32:]], axis=0)
        odd = jnp.concatenate([parts[1], parts[3]], axis=0)
        odd = odd - dot3(halves(odd), halves(left))
        first = jnp.concatenate([parts[0], odd[:32]], axis=0)
        second = jnp.concatenate([parts[2], odd[32:]], axis=0)
        half = jnp.concatenate([first, second], axis=0)
        cross = jnp.where(lanes((64, 128)) < 64, tile[64:], 0.0)
        left = dot3(halves(cross), halves(half))
        left = jnp.concatenate([jnp.zeros_like(left), left], axis=0)
        results.append(jnp.concatenate([first, second - dot3(halves(second), halves(left))], axis=0))
    return results


def dot2(a, b, dims=((1,), (0,))):
    bh, bl = b
    return dot_by(a, bh, dims) + dot_by(a, bl, dims)


def spot_of(arc, slab):
    big = slab // 16
    pair = slab + big * (31 - 2 * slab)
    far = pair // 4
    near = pair - 4 * far
    place = (1 - arc) * (4 * far + near) + arc * (4 * near + far)
    return place, big, big * far


def tile_of(ref, arc, row, column):
    pieces = []
    for i in range(4):
        place, _, shift = spot_of(arc, 4 * row + i)
        pieces.append(ref[arc, place, shift + column])
    return jnp.concatenate(pieces, axis=0)


def diagonal_of(ref, arc, row):
    pieces = []
    for i in range(4):
        place, big, _ = spot_of(arc, 4 * row + i)
        pieces.append(
            ref[arc, place, 7 + 2 * big].astype(F32) + ref[arc, place, 8 + 2 * big].astype(F32)
        )
    return jnp.concatenate(pieces, axis=0)


def invert_all(step, factor_ref, inv):
    tiles = inv.shape[1] // 128
    found = []
    for part in range(GROUP):
        at = step * GROUP + part
        arc, tile = at // tiles, lax.rem(at, tiles)
        spot = pl.ds(pl.multiple_of(tile * 128, 128), 128)
        found.append((arc, spot, tile))
    done = invert_tiles([diagonal_of(factor_ref, arc, tile) for arc, spot, tile in found])
    for (arc, spot, _), value in zip(found, done):
        inv[arc, spot, :] = value


def join_tiles(arc, factor_ref, inv, fh, wh, wl):
    for b in range(inv.shape[1] // OBS_STEP):
        r = b * OBS_STEP
        one, two = inv[arc, r : r + 128, :], inv[arc, r + 128 : r + 256, :]
        cross = tile_of(factor_ref, arc, 2 * b + 1, 2 * b)
        corner = -dot3(halves(two), halves(dot2(cross, halves(one))))
        zero = jnp.zeros((128, 128), BF)
        for ref, a, c, d in zip((wh, wl), halves(one), halves(corner), halves(two)):
            ref[arc, r : r + 128, 0:128] = a
            ref[arc, r : r + 128, 128:256] = zero
            ref[arc, r + 128 : r + 256, 0:128] = c
            ref[arc, r + 128 : r + 256, 128:256] = d
        for row in (2 * b, 2 * b + 1):
            for column in range(2 * b):
                fh[arc, row * 128 : row * 128 + 128, column * 128 : column * 128 + 128] = tile_of(
                    factor_ref, arc, row, column
                )


def solve_forward(b, rhs_ref, fh, wh, wl, yh, yl):
    r = b * OBS_STEP
    here = slice(r, r + OBS_STEP)
    for arc in range(rhs_ref.shape[0]):
        value = rhs_ref[arc, here, :].astype(F32)
        if b:
            value = value - dot2(fh[arc, here, 0:r], (yh[arc, 0:r, :], yl[arc, 0:r, :]))
        value = dot3((wh[arc, here, :], wl[arc, here, :]), halves(value))
        yh[arc, here, :], yl[arc, here, :] = halves(value)


def solve_back(b, fh, wh, wl, yh, yl, qh, ql):
    flip = ((0,), (0,))
    size = yh.shape[1]
    r = b * OBS_STEP
    here, after = slice(r, r + OBS_STEP), slice(r + OBS_STEP, size)
    for arc in range(yh.shape[0]):
        value = yh[arc, here, :].astype(F32) + yl[arc, here, :].astype(F32)
        if r + OBS_STEP < size:
            value = value - dot2(fh[arc, after, here], (qh[arc, after, :], ql[arc, after, :]), flip)
        value = dot3((wh[arc, here, :], wl[arc, here, :]), halves(value), flip)
        qh[arc, here, :], ql[arc, here, :] = halves(value)


def block_tiles(yh, block_ref):
    at = 0
    for i in range(0, yh.shape[2], 128):
        strip = sum(
            dot_by(yh[arc, :, i : i + 128], yh[arc, :, i:], ((0,), (0,))) for arc in range(yh.shape[0])
        )
        for j in range(0, strip.shape[1], 128):
            block_ref[at : at + 128, :] = strip[:, j : j + 128]
            at += 128


def split_rows(u):
    high, less = halves(u)
    return jnp.concatenate([high, high, less], axis=0), jnp.concatenate([high, less, high], axis=0)


def eliminate(panel, first):
    row = rows_of((8, 128))
    scale = [jnp.zeros((8, 128), F32) for _ in range(4)]
    for group in range(4):
        cols = []
        for t in range(8):
            lane = first + group * 8 + t
            cols.append(
                [
                    jnp.broadcast_to(panel[g][0][:, lane : lane + 1], (8, 128)) if g >= group else None
                    for g in range(4)
                ]
            )
        for t in range(8):
            pivot = lax.rsqrt(jnp.broadcast_to(cols[t][group][t : t + 1], (8, 128)))
            scale[group] = jnp.where(row == t, pivot, scale[group])
            inv = pivot * pivot
            mult = [None if g < group else cols[t][g] * inv for g in range(4)]
            mult[group] = jnp.where(row > t, mult[group], 0.0)
            for t2 in range(t + 1, 8):
                top = jnp.broadcast_to(cols[t2][group][t : t + 1], (8, 128))
                for g in range(group, 4):
                    cols[t2][g] = cols[t2][g] - mult[g] * top
            for c in range(len(panel[0])):
                top = jnp.broadcast_to(panel[group][c][t : t + 1], (8, 128))
                for g in range(group, 4):
                    panel[g][c] = panel[g][c] - mult[g] * top
    return jnp.concatenate(
        [jnp.concatenate([piece * scale[g] for piece in panel[g]], axis=1) for g in range(4)], axis=0
    )


def factor_and_invert(work):
    size = work.shape[0]
    flip = ((0,), (0,))
    for k in range(size // 128):
        c0 = k * 128
        width = size + 128 + c0
        for q in range(4):
            r = c0 + q * 32
            panel = [
                [work[r + 8 * g : r + 8 * g + 8, c : c + 128] for c in range(c0, width, 128)]
                for g in range(4)
            ]
            done = eliminate(panel, q * 32)
            work[r : r + 32, c0:width] = done
            if q < 3:
                a, b = split_rows(done)
                less = dot_by(a[:, 0:128], b, flip)
                work[r + 32 : c0 + 128, c0:width] -= less[q * 32 + 32 : 128]
        if c0 + 128 < size:
            a, b = split_rows(work[c0 : c0 + 128, c0:width])
            for i in range(c0 + 128, size, 128):
                work[i : i + 128, i:width] -= dot_by(
                    a[:, i - c0 : i - c0 + 128], b[:, i - c0 :], flip
                )


def tile_list(size):
    return [(i, j) for i in range(size // 128) for j in range(i, size // 128)]


def factor_kernel(at_ref, block_ref, reg_ref, out_ref, work):
    size = out_ref.shape[0]
    square = (128, 128)
    eye = lanes(square) == rows_of(square)
    work[:, size:] = jnp.zeros((size, size), F32)
    for at, (i, j) in enumerate(tile_list(size)):
        value = block_ref[at * 128 : at * 128 + 128, :]
        if i == j:
            value = value + jnp.where(eye, reg_ref[0, :, i * 128 : i * 128 + 128], 0.0)
            work[i * 128 : i * 128 + 128, size + i * 128 : size + i * 128 + 128] = jnp.where(eye, 1.0, 0.0)
        work[i * 128 : i * 128 + 128, j * 128 : j * 128 + 128] = value
    factor_and_invert(work)
    out_ref[...] = work[:, size:]


def whole(shape):
    return pl.BlockSpec(shape, lambda i, at: (0,) * len(shape))


def factor_inverse(at, block, reg):
    size = reg.shape[-1]
    return pl.pallas_call(
        factor_kernel,
        out_shape=jax.ShapeDtypeStruct((size, size), F32),
        grid_spec=pltpu.PrefetchScalarGridSpec(
            num_scalar_prefetch=1,
            grid=(1,),
            in_specs=[whole(block.shape), pl.BlockSpec((1, 1, size), lambda i, at: (at[0], 0, 0))],
            out_specs=whole((size, size)),
            scratch_shapes=[pltpu.VMEM((size, 2 * size), F32)],
        ),
        compiler_params=pltpu.CompilerParams(vmem_limit_bytes=KERNEL_VMEM),
        cost_estimate=pl.CostEstimate(flops=30_000_000_000, bytes_accessed=60_000_000, transcendentals=0),
    )(at, block, reg)


def apply_kernel(at_ref, arrived_ref, own_ref, inverse_ref, reg_ref, out_ref):
    total = own_ref[...]
    for part in range(arrived_ref.shape[0]):
        total = total + jnp.where(at_ref[2] == part, 0.0, arrived_ref[part].astype(F32))
    on = rows_of(total.shape) + at_ref[1] == lanes(total.shape)
    total = total + jnp.where(on, reg_ref[0], 0.0)
    out_ref[...] = dot3(halves(total), halves(inverse_ref[...]), ((1,), (1,)))


def apply_inverse(at, arrived, own, inverse, reg):
    share, size = own.shape
    return pl.pallas_call(
        apply_kernel,
        out_shape=jax.ShapeDtypeStruct((share, size), F32),
        grid_spec=pltpu.PrefetchScalarGridSpec(
            num_scalar_prefetch=1,
            grid=(1,),
            in_specs=[
                whole(arrived.shape),
                whole(own.shape),
                whole(inverse.shape),
                pl.BlockSpec((1, 1, size), lambda i, at: (at[0], 0, 0)),
            ],
            out_specs=whole((share, size)),
        ),
        compiler_params=pltpu.CompilerParams(vmem_limit_bytes=KERNEL_VMEM),
    )(at, arrived, own, inverse, reg)


def window_kernel(at_ref, on_ref, design_ref, out_ref):
    part = pl.program_id(0)
    for arc in range(out_ref.shape[0]):
        on = on_ref[part * out_ref.shape[0] + arc] > 0
        out_ref[arc] = jnp.where(on, design_ref[arc], jnp.zeros((), BF))


def window_of(at, on, design):
    arcs, observed, _ = design.shape
    parts = at.shape[0]
    block = (arcs, observed, BLK)
    return pl.pallas_call(
        window_kernel,
        out_shape=jax.ShapeDtypeStruct((arcs, observed, parts * BLK), BF),
        grid_spec=pltpu.PrefetchScalarGridSpec(
            num_scalar_prefetch=2,
            grid=(parts,),
            in_specs=[pl.BlockSpec(block, lambda i, at, on: (0, 0, at[i]))],
            out_specs=pl.BlockSpec(block, lambda i, at, on: (0, 0, i)),
        ),
        compiler_params=pltpu.CompilerParams(vmem_limit_bytes=KERNEL_VMEM),
    )(at, on, design)


MESH = pl.DeviceIdType.MESH


def remote(src, dst, send, recv, device):
    return pltpu.make_async_remote_copy(
        src_ref=src, dst_ref=dst, send_sem=send, recv_sem=recv, device_id=device, device_id_type=MESH
    )


def meet(devices):
    barrier = pltpu.get_barrier_semaphore()
    for device in devices:
        pl.semaphore_signal(barrier, inc=1, device_id=device, device_id_type=MESH)
    pl.semaphore_wait(barrier, len(devices))


def ring_pair(slot, me, axis, send, recv):
    mine = slot(me)
    return [
        remote(mine, mine, send.at[d], recv.at[d], {axis: lax.rem(me + step, 4)})
        for d, step in enumerate((1, 3))
    ]


def ring_far(first, second, me, axis, send, recv):
    left, right = lax.rem(me + 3, 4), lax.rem(me + 1, 4)
    one, two = first(left), second(right)
    return [
        remote(one, one, send.at[2], recv.at[2], {axis: right}),
        remote(two, two, send.at[3], recv.at[3], {axis: left}),
    ]


def main_kernel(
    on_ref, cov_ref, win_ref, design_hbm, out_ref, sum_ref, own_ref,
    fac_ref, rhs_ref, slabs, got1, got2, gotz, sum1, sum2, inv, fh, wh, wl, yh, yl, qh, ql, design_ref,
    part_ref, gram, kept, mate, got, pair,
    ls, lr, m1s, m1r, m2s, m2r, mzs, mzr, gls, glr, gms, gmr,
    ds, ps, pr, qs, qr, rs, rr, gs, gr, fs, fr,
):
    z, x, y = (lax.axis_index(name) for name in ("par_0", "par_1", "par_2"))
    chip, core = lax.axis_index("line"), lax.axis_index("core")
    other = {"core": 1 - core}
    chips = [lax.rem(chip + k, 4) for k in (1, 2, 3)]
    peers = [{"line": c} for c in chips]
    load = pltpu.make_async_copy(design_hbm, design_ref, ds)
    load.start()
    arcs = cov_ref.shape[0]
    turned = lambda v: v + z * (3 - 2 * v)
    outer = [(x, "par_1"), (y, "par_2")]
    inner = [(y, "par_2"), (x, "par_1")]
    partner = {"par_0": 1 - z, "par_1": 3 - x, "par_2": 3 - y}
    ring = [{"par_1": lax.rem(x + k, 4)} for k in (1, 2, 3)] + [
        {"par_2": lax.rem(y + k, 4)} for k in (1, 2, 3)
    ]
    meet(ring + [{"par_0": 1 - z}, partner] + peers + [other])

    small = turned(x) + 1
    held = small + z * (9 - 2 * small)
    two = range(arcs)
    sent = []

    def piece(c):
        return remote(slabs.at[z, c], slabs.at[z, c], ls.at[c], lr.at[c], partner)

    def came(c):
        return remote(slabs.at[1 - z, c], slabs.at[1 - z, c], ls.at[c], lr.at[c], partner)

    def begin(copies):
        for copy in copies:
            copy.start()
        sent.extend(copies)
        return copies

    def arrive(copies):
        for copy in copies:
            copy.wait_recv()

    def near(slot, ax, s, r):
        return begin(
            [copy for arc in two for copy in ring_pair(slot(arc), *ax[arc], s.at[arc], r.at[arc])]
        )

    def far(first, second, ax, s, r):
        return begin(
            [
                copy for arc in two
                for copy in ring_far(first(arc), second(arc), *ax[arc], s.at[arc], r.at[arc])
            ]
        )

    def l_unit(low, size):
        return lambda arc: lambda r: fac_ref.at[
            arc, 4 * turned(outer[arc][0]) + turned(r), pl.ds(low, size)
        ]

    def l_group(low, size):
        return lambda arc: lambda r: fac_ref.at[arc, pl.ds(4 * turned(r) + low, size)]

    def factor_stream():
        last = cov_ref[:, :, pl.ds(pl.multiple_of((held - 1) * 128, 128), 128)]
        slabs[z, 8] = (last - last.astype(BF).astype(F32)).astype(BF)
        for c in range(8):
            slabs[z, c] = cov_ref[:, :, c * 128 : c * 128 + 128].astype(BF)
        pl.loop(0, held)(lambda c: piece(c).start())
        piece(8).start()
        yield
        pl.loop(0, 9 - held)(lambda c: came(c).wait_recv())
        came(8).wait_recv()
        for arc in two:
            place = 4 * turned(outer[arc][0]) + turned(inner[arc][0])

            @pl.loop(0, small - 1)
            def _(c):
                fac_ref[arc, place, c] = slabs[0, c, arc]

            @pl.loop(0, 8 - small)
            def _(c):
                fac_ref[arc, place, small - 1 + c] = slabs[1, c, arc]

            fac_ref[arc, place, 7] = slabs[0, small - 1, arc]
            fac_ref[arc, place, 8] = slabs[0, 8, arc]
            fac_ref[arc, place, 9] = slabs[1, 8 - small, arc]
            fac_ref[arc, place, 10] = slabs[1, 8, arc]
        s, r = gls.at[0], glr.at[0]
        l1 = near(l_unit(0, 11), inner, s, r)
        yield
        arrive(l1)
        l2 = far(l_unit(0, 6), l_unit(6, 5), inner, s, r)
        yield
        arrive(l2)
        s, r = gls.at[1], glr.at[1]
        l3 = near(l_group(0, 4), outer, s, r)
        yield
        arrive(l3)
        l4 = far(l_group(0, 2), l_group(2, 2), outer, s, r)
        yield
        arrive(l4)
        yield

    def panel_stream(part):
        cols = pl.ds(part * PART, PART)
        lines = lambda base, n: pl.ds(pl.multiple_of(base, 32), n)

        def m_unit(low, size):
            return lambda arc: lambda r: rhs_ref.at[
                arc, lines(outer[arc][0] * 256 + r * 64 + low, size), cols
            ]

        def m_group(low, size):
            return lambda arc: lambda r: rhs_ref.at[arc, lines(r * 256 + low, size), cols]

        def to_peers(source, target, ax, unit, s, r):
            copies = []
            for k in (1, 3, 2):
                for arc in two:
                    to = lax.rem(ax[arc][0] + k, 4)
                    copies.append(
                        remote(
                            source.at[arc, lines(to * unit, unit), cols],
                            target.at[arc, k - 1, :, cols],
                            s.at[part, arc, k - 1], r.at[part, arc, k - 1], {ax[arc][1]: to},
                        )
                    )
            return begin(copies)

        scatter1 = to_peers(win_ref, got1, outer, 256, m1s, m1r)
        yield
        arrive(scatter1)
        for arc in two:
            own = win_ref[arc, lines(outer[arc][0] * 256, 256), cols]
            sum1[arc, :, cols] = (own + got1[arc, 0, :, cols]) + (
                got1[arc, 1, :, cols] + got1[arc, 2, :, cols]
            )
        scatter2 = to_peers(sum1, got2, inner, 64, m2s, m2r)
        yield
        arrive(scatter2)
        for arc in two:
            own = sum1[arc, lines(inner[arc][0] * 64, 64), cols]
            sum2[arc, :, cols] = (own + got2[arc, 0, :, cols]) + (
                got2[arc, 1, :, cols] + got2[arc, 2, :, cols]
            )
        across = begin(
            [
                remote(
                    sum2.at[arc, :, cols], gotz.at[arc, :, cols],
                    mzs.at[part, arc], mzr.at[part, arc], {"par_0": 1 - z},
                )
                for arc in two
            ]
        )
        yield
        arrive(across)
        for arc in two:
            spot = lines(outer[arc][0] * 256 + inner[arc][0] * 64, 64)
            rhs_ref[arc, spot, cols] = sum2[arc, :, cols] + gotz[arc, :, cols]
        s, r = gms.at[part, 0], gmr.at[part, 0]
        g1 = near(m_unit(0, 64), inner, s, r)
        yield
        arrive(g1)
        g2 = far(m_unit(0, 32), m_unit(32, 32), inner, s, r)
        yield
        arrive(g2)
        s, r = gms.at[part, 1], gmr.at[part, 1]
        g3 = near(m_group(0, 256), outer, s, r)
        yield
        arrive(g3)
        g4 = far(m_group(0, 128), m_group(128, 128), outer, s, r)
        yield
        arrive(g4)
        yield

    def prepare(step):
        if step < 2:
            invert_all(step, fac_ref, inv)
        else:
            for arc in two:
                join_tiles(arc, fac_ref, inv, fh, wh, wl)

    streams = {"l": factor_stream(), "a": panel_stream(0)}
    if PARTS > 1:
        streams["b"] = panel_stream(1)
    for step in ORDER:
        if step.isdigit():
            prepare(int(step))
        else:
            next(streams[step])
    blocks = rhs_ref.shape[1] // OBS_STEP
    for b in range(blocks):
        solve_forward(b, rhs_ref, fh, wh, wl, yh, yl)
    block_tiles(yh, part_ref)

    half = part_ref.shape[0] // 2
    quarter = half // 4
    rows = lambda base, n: pl.ds(pl.multiple_of(base, 32), n)
    columns = design_ref.shape[2]
    width = qh.shape[2]
    share = gram.shape[2]
    swap = remote(part_ref.at[rows((1 - core) * half, half)], mate, ps, pr, other)
    swap.start()

    def product(block):
        flip = ((0,), (0,))
        total = jnp.zeros((BLK, width), F32)
        for arc in range(arcs):
            piece = design_ref[arc, :, block * BLK : block * BLK + BLK]
            on = on_ref[block * arcs + arc].astype(F32)
            one = dot_by(piece, qh[arc], flip) + dot_by(piece, ql[arc], flip)
            total = total + one * on
        low = block * BLK
        while low < block * BLK + BLK:
            at = low // share
            stop = min((at + 1) * share, block * BLK + BLK)
            gram[at // 2, at % 2, low - at * share : stop - at * share, :] = total[
                low - block * BLK : stop - block * BLK
            ]
            low = stop

    for b in reversed(range(1, blocks)):
        solve_back(b, fh, wh, wl, yh, yl, qh, ql)
        if b == blocks - 1:
            swap.wait_recv()
            kept[...] = part_ref[rows(core * half, half), :] + mate[...]
            scatter = begin([
                remote(kept.at[rows(c * quarter, quarter)], got.at[k], rs.at[k], rr.at[k], peer)
                for k, (c, peer) in enumerate(zip(chips, peers))
            ])
    solve_back(0, fh, wh, wl, yh, yl, qh, ql)
    load.wait()
    product(0)
    product(1)
    arrive(scatter)
    mine = rows(core * half + chip * quarter, quarter)
    out_ref[mine, :] = (kept[rows(chip * quarter, quarter), :] + got[0]) + (got[1] + got[2])
    gather = begin([
        remote(out_ref.at[mine], out_ref.at[mine], gs.at[k], gr.at[k], peer)
        for k, peer in enumerate(peers)
    ])
    forward = begin([remote(out_ref.at[mine], out_ref.at[mine], fs.at[0], fr.at[0], other)])
    for block in range(2, columns // BLK):
        product(block)
    trade = remote(gram.at[:, 1 - core], pair, qs, qr, other)
    trade.start()
    for k in range(3):
        gather[k].wait_recv()
        from_chip = rows(core * half + lax.rem(chip + 3 - k, 4) * quarter, quarter)
        forward += begin([
            remote(out_ref.at[from_chip], out_ref.at[from_chip], fs.at[k + 1], fr.at[k + 1], other)
        ])
    trade.wait_recv()
    for c in range(4):
        sum_ref[c] = (gram[c, core] + pair[c]).astype(BF)
    own_ref[...] = gram[chip, core] + pair[chip]
    arrive(forward)
    pl.loop(0, held)(lambda c: piece(c).wait_send())
    piece(8).wait_send()
    for copy in sent + [swap, trade]:
        copy.wait_send()


def block_and_gram(on, cov, window, design):
    arcs, lines, size = cov.shape
    _, observed, width = window.shape
    chips = 4
    share = design.shape[2] // (2 * chips)
    total = len(tile_list(width)) * 128
    vm, dma = pltpu.VMEM, pltpu.SemaphoreType.DMA
    return pl.pallas_call(
        main_kernel,
        out_shape=(
            jax.ShapeDtypeStruct((total, 128), F32),
            jax.ShapeDtypeStruct((chips, share, width), BF),
            jax.ShapeDtypeStruct((share, width), F32),
        ),
        in_specs=[pl.BlockSpec(memory_space=pltpu.SMEM)]
        + [pl.BlockSpec(memory_space=vm)] * 2
        + [pl.BlockSpec(memory_space=pl.ANY)],
        out_specs=(pl.BlockSpec(memory_space=vm),) * 3,
        scratch_shapes=[
            vm((arcs, 16, 11, lines, 128), BF),
            vm((arcs, size, width), BF),
            vm((2, 9, arcs, lines, 128), BF),
            vm((arcs, 3, 256, width), BF),
            vm((arcs, 3, 64, width), BF),
            vm((arcs, 64, width), BF),
            vm((arcs, 256, width), BF),
            vm((arcs, 64, width), BF),
            vm((arcs, size, 128), F32),
            vm((arcs, size, size), BF),
            vm((arcs, size, OBS_STEP), BF),
            vm((arcs, size, OBS_STEP), BF),
            vm((arcs, size, width), BF),
            vm((arcs, size, width), BF),
            vm((arcs, size, width), BF),
            vm((arcs, size, width), BF),
            vm(design.shape, BF),
            vm((total, 128), F32),
            vm((chips, 2, share, width), F32),
            vm((total // 2, 128), F32),
            vm((total // 2, 128), F32),
            vm((3, total // 8, 128), F32),
            vm((chips, share, width), F32),
            dma((9,)), dma((9,)),
            dma((PARTS, arcs, 3)), dma((PARTS, arcs, 3)), dma((PARTS, arcs, 3)), dma((PARTS, arcs, 3)),
            dma((PARTS, arcs)), dma((PARTS, arcs)),
            dma((2, arcs, 4)), dma((2, arcs, 4)), dma((PARTS, 2, arcs, 4)), dma((PARTS, 2, arcs, 4)),
            dma, dma, dma, dma, dma, dma((3,)), dma((3,)), dma((3,)), dma((3,)), dma((4,)), dma((4,)),
        ],
        compiler_params=pltpu.CompilerParams(
            vmem_limit_bytes=KERNEL_VMEM, collective_id=0, has_side_effects=True
        ),
    )(on, cov, window, design)


PANEL = 512
BLK = 256
PAR = ("par_0", "par_1", "par_2")


def on_device(design, cov_factor, active_blocks, panel_index, reg_diag):
    arcs, observed, columns = design.shape
    local_blocks = columns // BLK
    par_id = lax.axis_index(PAR)
    chip, core = lax.axis_index("line"), lax.axis_index("core")
    start = panel_index[0] * PANEL
    block_ids = par_id * local_blocks + jnp.arange(local_blocks, dtype=jnp.int32)
    hits = jnp.any(active_blocks[:, :, None] == block_ids[None, None, :], axis=1)
    parts = jnp.arange(PANEL // BLK, dtype=jnp.int32)
    wanted = panel_index[0] * (PANEL // BLK) + parts
    local = wanted - par_id * local_blocks
    inside = (local >= 0) & (local < local_blocks)
    active = jnp.any(active_blocks[None] == wanted[:, None, None], axis=2)
    window = window_of(
        jnp.clip(local, 0, local_blocks - 1),
        (inside[:, None] & active).astype(jnp.int32).reshape(-1),
        design,
    )
    share = columns // (4 * 2)
    on = hits.T.astype(jnp.int32).reshape(-1)
    block, sums, own = block_and_gram(on, cov_factor, window, design)
    arrived = lax.all_to_all(sums, "line", split_axis=0, concat_axis=0, tiled=True)
    reg = reg_diag.reshape(-1, 1, PANEL)
    shift = par_id * columns + (chip * 2 + core) * share - start
    at = jnp.stack([panel_index[0], shift, chip]).astype(jnp.int32)
    inverse = factor_inverse(at, block, reg)
    return apply_inverse(at, arrived, own, inverse, reg).T


def solution(mesh):
    split = Mesh(
        mesh.devices.reshape(mesh.shape["arc"] // 2, 2, 2, 4, 4), ("line", "core") + PAR
    )
    arc = ("line", "core")
    return jax.shard_map(
        on_device,
        mesh=split,
        in_specs=(P(arc, None, PAR), P(arc, PAR, None), P(arc, None), P(), P()),
        out_specs=P(None, PAR + arc),
        check_vma=False,
    )
```

```python
import functools
import jax
import jax.numpy as jnp
from jax import lax
from jax.experimental import pallas as pl
from jax.experimental.pallas import tpu as pltpu
from jax.sharding import Mesh
from jax.sharding import PartitionSpec as P

OBS_STEP = 256
GROUP = 8
PARTS = 2
PART = 512 // PARTS
ORDER = "lablablablabablabl0ab1ab2"
BF = jnp.bfloat16
F32 = jnp.float32
KERNEL_VMEM = 56 * 1024 * 1024


def halves(value):
    high = value.astype(BF)
    return high, (value - high.astype(F32)).astype(BF)


def dot_by(a, b, dims):
    return lax.dot_general(a, b, (dims, ((), ())), preferred_element_type=F32)


def dot3(a, b, dims=((1,), (0,))):
    (ah, al), (bh, bl) = a, b
    return dot_by(ah, bh, dims) + (dot_by(ah, bl, dims) + dot_by(al, bh, dims))


def lanes(shape):
    return lax.broadcasted_iota(jnp.int32, shape, 1)


def rows_of(shape):
    return lax.broadcasted_iota(jnp.int32, shape, 0)


def invert_tiles(tiles):
    lane = lanes((8, 128))
    row = rows_of((8, 128))
    base = lane - lax.rem(lane, 32)
    packed, inverse, scales = [], [], []
    for tile in tiles:
        pack, inv, scale = [], [], jnp.zeros((8, 128), F32)
        for g in range(4):
            piece = tile[96 + 8 * g : 104 + 8 * g]
            for part in (2, 1, 0):
                low = 32 * part + 8 * g
                piece = jnp.where(base == 32 * part, tile[low : low + 8], piece)
            pivot = 1.0 / jnp.take_along_axis(piece, base + row + 8 * g, axis=1)
            on = lane - base == row + 8 * g
            scale = scale + jnp.where(on, pivot, 0.0)
            pack.append(piece * pivot)
            inv.append(jnp.where(on, 1.0, 0.0).astype(F32))
        packed.append(pack)
        inverse.append(inv)
        scales.append(jnp.sum(scale, axis=0, keepdims=True))
    for j in range(31):
        at, sub = j // 8, j % 8
        index = base + j
        for pack, inv in zip(packed, inverse):
            top = jnp.broadcast_to(inv[at][sub : sub + 1], (8, 128))
            for g in range(at, 4):
                coef = jnp.take_along_axis(pack[g], index, axis=1)
                if g == at:
                    coef = jnp.where(row > sub, coef, 0.0)
                inv[g] = inv[g] - coef * top
    wide = lanes((32, 128)) // 32
    zero = jnp.zeros((32, 128), F32)
    results = []
    for tile, inv, scale in zip(tiles, inverse, scales):
        value = jnp.concatenate(inv, axis=0) * scale
        parts = [jnp.where(wide == g, value, 0.0) for g in range(4)]
        cross = [jnp.where(wide == g - 1, tile[32 * g : 32 * g + 32], 0.0) for g in (1, 3)]
        left = dot3(halves(jnp.concatenate(cross, axis=0)), halves(jnp.concatenate(parts, axis=0)))
        left = jnp.concatenate([zero, left[:32], zero, left[32:]], axis=0)
        odd = jnp.concatenate([parts[1], parts[3]], axis=0)
        odd = odd - dot3(halves(odd), halves(left))
        first = jnp.concatenate([parts[0], odd[:32]], axis=0)
        second = jnp.concatenate([parts[2], odd[32:]], axis=0)
        half = jnp.concatenate([first, second], axis=0)
        cross = jnp.where(lanes((64, 128)) < 64, tile[64:], 0.0)
        left = dot3(halves(cross), halves(half))
        left = jnp.concatenate([jnp.zeros_like(left), left], axis=0)
        results.append(jnp.concatenate([first, second - dot3(halves(second), halves(left))], axis=0))
    return results


def dot2(a, b, dims=((1,), (0,))):
    bh, bl = b
    return dot_by(a, bh, dims) + dot_by(a, bl, dims)


def spot_of(arc, slab):
    big = slab // 16
    pair = slab + big * (31 - 2 * slab)
    far = pair // 4
    near = pair - 4 * far
    place = (1 - arc) * (4 * far + near) + arc * (4 * near + far)
    return place, big, big * far


def tile_of(ref, arc, row, column):
    pieces = []
    for i in range(4):
        place, _, shift = spot_of(arc, 4 * row + i)
        pieces.append(ref[arc, place, shift + column])
    return jnp.concatenate(pieces, axis=0)


def diagonal_of(ref, arc, row):
    pieces = []
    for i in range(4):
        place, big, _ = spot_of(arc, 4 * row + i)
        pieces.append(
            ref[arc, place, 7 + 2 * big].astype(F32) + ref[arc, place, 8 + 2 * big].astype(F32)
        )
    return jnp.concatenate(pieces, axis=0)


def invert_all(step, factor_ref, inv):
    tiles = inv.shape[1] // 128
    found = []
    for part in range(GROUP):
        at = step * GROUP + part
        arc, tile = at // tiles, lax.rem(at, tiles)
        spot = pl.ds(pl.multiple_of(tile * 128, 128), 128)
        found.append((arc, spot, tile))
    done = invert_tiles([diagonal_of(factor_ref, arc, tile) for arc, spot, tile in found])
    for (arc, spot, _), value in zip(found, done):
        inv[arc, spot, :] = value


def join_tiles(arc, factor_ref, inv, fh, wh, wl):
    for b in range(inv.shape[1] // OBS_STEP):
        r = b * OBS_STEP
        one, two = inv[arc, r : r + 128, :], inv[arc, r + 128 : r + 256, :]
        cross = tile_of(factor_ref, arc, 2 * b + 1, 2 * b)
        corner = -dot3(halves(two), halves(dot2(cross, halves(one))))
        zero = jnp.zeros((128, 128), BF)
        for ref, a, c, d in zip((wh, wl), halves(one), halves(corner), halves(two)):
            ref[arc, r : r + 128, 0:128] = a
            ref[arc, r : r + 128, 128:256] = zero
            ref[arc, r + 128 : r + 256, 0:128] = c
            ref[arc, r + 128 : r + 256, 128:256] = d
        for row in (2 * b, 2 * b + 1):
            for column in range(2 * b):
                fh[arc, row * 128 : row * 128 + 128, column * 128 : column * 128 + 128] = tile_of(
                    factor_ref, arc, row, column
                )


def solve_forward(b, rhs_ref, fh, wh, wl, yh, yl):
    r = b * OBS_STEP
    here = slice(r, r + OBS_STEP)
    for arc in range(rhs_ref.shape[0]):
        value = rhs_ref[arc, here, :].astype(F32)
        if b:
            value = value - dot2(fh[arc, here, 0:r], (yh[arc, 0:r, :], yl[arc, 0:r, :]))
        value = dot3((wh[arc, here, :], wl[arc, here, :]), halves(value))
        yh[arc, here, :], yl[arc, here, :] = halves(value)


def solve_back(b, fh, wh, wl, yh, yl, qh, ql):
    flip = ((0,), (0,))
    size = yh.shape[1]
    r = b * OBS_STEP
    here, after = slice(r, r + OBS_STEP), slice(r + OBS_STEP, size)
    for arc in range(yh.shape[0]):
        value = yh[arc, here, :].astype(F32) + yl[arc, here, :].astype(F32)
        if r + OBS_STEP < size:
            value = value - dot2(fh[arc, after, here], (qh[arc, after, :], ql[arc, after, :]), flip)
        value = dot3((wh[arc, here, :], wl[arc, here, :]), halves(value), flip)
        qh[arc, here, :], ql[arc, here, :] = halves(value)


def block_tiles(yh, block_ref):
    at = 0
    for i in range(0, yh.shape[2], 128):
        strip = sum(
            dot_by(yh[arc, :, i : i + 128], yh[arc, :, i:], ((0,), (0,))) for arc in range(yh.shape[0])
        )
        for j in range(0, strip.shape[1], 128):
            block_ref[at : at + 128, :] = strip[:, j : j + 128]
            at += 128


def split_rows(u):
    high, less = halves(u)
    return jnp.concatenate([high, high, less], axis=0), jnp.concatenate([high, less, high], axis=0)


def eliminate(panel, first):
    row = rows_of((8, 128))
    scale = [jnp.zeros((8, 128), F32) for _ in range(4)]
    for group in range(4):
        cols = []
        for t in range(8):
            lane = first + group * 8 + t
            cols.append(
                [
                    jnp.broadcast_to(panel[g][0][:, lane : lane + 1], (8, 128)) if g >= group else None
                    for g in range(4)
                ]
            )
        for t in range(8):
            pivot = lax.rsqrt(jnp.broadcast_to(cols[t][group][t : t + 1], (8, 128)))
            scale[group] = jnp.where(row == t, pivot, scale[group])
            inv = pivot * pivot
            mult = [None if g < group else cols[t][g] * inv for g in range(4)]
            mult[group] = jnp.where(row > t, mult[group], 0.0)
            for t2 in range(t + 1, 8):
                top = jnp.broadcast_to(cols[t2][group][t : t + 1], (8, 128))
                for g in range(group, 4):
                    cols[t2][g] = cols[t2][g] - mult[g] * top
            for c in range(len(panel[0])):
                top = jnp.broadcast_to(panel[group][c][t : t + 1], (8, 128))
                for g in range(group, 4):
                    panel[g][c] = panel[g][c] - mult[g] * top
    return jnp.concatenate(
        [jnp.concatenate([piece * scale[g] for piece in panel[g]], axis=1) for g in range(4)], axis=0
    )


def factor_and_invert(work):
    size = work.shape[0]
    width = size + 128
    flip = ((0,), (0,))
    at = lambda base, n: pl.ds(pl.multiple_of(base, 128), n)

    @pl.loop(0, size // 128)
    def _(k):
        c0 = k * 128
        wide = at(c0, width)
        for q in range(4):
            top = lambda g, n: pl.ds(pl.multiple_of(c0 + q * 32 + 8 * g, 8), n)
            panel = [
                [work[top(g, 8), at(c0 + c, 128)] for c in range(0, width, 128)] for g in range(4)
            ]
            done = eliminate(panel, q * 32)
            work[top(0, 32), wide] = done
            if q < 3:
                a, b = split_rows(done)
                less = dot_by(a[:, 0:128], b, flip)
                work[top(4, 96 - q * 32), wide] -= less[q * 32 + 32 : 128]

        @pl.when(k < size // 128 - 1)
        def _():
            _, b = split_rows(work[at(c0, 128), wide])

            @pl.loop(k + 1, size // 128)
            def _(i):
                a, _ = split_rows(work[at(c0, 128), at(i * 128, 128)])
                work[at(i * 128, 128), wide] -= dot_by(a, b, flip)


def tile_list(size):
    return [(i, j) for i in range(size // 128) for j in range(i, size // 128)]


def window_kernel(at_ref, on_ref, design_ref, out_ref):
    part = pl.program_id(0)
    for arc in range(out_ref.shape[0]):
        on = on_ref[part * out_ref.shape[0] + arc] > 0
        out_ref[arc] = jnp.where(on, design_ref[arc], jnp.zeros((), BF))


def window_of(at, on, design):
    arcs, observed, _ = design.shape
    parts = at.shape[0]
    block = (arcs, observed, BLK)
    return pl.pallas_call(
        window_kernel,
        out_shape=jax.ShapeDtypeStruct((arcs, observed, parts * BLK), BF),
        grid_spec=pltpu.PrefetchScalarGridSpec(
            num_scalar_prefetch=2,
            grid=(parts,),
            in_specs=[pl.BlockSpec(block, lambda i, at, on: (0, 0, at[i]))],
            out_specs=pl.BlockSpec(block, lambda i, at, on: (0, 0, i)),
        ),
        compiler_params=pltpu.CompilerParams(vmem_limit_bytes=KERNEL_VMEM),
    )(at, on, design)


MESH = pl.DeviceIdType.MESH


def remote(src, dst, send, recv, device):
    return pltpu.make_async_remote_copy(
        src_ref=src, dst_ref=dst, send_sem=send, recv_sem=recv, device_id=device, device_id_type=MESH
    )


def meet(devices):
    barrier = pltpu.get_barrier_semaphore()
    for device in devices:
        pl.semaphore_signal(barrier, inc=1, device_id=device, device_id_type=MESH)
    pl.semaphore_wait(barrier, len(devices))


def ring_pair(slot, me, axis, send, recv):
    mine = slot(me)
    return [
        remote(mine, mine, send.at[d], recv.at[d], {axis: lax.rem(me + step, 4)})
        for d, step in enumerate((1, 3))
    ]


def ring_far(first, second, me, axis, send, recv):
    left, right = lax.rem(me + 3, 4), lax.rem(me + 1, 4)
    one, two = first(left), second(right)
    return [
        remote(one, one, send.at[2], recv.at[2], {axis: right}),
        remote(two, two, send.at[3], recv.at[3], {axis: left}),
    ]


def main_kernel(
    at_ref, on_ref, cov_ref, win_ref, reg_ref, design_hbm, final_ref,
    fac_ref, rhs_ref, slabs, got1, got2, gotz, sum1, sum2, inv, fh, wh, wl, yh, yl, qh, ql, design_ref,
    part_ref, gram, kept, mate, got, pair, out_ref, sum_ref, own_ref, arrived, work,
    ls, lr, m1s, m1r, m2s, m2r, mzs, mzr, gls, glr, gms, gmr,
    ds, ps, pr, qs, qr, rs, rr, gs, gr, fs, fr, es, er,
):
    z, x, y = (lax.axis_index(name) for name in ("par_0", "par_1", "par_2"))
    chip, core = lax.axis_index("line"), lax.axis_index("core")
    other = {"core": 1 - core}
    chips = [lax.rem(chip + k, 4) for k in (1, 2, 3)]
    peers = [{"line": c} for c in chips]
    load = pltpu.make_async_copy(design_hbm, design_ref, ds)
    load.start()
    arcs = cov_ref.shape[0]
    turned = lambda v: v + z * (3 - 2 * v)
    outer = [(x, "par_1"), (y, "par_2")]
    inner = [(y, "par_2"), (x, "par_1")]
    partner = {"par_0": 1 - z, "par_1": 3 - x, "par_2": 3 - y}
    ring = [{"par_1": lax.rem(x + k, 4)} for k in (1, 2, 3)] + [
        {"par_2": lax.rem(y + k, 4)} for k in (1, 2, 3)
    ]
    meet(ring + [{"par_0": 1 - z}, partner] + peers + [other])

    small = turned(x) + 1
    held = small + z * (9 - 2 * small)
    two = range(arcs)
    sent = []

    def piece(c):
        return remote(slabs.at[z, c], slabs.at[z, c], ls.at[c], lr.at[c], partner)

    def came(c):
        return remote(slabs.at[1 - z, c], slabs.at[1 - z, c], ls.at[c], lr.at[c], partner)

    def begin(copies):
        for copy in copies:
            copy.start()
        sent.extend(copies)
        return copies

    def arrive(copies):
        for copy in copies:
            copy.wait_recv()

    def near(slot, ax, s, r):
        return begin(
            [copy for arc in two for copy in ring_pair(slot(arc), *ax[arc], s.at[arc], r.at[arc])]
        )

    def far(first, second, ax, s, r):
        return begin(
            [
                copy for arc in two
                for copy in ring_far(first(arc), second(arc), *ax[arc], s.at[arc], r.at[arc])
            ]
        )

    def l_unit(low, size):
        return lambda arc: lambda r: fac_ref.at[
            arc, 4 * turned(outer[arc][0]) + turned(r), pl.ds(low, size)
        ]

    def l_group(low, size):
        return lambda arc: lambda r: fac_ref.at[arc, pl.ds(4 * turned(r) + low, size)]

    def factor_stream():
        last = cov_ref[:, :, pl.ds(pl.multiple_of((held - 1) * 128, 128), 128)]
        slabs[z, 8] = (last - last.astype(BF).astype(F32)).astype(BF)
        for c in range(8):
            slabs[z, c] = cov_ref[:, :, c * 128 : c * 128 + 128].astype(BF)
        pl.loop(0, held)(lambda c: piece(c).start())
        piece(8).start()
        yield
        pl.loop(0, 9 - held)(lambda c: came(c).wait_recv())
        came(8).wait_recv()
        for arc in two:
            place = 4 * turned(outer[arc][0]) + turned(inner[arc][0])

            @pl.loop(0, small - 1)
            def _(c):
                fac_ref[arc, place, c] = slabs[0, c, arc]

            @pl.loop(0, 8 - small)
            def _(c):
                fac_ref[arc, place, small - 1 + c] = slabs[1, c, arc]

            fac_ref[arc, place, 7] = slabs[0, small - 1, arc]
            fac_ref[arc, place, 8] = slabs[0, 8, arc]
            fac_ref[arc, place, 9] = slabs[1, 8 - small, arc]
            fac_ref[arc, place, 10] = slabs[1, 8, arc]
        s, r = gls.at[0], glr.at[0]
        l1 = near(l_unit(0, 11), inner, s, r)
        yield
        arrive(l1)
        l2 = far(l_unit(0, 6), l_unit(6, 5), inner, s, r)
        yield
        arrive(l2)
        s, r = gls.at[1], glr.at[1]
        l3 = near(l_group(0, 4), outer, s, r)
        yield
        arrive(l3)
        l4 = far(l_group(0, 2), l_group(2, 2), outer, s, r)
        yield
        arrive(l4)
        yield

    def panel_stream(part):
        cols = pl.ds(part * PART, PART)
        lines = lambda base, n: pl.ds(pl.multiple_of(base, 32), n)

        def m_unit(low, size):
            return lambda arc: lambda r: rhs_ref.at[
                arc, lines(outer[arc][0] * 256 + r * 64 + low, size), cols
            ]

        def m_group(low, size):
            return lambda arc: lambda r: rhs_ref.at[arc, lines(r * 256 + low, size), cols]

        def to_peers(source, target, ax, unit, s, r):
            copies = []
            for k in (1, 3, 2):
                for arc in two:
                    to = lax.rem(ax[arc][0] + k, 4)
                    copies.append(
                        remote(
                            source.at[arc, lines(to * unit, unit), cols],
                            target.at[arc, k - 1, :, cols],
                            s.at[part, arc, k - 1], r.at[part, arc, k - 1], {ax[arc][1]: to},
                        )
                    )
            return begin(copies)

        scatter1 = to_peers(win_ref, got1, outer, 256, m1s, m1r)
        yield
        arrive(scatter1)
        for arc in two:
            own = win_ref[arc, lines(outer[arc][0] * 256, 256), cols]
            sum1[arc, :, cols] = (own + got1[arc, 0, :, cols]) + (
                got1[arc, 1, :, cols] + got1[arc, 2, :, cols]
            )
        scatter2 = to_peers(sum1, got2, inner, 64, m2s, m2r)
        yield
        arrive(scatter2)
        for arc in two:
            own = sum1[arc, lines(inner[arc][0] * 64, 64), cols]
            sum2[arc, :, cols] = (own + got2[arc, 0, :, cols]) + (
                got2[arc, 1, :, cols] + got2[arc, 2, :, cols]
            )
        across = begin(
            [
                remote(
                    sum2.at[arc, :, cols], gotz.at[arc, :, cols],
                    mzs.at[part, arc], mzr.at[part, arc], {"par_0": 1 - z},
                )
                for arc in two
            ]
        )
        yield
        arrive(across)
        for arc in two:
            spot = lines(outer[arc][0] * 256 + inner[arc][0] * 64, 64)
            rhs_ref[arc, spot, cols] = sum2[arc, :, cols] + gotz[arc, :, cols]
        s, r = gms.at[part, 0], gmr.at[part, 0]
        g1 = near(m_unit(0, 64), inner, s, r)
        yield
        arrive(g1)
        g2 = far(m_unit(0, 32), m_unit(32, 32), inner, s, r)
        yield
        arrive(g2)
        s, r = gms.at[part, 1], gmr.at[part, 1]
        g3 = near(m_group(0, 256), outer, s, r)
        yield
        arrive(g3)
        g4 = far(m_group(0, 128), m_group(128, 128), outer, s, r)
        yield
        arrive(g4)
        yield

    def prepare(step):
        if step < 2:
            invert_all(step, fac_ref, inv)
        else:
            for arc in two:
                join_tiles(arc, fac_ref, inv, fh, wh, wl)

    streams = {"l": factor_stream(), "a": panel_stream(0)}
    if PARTS > 1:
        streams["b"] = panel_stream(1)
    for step in ORDER:
        if step.isdigit():
            prepare(int(step))
        else:
            next(streams[step])
    blocks = rhs_ref.shape[1] // OBS_STEP
    for b in range(blocks):
        solve_forward(b, rhs_ref, fh, wh, wl, yh, yl)
    block_tiles(yh, part_ref)

    half = part_ref.shape[0] // 2
    quarter = half // 4
    rows = lambda base, n: pl.ds(pl.multiple_of(base, 32), n)
    columns = design_ref.shape[2]
    width = qh.shape[2]
    share = gram.shape[2]
    swap = remote(part_ref.at[rows((1 - core) * half, half)], mate, ps, pr, other)
    swap.start()

    def product(block):
        flip = ((0,), (0,))
        total = jnp.zeros((BLK, width), F32)
        for arc in range(arcs):
            piece = design_ref[arc, :, block * BLK : block * BLK + BLK]
            on = on_ref[block * arcs + arc].astype(F32)
            one = dot_by(piece, qh[arc], flip) + dot_by(piece, ql[arc], flip)
            total = total + one * on
        low = block * BLK
        while low < block * BLK + BLK:
            at = low // share
            stop = min((at + 1) * share, block * BLK + BLK)
            gram[at // 2, at % 2, low - at * share : stop - at * share, :] = total[
                low - block * BLK : stop - block * BLK
            ]
            low = stop

    for b in reversed(range(1, blocks)):
        solve_back(b, fh, wh, wl, yh, yl, qh, ql)
        if b == blocks - 1:
            swap.wait_recv()
            kept[...] = part_ref[rows(core * half, half), :] + mate[...]
            scatter = begin([
                remote(kept.at[rows(c * quarter, quarter)], got.at[k], rs.at[k], rr.at[k], peer)
                for k, (c, peer) in enumerate(zip(chips, peers))
            ])
    solve_back(0, fh, wh, wl, yh, yl, qh, ql)
    load.wait()
    product(0)
    product(1)
    arrive(scatter)
    mine = rows(core * half + chip * quarter, quarter)
    out_ref[mine, :] = (kept[rows(chip * quarter, quarter), :] + got[0]) + (got[1] + got[2])
    gather = begin([
        remote(out_ref.at[mine], out_ref.at[mine], gs.at[k], gr.at[k], peer)
        for k, peer in enumerate(peers)
    ])
    forward = begin([remote(out_ref.at[mine], out_ref.at[mine], fs.at[0], fr.at[0], other)])
    for block in range(2, columns // BLK):
        product(block)
    trade = remote(gram.at[:, 1 - core], pair, qs, qr, other)
    trade.start()
    for k in range(3):
        gather[k].wait_recv()
        from_chip = rows(core * half + lax.rem(chip + 3 - k, 4) * quarter, quarter)
        forward += begin([
            remote(out_ref.at[from_chip], out_ref.at[from_chip], fs.at[k + 1], fr.at[k + 1], other)
        ])
    trade.wait_recv()
    for c in range(4):
        sum_ref[c] = (gram[c, core] + pair[c]).astype(BF)
    exchange = begin([
        remote(sum_ref.at[c], arrived.at[k], es.at[k], er.at[k], peer)
        for k, (c, peer) in enumerate(zip(chips, peers))
    ])
    own_ref[...] = gram[chip, core] + pair[chip]
    reg = reg_ref[at_ref[0]]
    square = (128, 128)
    eye = lanes(square) == rows_of(square)
    work[...] = jnp.zeros_like(work)
    arrive(forward)
    for at, (i, j) in enumerate(tile_list(width)):
        value = out_ref[at * 128 : at * 128 + 128, :]
        if i == j:
            value = value + jnp.where(eye, reg[:, i * 128 : i * 128 + 128], 0.0)
            work[i * 128 : i * 128 + 128, width + i * 128 : width + i * 128 + 128] = jnp.where(
                eye, 1.0, 0.0
            )
        work[i * 128 : i * 128 + 128, j * 128 : j * 128 + 128] = value
    factor_and_invert(work)
    arrive(exchange)
    total = own_ref[...]
    for k in range(3):
        total = total + arrived[k].astype(F32)
    first = ((z * 4 + x) * 4 + y) * columns + (chip * 2 + core) * share - at_ref[0] * width
    total = total + jnp.where(rows_of(total.shape) + first == lanes(total.shape), reg, 0.0)
    final_ref[...] = dot3(halves(total), halves(work[:, width:]), ((1,), (1,)))
    pl.loop(0, held)(lambda c: piece(c).wait_send())
    piece(8).wait_send()
    for copy in sent + [swap, trade]:
        copy.wait_send()


def solve_panel(at, on, cov, window, reg, design):
    arcs, lines, size = cov.shape
    _, observed, width = window.shape
    chips = 4
    share = design.shape[2] // (2 * chips)
    total = len(tile_list(width)) * 128
    vm, dma = pltpu.VMEM, pltpu.SemaphoreType.DMA
    return pl.pallas_call(
        main_kernel,
        out_shape=jax.ShapeDtypeStruct((share, width), F32),
        in_specs=[pl.BlockSpec(memory_space=pltpu.SMEM)] * 2
        + [pl.BlockSpec(memory_space=vm)] * 3
        + [pl.BlockSpec(memory_space=pl.ANY)],
        out_specs=pl.BlockSpec(memory_space=vm),
        scratch_shapes=[
            vm((arcs, 16, 11, lines, 128), BF),
            vm((arcs, size, width), BF),
            vm((2, 9, arcs, lines, 128), BF),
            vm((arcs, 3, 256, width), BF),
            vm((arcs, 3, 64, width), BF),
            vm((arcs, 64, width), BF),
            vm((arcs, 256, width), BF),
            vm((arcs, 64, width), BF),
            vm((arcs, size, 128), F32),
            vm((arcs, size, size), BF),
            vm((arcs, size, OBS_STEP), BF),
            vm((arcs, size, OBS_STEP), BF),
            vm((arcs, size, width), BF),
            vm((arcs, size, width), BF),
            vm((arcs, size, width), BF),
            vm((arcs, size, width), BF),
            vm(design.shape, BF),
            vm((total, 128), F32),
            vm((chips, 2, share, width), F32),
            vm((total // 2, 128), F32),
            vm((total // 2, 128), F32),
            vm((3, total // 8, 128), F32),
            vm((chips, share, width), F32),
            vm((total, 128), F32),
            vm((chips, share, width), BF),
            vm((share, width), F32),
            vm((chips - 1, share, width), BF),
            vm((width, 2 * width), F32),
            dma((9,)), dma((9,)),
            dma((PARTS, arcs, 3)), dma((PARTS, arcs, 3)), dma((PARTS, arcs, 3)), dma((PARTS, arcs, 3)),
            dma((PARTS, arcs)), dma((PARTS, arcs)),
            dma((2, arcs, 4)), dma((2, arcs, 4)), dma((PARTS, 2, arcs, 4)), dma((PARTS, 2, arcs, 4)),
            dma, dma, dma, dma, dma, dma((3,)), dma((3,)), dma((3,)), dma((3,)), dma((4,)), dma((4,)),
            dma((3,)), dma((3,)),
        ],
        compiler_params=pltpu.CompilerParams(
            vmem_limit_bytes=KERNEL_VMEM, collective_id=0, has_side_effects=True
        ),
    )(at, on, cov, window, reg, design)


PANEL = 512
BLK = 256
PAR = ("par_0", "par_1", "par_2")


def on_device(design, cov_factor, active_blocks, panel_index, reg_diag):
    arcs, observed, columns = design.shape
    local_blocks = columns // BLK
    par_id = lax.axis_index(PAR)
    block_ids = par_id * local_blocks + jnp.arange(local_blocks, dtype=jnp.int32)
    hits = jnp.any(active_blocks[:, :, None] == block_ids[None, None, :], axis=1)
    parts = jnp.arange(PANEL // BLK, dtype=jnp.int32)
    wanted = panel_index[0] * (PANEL // BLK) + parts
    local = wanted - par_id * local_blocks
    inside = (local >= 0) & (local < local_blocks)
    active = jnp.any(active_blocks[None] == wanted[:, None, None], axis=2)
    window = window_of(
        jnp.clip(local, 0, local_blocks - 1),
        (inside[:, None] & active).astype(jnp.int32).reshape(-1),
        design,
    )
    on = hits.T.astype(jnp.int32).reshape(-1)
    reg = reg_diag.reshape(-1, 1, PANEL)
    return solve_panel(panel_index, on, cov_factor, window, reg, design).T


def solution(mesh):
    split = Mesh(
        mesh.devices.reshape(mesh.shape["arc"] // 2, 2, 2, 4, 4), ("line", "core") + PAR
    )
    arc = ("line", "core")
    return jax.shard_map(
        on_device,
        mesh=split,
        in_specs=(P(arc, None, PAR), P(arc, PAR, None), P(arc, None), P(), P()),
        out_specs=P(None, PAR + arc),
        check_vma=False,
    )
```

```python
import functools
import jax
import jax.numpy as jnp
from jax import lax
from jax.experimental import pallas as pl
from jax.experimental.pallas import tpu as pltpu
from jax.sharding import Mesh
from jax.sharding import PartitionSpec as P

OBS_STEP = 256
GROUP = 8
PARTS = 2
PART = 512 // PARTS
ORDER = "lablablablabablabl0ab1ab2"
BF = jnp.bfloat16
F32 = jnp.float32
KERNEL_VMEM = 56 * 1024 * 1024


def halves(value):
    high = value.astype(BF)
    return high, (value - high.astype(F32)).astype(BF)


def dot_by(a, b, dims):
    return lax.dot_general(a, b, (dims, ((), ())), preferred_element_type=F32)


def dot3(a, b, dims=((1,), (0,))):
    (ah, al), (bh, bl) = a, b
    return dot_by(ah, bh, dims) + (dot_by(ah, bl, dims) + dot_by(al, bh, dims))


def lanes(shape):
    return lax.broadcasted_iota(jnp.int32, shape, 1)


def rows_of(shape):
    return lax.broadcasted_iota(jnp.int32, shape, 0)


def invert_tiles(tiles):
    lane = lanes((8, 128))
    row = rows_of((8, 128))
    base = lane - lax.rem(lane, 32)
    packed, inverse, scales = [], [], []
    for tile in tiles:
        pack, inv, scale = [], [], jnp.zeros((8, 128), F32)
        for g in range(4):
            piece = tile[96 + 8 * g : 104 + 8 * g]
            for part in (2, 1, 0):
                low = 32 * part + 8 * g
                piece = jnp.where(base == 32 * part, tile[low : low + 8], piece)
            pivot = 1.0 / jnp.take_along_axis(piece, base + row + 8 * g, axis=1)
            on = lane - base == row + 8 * g
            scale = scale + jnp.where(on, pivot, 0.0)
            pack.append(piece * pivot)
            inv.append(jnp.where(on, 1.0, 0.0).astype(F32))
        packed.append(pack)
        inverse.append(inv)
        scales.append(jnp.sum(scale, axis=0, keepdims=True))
    for j in range(31):
        at, sub = j // 8, j % 8
        index = base + j
        for pack, inv in zip(packed, inverse):
            top = jnp.broadcast_to(inv[at][sub : sub + 1], (8, 128))
            for g in range(at, 4):
                coef = jnp.take_along_axis(pack[g], index, axis=1)
                if g == at:
                    coef = jnp.where(row > sub, coef, 0.0)
                inv[g] = inv[g] - coef * top
    wide = lanes((32, 128)) // 32
    zero = jnp.zeros((32, 128), F32)
    results = []
    for tile, inv, scale in zip(tiles, inverse, scales):
        value = jnp.concatenate(inv, axis=0) * scale
        parts = [jnp.where(wide == g, value, 0.0) for g in range(4)]
        cross = [jnp.where(wide == g - 1, tile[32 * g : 32 * g + 32], 0.0) for g in (1, 3)]
        left = dot3(halves(jnp.concatenate(cross, axis=0)), halves(jnp.concatenate(parts, axis=0)))
        left = jnp.concatenate([zero, left[:32], zero, left[32:]], axis=0)
        odd = jnp.concatenate([parts[1], parts[3]], axis=0)
        odd = odd - dot3(halves(odd), halves(left))
        first = jnp.concatenate([parts[0], odd[:32]], axis=0)
        second = jnp.concatenate([parts[2], odd[32:]], axis=0)
        half = jnp.concatenate([first, second], axis=0)
        cross = jnp.where(lanes((64, 128)) < 64, tile[64:], 0.0)
        left = dot3(halves(cross), halves(half))
        left = jnp.concatenate([jnp.zeros_like(left), left], axis=0)
        results.append(jnp.concatenate([first, second - dot3(halves(second), halves(left))], axis=0))
    return results


def dot2(a, b, dims=((1,), (0,))):
    bh, bl = b
    return dot_by(a, bh, dims) + dot_by(a, bl, dims)


def spot_of(arc, slab):
    big = slab // 16
    pair = slab + big * (31 - 2 * slab)
    far = pair // 4
    near = pair - 4 * far
    place = (1 - arc) * (4 * far + near) + arc * (4 * near + far)
    return place, big, big * far


def tile_of(ref, arc, row, column):
    pieces = []
    for i in range(4):
        place, _, shift = spot_of(arc, 4 * row + i)
        pieces.append(ref[arc, place, shift + column])
    return jnp.concatenate(pieces, axis=0)


def diagonal_of(ref, arc, row):
    pieces = []
    for i in range(4):
        place, big, _ = spot_of(arc, 4 * row + i)
        pieces.append(
            ref[arc, place, 7 + 2 * big].astype(F32) + ref[arc, place, 8 + 2 * big].astype(F32)
        )
    return jnp.concatenate(pieces, axis=0)


def invert_all(step, factor_ref, inv):
    tiles = inv.shape[1] // 128
    found = []
    for part in range(GROUP):
        at = step * GROUP + part
        arc, tile = at // tiles, lax.rem(at, tiles)
        spot = pl.ds(pl.multiple_of(tile * 128, 128), 128)
        found.append((arc, spot, tile))
    done = invert_tiles([diagonal_of(factor_ref, arc, tile) for arc, spot, tile in found])
    for (arc, spot, _), value in zip(found, done):
        inv[arc, spot, :] = value


def join_tiles(arc, factor_ref, inv, fh, wh, wl):
    for b in range(inv.shape[1] // OBS_STEP):
        r = b * OBS_STEP
        one, two = inv[arc, r : r + 128, :], inv[arc, r + 128 : r + 256, :]
        cross = tile_of(factor_ref, arc, 2 * b + 1, 2 * b)
        corner = -dot3(halves(two), halves(dot2(cross, halves(one))))
        zero = jnp.zeros((128, 128), BF)
        for ref, a, c, d in zip((wh, wl), halves(one), halves(corner), halves(two)):
            ref[arc, r : r + 128, 0:128] = a
            ref[arc, r : r + 128, 128:256] = zero
            ref[arc, r + 128 : r + 256, 0:128] = c
            ref[arc, r + 128 : r + 256, 128:256] = d
        for row in (2 * b, 2 * b + 1):
            for column in range(2 * b):
                fh[arc, row * 128 : row * 128 + 128, column * 128 : column * 128 + 128] = tile_of(
                    factor_ref, arc, row, column
                )


def solve_forward(b, rhs_ref, fh, wh, wl, yh, yl):
    r = b * OBS_STEP
    here = slice(r, r + OBS_STEP)
    for arc in range(rhs_ref.shape[0]):
        value = rhs_ref[arc, here, :].astype(F32)
        if b:
            value = value - dot2(fh[arc, here, 0:r], (yh[arc, 0:r, :], yl[arc, 0:r, :]))
        value = dot3((wh[arc, here, :], wl[arc, here, :]), halves(value))
        yh[arc, here, :], yl[arc, here, :] = halves(value)


def solve_back(b, fh, wh, wl, yh, yl, qh, ql):
    flip = ((0,), (0,))
    size = yh.shape[1]
    r = b * OBS_STEP
    here, after = slice(r, r + OBS_STEP), slice(r + OBS_STEP, size)
    for arc in range(yh.shape[0]):
        value = yh[arc, here, :].astype(F32) + yl[arc, here, :].astype(F32)
        if r + OBS_STEP < size:
            value = value - dot2(fh[arc, after, here], (qh[arc, after, :], ql[arc, after, :]), flip)
        value = dot3((wh[arc, here, :], wl[arc, here, :]), halves(value), flip)
        qh[arc, here, :], ql[arc, here, :] = halves(value)


def block_tiles(yh, block_ref):
    at = 0
    for i in range(0, yh.shape[2], 128):
        strip = sum(
            dot_by(yh[arc, :, i : i + 128], yh[arc, :, i:], ((0,), (0,))) for arc in range(yh.shape[0])
        )
        for j in range(0, strip.shape[1], 128):
            block_ref[at : at + 128, :] = strip[:, j : j + 128]
            at += 128


def split_rows(u):
    high, less = halves(u)
    return jnp.concatenate([high, high, less], axis=0), jnp.concatenate([high, less, high], axis=0)


def eliminate(panel, first):
    row = rows_of((8, 128))
    scale = [jnp.zeros((8, 128), F32) for _ in range(4)]
    for group in range(4):
        cols = []
        for t in range(8):
            lane = first + group * 8 + t
            cols.append(
                [
                    jnp.broadcast_to(panel[g][0][:, lane : lane + 1], (8, 128)) if g >= group else None
                    for g in range(4)
                ]
            )
        for t in range(8):
            pivot = lax.rsqrt(jnp.broadcast_to(cols[t][group][t : t + 1], (8, 128)))
            scale[group] = jnp.where(row == t, pivot, scale[group])
            inv = pivot * pivot
            mult = [None if g < group else cols[t][g] * inv for g in range(4)]
            mult[group] = jnp.where(row > t, mult[group], 0.0)
            for t2 in range(t + 1, 8):
                top = jnp.broadcast_to(cols[t2][group][t : t + 1], (8, 128))
                for g in range(group, 4):
                    cols[t2][g] = cols[t2][g] - mult[g] * top
            for c in range(len(panel[0])):
                top = jnp.broadcast_to(panel[group][c][t : t + 1], (8, 128))
                for g in range(group, 4):
                    panel[g][c] = panel[g][c] - mult[g] * top
    return jnp.concatenate(
        [jnp.concatenate([piece * scale[g] for piece in panel[g]], axis=1) for g in range(4)], axis=0
    )


def factor_and_invert(work):
    size = work.shape[0]
    width = size + 128
    flip = ((0,), (0,))
    at = lambda base, n: pl.ds(pl.multiple_of(base, 128), n)

    @pl.loop(0, size // 128)
    def _(k):
        c0 = k * 128
        wide = at(c0, width)
        for q in range(4):
            top = lambda g, n: pl.ds(pl.multiple_of(c0 + q * 32 + 8 * g, 8), n)
            panel = [
                [work[top(g, 8), at(c0 + c, 128)] for c in range(0, width, 128)] for g in range(4)
            ]
            done = eliminate(panel, q * 32)
            work[top(0, 32), wide] = done
            if q < 3:
                a, b = split_rows(done)
                less = dot_by(a[:, 0:128], b, flip)
                work[top(4, 96 - q * 32), wide] -= less[q * 32 + 32 : 128]

        @pl.when(k < size // 128 - 1)
        def _():
            _, b = split_rows(work[at(c0, 128), wide])

            @pl.loop(k + 1, size // 128)
            def _(i):
                a, _ = split_rows(work[at(c0, 128), at(i * 128, 128)])
                work[at(i * 128, 128), wide] -= dot_by(a, b, flip)


def tile_list(size):
    return [(i, j) for i in range(size // 128) for j in range(i, size // 128)]


MESH = pl.DeviceIdType.MESH


def remote(src, dst, send, recv, device):
    return pltpu.make_async_remote_copy(
        src_ref=src, dst_ref=dst, send_sem=send, recv_sem=recv, device_id=device, device_id_type=MESH
    )


def meet(devices):
    barrier = pltpu.get_barrier_semaphore()
    for device in devices:
        pl.semaphore_signal(barrier, inc=1, device_id=device, device_id_type=MESH)
    pl.semaphore_wait(barrier, len(devices))


def ring_pair(slot, me, axis, send, recv):
    mine = slot(me)
    return [
        remote(mine, mine, send.at[d], recv.at[d], {axis: lax.rem(me + step, 4)})
        for d, step in enumerate((1, 3))
    ]


def ring_far(first, second, me, axis, send, recv):
    left, right = lax.rem(me + 3, 4), lax.rem(me + 1, 4)
    one, two = first(left), second(right)
    return [
        remote(one, one, send.at[2], recv.at[2], {axis: right}),
        remote(two, two, send.at[3], recv.at[3], {axis: left}),
    ]


def main_kernel(
    at_ref, active_ref, cov_ref, reg_ref, design_hbm, final_ref, win_ref,
    fac_ref, rhs_ref, slabs, got1, got2, gotz, sum1, sum2, inv, fh, wh, wl, yh, yl, qh, ql, design_ref,
    part_ref, gram, kept, mate, got, pair, out_ref, sum_ref, own_ref, arrived, work,
    ls, lr, m1s, m1r, m2s, m2r, mzs, mzr, gls, glr, gms, gmr,
    ds, ps, pr, qs, qr, rs, rr, gs, gr, fs, fr, es, er,
):
    z, x, y = (lax.axis_index(name) for name in ("par_0", "par_1", "par_2"))
    chip, core = lax.axis_index("line"), lax.axis_index("core")
    other = {"core": 1 - core}
    chips = [lax.rem(chip + k, 4) for k in (1, 2, 3)]
    peers = [{"line": c} for c in chips]
    load = pltpu.make_async_copy(design_hbm, design_ref, ds)
    load.start()
    arcs = cov_ref.shape[0]
    turned = lambda v: v + z * (3 - 2 * v)
    outer = [(x, "par_1"), (y, "par_2")]
    inner = [(y, "par_2"), (x, "par_1")]
    partner = {"par_0": 1 - z, "par_1": 3 - x, "par_2": 3 - y}
    ring = [{"par_1": lax.rem(x + k, 4)} for k in (1, 2, 3)] + [
        {"par_2": lax.rem(y + k, 4)} for k in (1, 2, 3)
    ]
    meet(ring + [{"par_0": 1 - z}, partner] + peers + [other])

    small = turned(x) + 1
    held = small + z * (9 - 2 * small)
    two = range(arcs)
    sent = []

    def piece(c):
        return remote(slabs.at[z, c], slabs.at[z, c], ls.at[c], lr.at[c], partner)

    def came(c):
        return remote(slabs.at[1 - z, c], slabs.at[1 - z, c], ls.at[c], lr.at[c], partner)

    def begin(copies):
        for copy in copies:
            copy.start()
        sent.extend(copies)
        return copies

    def arrive(copies):
        for copy in copies:
            copy.wait_recv()

    def near(slot, ax, s, r):
        return begin(
            [copy for arc in two for copy in ring_pair(slot(arc), *ax[arc], s.at[arc], r.at[arc])]
        )

    def far(first, second, ax, s, r):
        return begin(
            [
                copy for arc in two
                for copy in ring_far(first(arc), second(arc), *ax[arc], s.at[arc], r.at[arc])
            ]
        )

    def l_unit(low, size):
        return lambda arc: lambda r: fac_ref.at[
            arc, 4 * turned(outer[arc][0]) + turned(r), pl.ds(low, size)
        ]

    def l_group(low, size):
        return lambda arc: lambda r: fac_ref.at[arc, pl.ds(4 * turned(r) + low, size)]

    def factor_stream():
        last = cov_ref[:, :, pl.ds(pl.multiple_of((held - 1) * 128, 128), 128)]
        slabs[z, 8] = (last - last.astype(BF).astype(F32)).astype(BF)
        for c in range(8):
            slabs[z, c] = cov_ref[:, :, c * 128 : c * 128 + 128].astype(BF)
        pl.loop(0, held)(lambda c: piece(c).start())
        piece(8).start()
        yield
        pl.loop(0, 9 - held)(lambda c: came(c).wait_recv())
        came(8).wait_recv()
        for arc in two:
            place = 4 * turned(outer[arc][0]) + turned(inner[arc][0])

            @pl.loop(0, small - 1)
            def _(c):
                fac_ref[arc, place, c] = slabs[0, c, arc]

            @pl.loop(0, 8 - small)
            def _(c):
                fac_ref[arc, place, small - 1 + c] = slabs[1, c, arc]

            fac_ref[arc, place, 7] = slabs[0, small - 1, arc]
            fac_ref[arc, place, 8] = slabs[0, 8, arc]
            fac_ref[arc, place, 9] = slabs[1, 8 - small, arc]
            fac_ref[arc, place, 10] = slabs[1, 8, arc]
        s, r = gls.at[0], glr.at[0]
        l1 = near(l_unit(0, 11), inner, s, r)
        yield
        arrive(l1)
        l2 = far(l_unit(0, 6), l_unit(6, 5), inner, s, r)
        yield
        arrive(l2)
        s, r = gls.at[1], glr.at[1]
        l3 = near(l_group(0, 4), outer, s, r)
        yield
        arrive(l3)
        l4 = far(l_group(0, 2), l_group(2, 2), outer, s, r)
        yield
        arrive(l4)
        yield

    def panel_stream(part):
        cols = pl.ds(part * PART, PART)
        lines = lambda base, n: pl.ds(pl.multiple_of(base, 32), n)

        def m_unit(low, size):
            return lambda arc: lambda r: rhs_ref.at[
                arc, lines(outer[arc][0] * 256 + r * 64 + low, size), cols
            ]

        def m_group(low, size):
            return lambda arc: lambda r: rhs_ref.at[arc, lines(r * 256 + low, size), cols]

        def to_peers(source, target, ax, unit, s, r):
            copies = []
            for k in (1, 3, 2):
                for arc in two:
                    to = lax.rem(ax[arc][0] + k, 4)
                    copies.append(
                        remote(
                            source.at[arc, lines(to * unit, unit), cols],
                            target.at[arc, k - 1, :, cols],
                            s.at[part, arc, k - 1], r.at[part, arc, k - 1], {ax[arc][1]: to},
                        )
                    )
            return begin(copies)

        scatter1 = to_peers(win_ref, got1, outer, 256, m1s, m1r)
        yield
        arrive(scatter1)
        for arc in two:
            own = win_ref[arc, lines(outer[arc][0] * 256, 256), cols]
            sum1[arc, :, cols] = (own + got1[arc, 0, :, cols]) + (
                got1[arc, 1, :, cols] + got1[arc, 2, :, cols]
            )
        scatter2 = to_peers(sum1, got2, inner, 64, m2s, m2r)
        yield
        arrive(scatter2)
        for arc in two:
            own = sum1[arc, lines(inner[arc][0] * 64, 64), cols]
            sum2[arc, :, cols] = (own + got2[arc, 0, :, cols]) + (
                got2[arc, 1, :, cols] + got2[arc, 2, :, cols]
            )
        across = begin(
            [
                remote(
                    sum2.at[arc, :, cols], gotz.at[arc, :, cols],
                    mzs.at[part, arc], mzr.at[part, arc], {"par_0": 1 - z},
                )
                for arc in two
            ]
        )
        yield
        arrive(across)
        for arc in two:
            spot = lines(outer[arc][0] * 256 + inner[arc][0] * 64, 64)
            rhs_ref[arc, spot, cols] = sum2[arc, :, cols] + gotz[arc, :, cols]
        s, r = gms.at[part, 0], gmr.at[part, 0]
        g1 = near(m_unit(0, 64), inner, s, r)
        yield
        arrive(g1)
        g2 = far(m_unit(0, 32), m_unit(32, 32), inner, s, r)
        yield
        arrive(g2)
        s, r = gms.at[part, 1], gmr.at[part, 1]
        g3 = near(m_group(0, 256), outer, s, r)
        yield
        arrive(g3)
        g4 = far(m_group(0, 128), m_group(128, 128), outer, s, r)
        yield
        arrive(g4)
        yield

    def prepare(step):
        if step < 2:
            invert_all(step, fac_ref, inv)
        else:
            for arc in two:
                join_tiles(arc, fac_ref, inv, fh, wh, wl)

    place_of_device = (z * 4 + x) * 4 + y

    def active(*ids):
        found = jnp.ones(active_ref.shape, F32)
        for one in ids:
            found = found * jnp.where(active_ref[...] == one, 1.0, 0.0)
        return [jnp.sum(found[arc : arc + 1], axis=1, keepdims=True) for arc in two]

    def cut_window():
        load.wait()
        many = design_ref.shape[2] // BLK
        for part in range(win_ref.shape[2] // BLK):
            wanted = at_ref[0] * (win_ref.shape[2] // BLK) + part
            marks = [active(wanted, place_of_device * many + block) for block in range(many)]
            for arc in two:
                marks_here = [mark[arc].astype(BF) for mark in marks]

                @pl.loop(0, design_ref.shape[1] // 128)
                def _(step):
                    spot = pl.ds(pl.multiple_of(step * 128, 128), 128)
                    total = design_ref[arc, spot, 0:BLK] * marks_here[0]
                    for block in range(1, many):
                        low = block * BLK
                        total = total + design_ref[arc, spot, low : low + BLK] * marks_here[block]
                    win_ref[arc, spot, part * BLK : part * BLK + BLK] = total

    streams = {"l": factor_stream(), "a": panel_stream(0)}
    if PARTS > 1:
        streams["b"] = panel_stream(1)
    for at, step in enumerate(ORDER):
        if at == 1:
            cut_window()
        if step.isdigit():
            prepare(int(step))
        else:
            next(streams[step])
    blocks = rhs_ref.shape[1] // OBS_STEP
    for b in range(blocks):
        solve_forward(b, rhs_ref, fh, wh, wl, yh, yl)
    block_tiles(yh, part_ref)

    half = part_ref.shape[0] // 2
    quarter = half // 4
    rows = lambda base, n: pl.ds(pl.multiple_of(base, 32), n)
    columns = design_ref.shape[2]
    width = qh.shape[2]
    share = gram.shape[2]
    swap = remote(part_ref.at[rows((1 - core) * half, half)], mate, ps, pr, other)
    swap.start()

    def product(block):
        flip = ((0,), (0,))
        total = jnp.zeros((BLK, width), F32)
        for arc, on in zip(two, active(place_of_device * (columns // BLK) + block)):
            piece = design_ref[arc, :, block * BLK : block * BLK + BLK]
            one = dot_by(piece, qh[arc], flip) + dot_by(piece, ql[arc], flip)
            total = total + one * on
        low = block * BLK
        while low < block * BLK + BLK:
            at = low // share
            stop = min((at + 1) * share, block * BLK + BLK)
            gram[at // 2, at % 2, low - at * share : stop - at * share, :] = total[
                low - block * BLK : stop - block * BLK
            ]
            low = stop

    for b in reversed(range(1, blocks)):
        solve_back(b, fh, wh, wl, yh, yl, qh, ql)
        if b == blocks - 1:
            swap.wait_recv()
            kept[...] = part_ref[rows(core * half, half), :] + mate[...]
            scatter = begin([
                remote(kept.at[rows(c * quarter, quarter)], got.at[k], rs.at[k], rr.at[k], peer)
                for k, (c, peer) in enumerate(zip(chips, peers))
            ])
    solve_back(0, fh, wh, wl, yh, yl, qh, ql)
    product(0)
    product(1)
    arrive(scatter)
    mine = rows(core * half + chip * quarter, quarter)
    out_ref[mine, :] = (kept[rows(chip * quarter, quarter), :] + got[0]) + (got[1] + got[2])
    gather = begin([
        remote(out_ref.at[mine], out_ref.at[mine], gs.at[k], gr.at[k], peer)
        for k, peer in enumerate(peers)
    ])
    forward = begin([remote(out_ref.at[mine], out_ref.at[mine], fs.at[0], fr.at[0], other)])
    for block in range(2, columns // BLK):
        product(block)
    trade = remote(gram.at[:, 1 - core], pair, qs, qr, other)
    trade.start()
    for k in range(3):
        gather[k].wait_recv()
        from_chip = rows(core * half + lax.rem(chip + 3 - k, 4) * quarter, quarter)
        forward += begin([
            remote(out_ref.at[from_chip], out_ref.at[from_chip], fs.at[k + 1], fr.at[k + 1], other)
        ])
    trade.wait_recv()
    for c in range(4):
        sum_ref[c] = (gram[c, core] + pair[c]).astype(BF)
    exchange = begin([
        remote(sum_ref.at[c], arrived.at[k], es.at[k], er.at[k], peer)
        for k, (c, peer) in enumerate(zip(chips, peers))
    ])
    own_ref[...] = gram[chip, core] + pair[chip]
    reg = reg_ref[at_ref[0]]
    square = (128, 128)
    eye = lanes(square) == rows_of(square)
    work[...] = jnp.zeros_like(work)
    arrive(forward)
    for at, (i, j) in enumerate(tile_list(width)):
        value = out_ref[at * 128 : at * 128 + 128, :]
        if i == j:
            value = value + jnp.where(eye, reg[:, i * 128 : i * 128 + 128], 0.0)
            work[i * 128 : i * 128 + 128, width + i * 128 : width + i * 128 + 128] = jnp.where(
                eye, 1.0, 0.0
            )
        work[i * 128 : i * 128 + 128, j * 128 : j * 128 + 128] = value
    factor_and_invert(work)
    arrive(exchange)
    total = own_ref[...]
    for k in range(3):
        total = total + arrived[k].astype(F32)
    first = place_of_device * columns + (chip * 2 + core) * share - at_ref[0] * width
    total = total + jnp.where(rows_of(total.shape) + first == lanes(total.shape), reg, 0.0)
    final_ref[...] = dot3(halves(total), halves(work[:, width:]), ((1,), (1,)))
    pl.loop(0, held)(lambda c: piece(c).wait_send())
    piece(8).wait_send()
    for copy in sent + [swap, trade]:
        copy.wait_send()


def solve_panel(at, active, cov, reg, design):
    arcs, lines, size = cov.shape
    width = reg.shape[2]
    chips = 4
    share = design.shape[2] // (2 * chips)
    total = len(tile_list(width)) * 128
    vm, dma = pltpu.VMEM, pltpu.SemaphoreType.DMA
    return pl.pallas_call(
        main_kernel,
        out_shape=jax.ShapeDtypeStruct((share, width), F32),
        in_specs=[pl.BlockSpec(memory_space=pltpu.SMEM)]
        + [pl.BlockSpec(memory_space=vm)] * 3
        + [pl.BlockSpec(memory_space=pl.ANY)],
        out_specs=pl.BlockSpec(memory_space=vm),
        scratch_shapes=[
            vm((arcs, size, width), BF),
            vm((arcs, 16, 11, lines, 128), BF),
            vm((arcs, size, width), BF),
            vm((2, 9, arcs, lines, 128), BF),
            vm((arcs, 3, 256, width), BF),
            vm((arcs, 3, 64, width), BF),
            vm((arcs, 64, width), BF),
            vm((arcs, 256, width), BF),
            vm((arcs, 64, width), BF),
            vm((arcs, size, 128), F32),
            vm((arcs, size, size), BF),
            vm((arcs, size, OBS_STEP), BF),
            vm((arcs, size, OBS_STEP), BF),
            vm((arcs, size, width), BF),
            vm((arcs, size, width), BF),
            vm((arcs, size, width), BF),
            vm((arcs, size, width), BF),
            vm(design.shape, BF),
            vm((total, 128), F32),
            vm((chips, 2, share, width), F32),
            vm((total // 2, 128), F32),
            vm((total // 2, 128), F32),
            vm((3, total // 8, 128), F32),
            vm((chips, share, width), F32),
            vm((total, 128), F32),
            vm((chips, share, width), BF),
            vm((share, width), F32),
            vm((chips - 1, share, width), BF),
            vm((width, 2 * width), F32),
            dma((9,)), dma((9,)),
            dma((PARTS, arcs, 3)), dma((PARTS, arcs, 3)), dma((PARTS, arcs, 3)), dma((PARTS, arcs, 3)),
            dma((PARTS, arcs)), dma((PARTS, arcs)),
            dma((2, arcs, 4)), dma((2, arcs, 4)), dma((PARTS, 2, arcs, 4)), dma((PARTS, 2, arcs, 4)),
            dma, dma, dma, dma, dma, dma((3,)), dma((3,)), dma((3,)), dma((3,)), dma((4,)), dma((4,)),
            dma((3,)), dma((3,)),
        ],
        compiler_params=pltpu.CompilerParams(
            vmem_limit_bytes=KERNEL_VMEM, collective_id=0, has_side_effects=True
        ),
    )(at, active, cov, reg, design)


PANEL = 512
BLK = 256
PAR = ("par_0", "par_1", "par_2")


def on_device(design, cov_factor, active_blocks, panel_index, reg_diag):
    reg = reg_diag.reshape(-1, 1, PANEL)
    return solve_panel(panel_index, active_blocks, cov_factor, reg, design).T


def solution(mesh):
    split = Mesh(
        mesh.devices.reshape(mesh.shape["arc"] // 2, 2, 2, 4, 4), ("line", "core") + PAR
    )
    arc = ("line", "core")
    return jax.shard_map(
        on_device,
        mesh=split,
        in_specs=(P(arc, None, PAR), P(arc, PAR, None), P(arc, None), P(), P()),
        out_specs=P(None, PAR + arc),
        check_vma=False,
    )
```
